512 devices in a mesh: seg: 64 (over x, z, core), tp: 8 (over y).
Axes of the slice: x: 4, y: 8, z: 8, core: 2. Of those that a mesh axis runs over, the one named last changes fastest.
Arguments:
- natural_logged_absorbance: float32 [786432], P('seg'), may hold values from -4 to 4
- lower_state_level: float32 [786432], P('seg'), may hold values from 0 to 3000
- subgrid_shift_ratio: float32 [786432], P('seg'), may hold values from 0 to 1
- local_grid_slot: int32 [786432], P('seg'), may hold values from 0 to 2046
- broadening_class: int32 [786432], P('seg'), may hold values from 0 to 15
- tallies_per_shard: int32 [64, 64], replicated, may hold values from 0 to 768, as said below
- heat_levels: float32 [8], P('tp'), may hold values from 600 to 1200
- sum_over_states_ratio: float32 [8], P('tp'), may hold values from 0.5 to 2
- shape_kernels: float32 [8, 16, 256], P('tp'), may hold values from 0 to 0.00390625
Outputs:
- opacity: float32 [8, 131072], P('tp', 'seg')
The draws below stay inside these ranges and needn't reach their ends.
Inputs may be any that keep to these rules, and one draw needn't show every extreme that they name: `tallies_per_shard`: each row of counts sums to 12288; one segment, the same for every shard, receives exactly 768 lines from every shard, and no entry exceeds 768.
All inputs are finite; a program needn't handle non-finite values.
Results may differ from the reference program's by a relative error of at most 0.0003.
Values sent between devices are 32-bit elements; how exact they have to be, the bound alone decides.
A program may use at most 64 MiB of HBM per device.

```python
import math
import jax
import jax.numpy as jnp
from jax import lax

G = 2048
L_DEV = 12288
NW = 16
KLEN = 256
HALF = 128
STATE_COUNT = 8
CAP = 768
LINES = 786432
NGRID = 131072
N_SEG = 64


def draw_tallies_per_shard(key, part):
    key = jax.random.fold_in(key, 11)
    key_hot, key_band, key_weight = jax.random.split(key, 3)
    hottest = jax.random.randint(key_hot, (), 0, N_SEG)
    band_factor = jax.random.randint(key_band, (N_SEG,), 1, 3)
    weights = jax.random.randint(key_weight, (N_SEG, N_SEG), 2, 5) * band_factor[None, :]
    columns = jnp.arange(N_SEG, dtype=jnp.int32)
    is_hot = columns[None, :] == hottest
    weights = jnp.where(is_hot, 0, weights)
    remaining = L_DEV - CAP
    weight_total = jnp.sum(weights, axis=1, keepdims=True)
    shares = remaining * weights // weight_total
    leftover = remaining - jnp.sum(shares, axis=1, keepdims=True)
    ranking = jnp.cumsum(jnp.where(is_hot, 0, 1), axis=1) - 1
    shares = shares + jnp.where(jnp.logical_and(jnp.logical_not(is_hot), ranking < leftover), 1, 0)
    return jnp.where(is_hot, CAP, shares).astype(jnp.int32)


def with_ends(entries, key, low, largest):
    dims = entries.shape
    place = [jax.random.randint(jax.random.fold_in(key, axis), (), 0, dims[axis]) for axis in range(len(dims))]
    entries = entries.at[tuple(place)].set(low)
    longest = dims.index(max(dims))
    place[longest] = (place[longest] + 1) % dims[longest]
    return entries.at[tuple(place)].set(largest)


def steps_of(key, dims, cuts, least, largest):
    loudness = 1.0
    for dim, shards_of in cuts:
        steps = jax.random.uniform(jax.random.fold_in(jax.random.fold_in(key, 6), dim), (shards_of,), jnp.float32, least / len(cuts), largest / len(cuts))
        loudness = loudness * jnp.repeat(jnp.exp(steps), dims[dim] // shards_of).reshape((-1,) + (1,) * (len(dims) - 1 - dim))
    return loudness


def gaussian(own_key, shape, scale, most, cuts=(), kind=jnp.bfloat16):
    loudness = steps_of(own_key, shape, cuts, -0.22, 0.18) if cuts else 1.0
    result = jax.random.normal(own_key, shape, jnp.float32) * scale * loudness
    return jnp.minimum(jnp.maximum(result, -most), most).astype(kind)


def setup_inputs(seed: int = 0) -> dict:
    key_of = jax.random.split(jax.random.key(seed), 10)
    natural_logged_absorbance = gaussian(key_of[0], (LINES,), 1.0, 4.0, ((0, 64),), jnp.float32)
    lower_state_level = jnp.clip(3000.0 * jax.random.uniform(key_of[1], (LINES,), jnp.float32) ** steps_of(key_of[1], (LINES,), ((0, 64),), -0.2, 0.2), 0.0, 3000.0)
    subgrid_shift_ratio = jnp.clip(1.0 * jax.random.uniform(key_of[2], (LINES,), jnp.float32) ** steps_of(key_of[2], (LINES,), ((0, 64),), -0.2, 0.2), 0.0, 1.0)
    local_grid_slot = with_ends(jax.random.randint(key_of[3], (LINES,), 0, G - 1), jax.random.fold_in(key_of[3], 1), 0, (G - 1) - 1).astype(jnp.int32)
    broadening_class = with_ends(jax.random.randint(key_of[4], (LINES,), 0, NW), jax.random.fold_in(key_of[4], 1), 0, NW - 1).astype(jnp.int32)
    tallies_per_shard = draw_tallies_per_shard(jax.random.fold_in(key_of[9], 71), 0)
    heat_levels = jnp.clip(600.0 + 600.0 * jax.random.uniform(key_of[6], (STATE_COUNT,), jnp.float32) ** steps_of(key_of[6], (STATE_COUNT,), ((0, 8),), -0.2, 0.2), 600.0, 1200.0)
    sum_over_states_ratio = jnp.clip(jnp.exp(math.log(2.0) - 1.3862944 * jax.random.uniform(key_of[7], (STATE_COUNT,), jnp.float32) ** steps_of(key_of[7], (STATE_COUNT,), ((0, 8),), -0.2, 0.2)), 0.5, 2.0)
    shape_kernels = jnp.clip(0.00390625 * jax.random.uniform(key_of[8], (STATE_COUNT, NW, KLEN), jnp.float32) ** steps_of(key_of[8], (STATE_COUNT, NW, KLEN), ((0, 8),), -0.2, 0.2), 0.0, 0.00390625)
    return {"natural_logged_absorbance": natural_logged_absorbance, "lower_state_level": lower_state_level, "subgrid_shift_ratio": subgrid_shift_ratio, "local_grid_slot": local_grid_slot, "broadening_class": broadening_class, "tallies_per_shard": tallies_per_shard, "heat_levels": heat_levels, "sum_over_states_ratio": sum_over_states_ratio, "shape_kernels": shape_kernels}


planck_hc_over_boltzmann = 1.4388
baseline_heat_level = 900.0


def reference(natural_logged_absorbance, lower_state_level, subgrid_shift_ratio, local_grid_slot, broadening_class, tallies_per_shard, heat_levels, sum_over_states_ratio, shape_kernels):
    position = jnp.arange(L_DEV, dtype=jnp.int32)
    segment_ends = jnp.cumsum(tallies_per_shard, axis=1).astype(jnp.int32)
    target = jnp.sum((position[None, :, None] >= segment_ends[:, None, :]).astype(jnp.int32), axis=2).reshape(-1)
    global_cell = (target * G + local_grid_slot).astype(jnp.int32)
    flat_index = (broadening_class * NGRID + global_cell).astype(jnp.int32)
    length = NGRID + KLEN
    kernel_spec = jnp.fft.rfft(shape_kernels, n=length, axis=-1)
    results = []
    for atmosphere_state in range(STATE_COUNT):
        transition_absorbance = sum_over_states_ratio[atmosphere_state] * jnp.exp(natural_logged_absorbance - planck_hc_over_boltzmann * lower_state_level * (1.0 / heat_levels[atmosphere_state] - 1.0 / baseline_heat_level))
        weight_low = lax.optimization_barrier((transition_absorbance * (1.0 - subgrid_shift_ratio)).astype(jnp.bfloat16)).astype(jnp.float32)
        weight_high = lax.optimization_barrier((transition_absorbance * subgrid_shift_ratio).astype(jnp.bfloat16)).astype(jnp.float32)
        binned = jnp.zeros((NW * NGRID,), jnp.float32)
        binned = binned.at[flat_index].add(weight_low).at[flat_index + 1].add(weight_high)
        binned = binned.reshape(NW, NGRID)
        spectrum = jnp.sum(jnp.fft.rfft(binned, n=length, axis=-1) * kernel_spec[atmosphere_state], axis=0)
        full_line = jnp.fft.irfft(spectrum, n=length)
        results.append(full_line[HALF:HALF + NGRID].astype(jnp.float32))
    return jnp.stack(results)
```

```python
import functools

import jax
import jax.numpy as jnp
from jax import lax
from jax.experimental import pallas as pl
from jax.experimental.pallas import tpu as pltpu
from jax.sharding import PartitionSpec as P

MESH = pl.DeviceIdType.MESH

G = 2048
NW = 16
POINTS = 8
CAP = 768
FIELDS = 5
J = 9
JW = 8 * NW
COLS = POINTS * JW + JW
BLOCKS = G // 8
PARTS = CAP // 128
SPAN = 384
REACH = 272
PACK = 4

planck_hc_over_boltzmann = 1.4388
baseline_heat_level = 900.0


def split(x):
    high = x.astype(jnp.bfloat16)
    return high, (x - high.astype(jnp.float32)).astype(jnp.bfloat16)


def kernel(
    n,
    heat_ref,
    ratio_ref,
    tallies_ref,
    absorb_ref,
    level_ref,
    shift_ref,
    slot_ref,
    class_ref,
    shape_ref,
    out_ref,
    heat,
    ratio,
    tallies,
    absorb,
    level,
    shift,
    slot,
    width,
    lines,
    starts,
    send,
    recv,
    points,
    shapes,
    rows0,
    cols0,
    rows1,
    cols1,
    acc,
    taps_high,
    taps_low,
    bins_high,
    bins_low,
    main_send,
    left_send,
    right_send,
    main_recv,
    left_recv,
    right_recv,
    ordered,
    in_sem,
    send_sem,
    first_sem,
    recv_sem,
    point_send_sem,
    point_sem,
    shape_send_sem,
    shape_sem,
    main_send_sem,
    main_sem,
    halo_send_sem,
    halo_sem,
):
    me = lax.axis_index("seg")
    tp = lax.axis_index("tp")
    left = lax.rem(me + n - 1, n)
    right = lax.rem(me + 1, n)

    eight = pl.multiple_of((me // 8) * 8, 8)
    copies = [
        pltpu.make_async_copy(src, dst, in_sem.at[k])
        for k, (src, dst) in enumerate(
            (
                (heat_ref, heat),
                (ratio_ref, ratio),
                (tallies_ref.at[pl.ds(eight, 8)], tallies),
                (absorb_ref, absorb),
                (level_ref, level),
                (shift_ref, shift),
                (slot_ref, slot),
                (class_ref, width),
                (shape_ref, shapes.at[0]),
            )
        )
    ]
    for copy in copies:
        copy.start()

    eighth = lax.rem(tp + n - lax.rem(me, 8), 8)
    stays = eighth == lax.rem(me, 8)
    octets = n // 8

    def partner(i):
        return eighth + 8 * lax.rem(me // 8 + i, octets)

    barrier = pltpu.get_barrier_semaphore()

    def greet(segment, point):
        pl.semaphore_signal(
            barrier, inc=1, device_id=(segment, point), device_id_type=MESH
        )

    for i in range(octets):
        if i == 0:
            pl.when(jnp.logical_not(stays))(lambda: greet(partner(0), tp))
        else:
            greet(partner(i), tp)
    for i in range(1, POINTS):
        for segment in (me, left, right):
            greet(segment, lax.rem(tp + i, POINTS))
    greet(left, tp)
    greet(right, tp)

    lane8 = lax.broadcasted_iota(jnp.int32, (8, 128), 1)
    sub8 = lax.broadcasted_iota(jnp.int32, (8, 128), 0)
    acc[...] = jnp.zeros_like(acc)

    for copy in copies[:3]:
        copy.wait()

    points[0] = jnp.where(lane8[:1] < 64, heat[0, 0], ratio[0, 0])

    def add_up(d, total):
        for u in range(8):
            starts[8 * d + u] = total
            total = total + tallies[lax.rem(me, 8), 8 * d + u]
        return total

    lax.fori_loop(0, octets, add_up, jnp.int32(0))

    for copy in copies[3:]:
        copy.wait()

    tiles = absorb.shape[0]
    lines[pl.ds(0, tiles), 0, :] = absorb[...]
    lines[pl.ds(0, tiles), 1, :] = level[...]
    lines[pl.ds(0, tiles), 2, :] = shift[...]
    lines[pl.ds(0, tiles), 3, :] = slot[...].astype(jnp.float32)
    lines[pl.ds(0, tiles), 4, :] = width[...].astype(jnp.float32)
    lines[pl.ds(tiles, 8)] = jnp.zeros((8, 8, 128), jnp.float32)

    def pack(target):
        begin = starts[target]
        count = tallies[lax.rem(me, 8), target]
        tile = lax.shift_right_logical(begin, 7)
        offset = jnp.full((8, 128), lax.bitwise_and(begin, 127))
        held = [lines[tile + q] for q in range(PARTS + 1)]
        windows = []
        for q in range(PARTS):
            window = jnp.where(lane8 >= offset, held[q], held[q + 1])
            for unit in (1, 4, 16):
                digit = lax.bitwise_and(offset, 3 * unit)
                turned = [pltpu.roll(window, 128 - k * unit, 1) for k in (1, 2, 3)]
                for k in (1, 2, 3):
                    window = jnp.where(digit == k * unit, turned[k - 1], window)
            turned = pltpu.roll(window, 64, 1)
            window = jnp.where(offset >= 64, turned, window)
            dead = jnp.logical_and(sub8 == 4, lane8 + 128 * q >= count)
            windows.append(jnp.where(dead, float(NW), window)[:FIELDS])
        return windows

    def pack_some(batch, _):
        first = batch * PACK
        packed = [pack(partner(first + u)) for u in range(PACK)]
        for u in range(PACK):
            for q in range(PARTS):
                send[first + u, q] = packed[u][q]
        return 0

    lax.fori_loop(0, octets // PACK, pack_some, 0)

    pl.semaphore_wait(barrier, octets + 2 + 3 * (POINTS - 1) - jnp.where(stays, 1, 0))

    def share(src, dst, sem_send, sem_recv):
        for i in range(1, POINTS):
            pltpu.make_async_remote_copy(
                src_ref=src.at[0],
                dst_ref=dst.at[i],
                send_sem=sem_send,
                recv_sem=sem_recv,
                device_id=(me, lax.rem(tp + i, POINTS)),
                device_id_type=MESH,
            ).start()

    def lines_to(i, sem):
        return pltpu.make_async_remote_copy(
            src_ref=send.at[i],
            dst_ref=recv.at[i],
            send_sem=sem,
            recv_sem=recv_sem.at[i],
            device_id=(partner(i), tp),
            device_id_type=MESH,
        )

    pl.when(jnp.logical_not(stays))(lambda: lines_to(0, first_sem).start())
    pl.when(stays)(
        lambda: pltpu.make_async_copy(
            send.at[0], recv.at[0], recv_sem.at[0]
        ).start()
    )
    share(points, points, point_send_sem, point_sem)
    for i in range(1, octets):
        lines_to(i, send_sem).start()
    share(shapes, shapes, shape_send_sem, shape_sem)

    def all_points(src, dst, sem_send, sem_recv):
        return pltpu.make_async_remote_copy(
            src_ref=src.at[pl.ds(1, POINTS - 1)],
            dst_ref=dst.at[pl.ds(1, POINTS - 1)],
            send_sem=sem_send,
            recv_sem=sem_recv,
            device_id=(me, lax.rem(tp + 1, POINTS)),
            device_id_type=MESH,
        )

    all_points(points, points, point_send_sem, point_sem).wait_recv()
    both = jnp.concatenate([points[i] for i in range(POINTS)], axis=0)
    heats = jnp.where(lane8 < 64, both, pltpu.roll(both, 64, 1))
    ratios = jnp.where(lane8 < 64, pltpu.roll(both, 64, 1), both)
    inverse_gap = 1.0 / heats - 1.0 / baseline_heat_level

    block_ids = lax.broadcasted_iota(jnp.int32, (128, BLOCKS), 1).astype(jnp.float32)
    width_ids = lax.broadcasted_iota(jnp.int32, (NW, 128), 0).astype(jnp.float32)
    width_row = lax.broadcasted_iota(jnp.int32, (JW, SPAN), 0)

    def spread(row):
        return jnp.broadcast_to(row, (NW, 128)).astype(jnp.bfloat16)

    def arrived(g):
        pltpu.make_async_remote_copy(
            src_ref=send.at[g],
            dst_ref=recv.at[g],
            send_sem=send_sem,
            recv_sem=recv_sem.at[g],
            device_id=(partner(1), tp),
            device_id_type=MESH,
        ).wait_recv()

    def one_hots(g, rows, cols):
        slots = [recv[g, part, 3:4, :] for part in range(PARTS)]
        slots = jnp.concatenate(slots + [slots[0]] * (8 - PARTS), axis=0)
        blocks = jnp.floor(slots * 0.125)
        cells = slots - 8.0 * blocks
        tall = blocks.T
        return [
            functools.partial(one_hot, g, part, cells[part : part + 1], tall, rows, cols)
            for part in range(PARTS)
        ]

    def one_hot(g, part, cell, tall, rows, cols):
        piece = recv[g, part]
        at = part * 128
        hits = jnp.broadcast_to(tall[:, part : part + 1], (128, BLOCKS)) == block_ids
        rows[pl.ds(at, 128), :] = jnp.where(hits, 1.0, 0.0).astype(jnp.bfloat16)
        strength = ratios * jnp.exp(
            piece[0:1] - planck_hc_over_boltzmann * piece[1:2] * inverse_gap
        )
        low = strength * (1.0 - piece[2:3])
        high = strength * piece[2:3]
        half_cell = cell * 0.5
        is_even = jnp.broadcast_to(half_cell == jnp.floor(half_cell), (POINTS, 128))
        evens = jnp.where(is_even, low, high)
        odds = jnp.where(is_even, high, low)
        is_width = jnp.broadcast_to(piece[4:5], (NW, 128)) == width_ids
        is_width = jnp.where(is_width, 1.0, 0.0).astype(jnp.bfloat16)
        here = [cell == float(j) for j in range(8)]
        touched = [
            here[0],
            *(jnp.logical_or(here[j], here[j - 1]) for j in range(1, 8)),
            here[7],
        ]
        touched = [spread(jnp.where(t, 1.0, 0.0)) for t in touched]
        for p in range(POINTS):
            even = spread(evens[p : p + 1]) * is_width
            odd = spread(odds[p : p + 1]) * is_width
            for j in range(J):
                top = p * JW + j * NW if j < 8 else POINTS * JW + p * NW
                value = (odd if j % 2 else even) * touched[j]
                cols[pl.ds(top, NW), pl.ds(at, 128)] = value

    def add_product(piece, rows, cols):
        some = pl.ds(piece * (COLS // PARTS), COLS // PARTS)
        acc[some] += jnp.dot(
            cols[some], rows[...], preferred_element_type=jnp.float32
        )

    def make_taps(p):
        taps = jnp.concatenate([shapes[p], jnp.zeros((NW, 128), jnp.float32)], axis=1)
        moved = [taps] + [pltpu.roll(taps, j, 1) for j in range(1, J)]
        ninth = jnp.concatenate([moved[8]] * POINTS, axis=0)
        ninth = jnp.where(width_row // NW == p, ninth, 0.0)
        every = jnp.concatenate(moved[:8] + [ninth], axis=0)
        high, low = split(every.T[:REACH])
        taps_high[p] = high
        taps_low[p] = low

    def step(g, rows, cols, last_rows, last_cols):
        arrived(g)
        for part, make in enumerate(one_hots(g, rows, cols)):
            make()
            add_product(part, last_rows, last_cols)
        make_taps(g)

    arrived(0)
    for make in one_hots(0, rows0, cols0):
        make()
    all_points(shapes, shapes, shape_send_sem, shape_sem).wait_recv()

    def deposit(h, _):
        step(2 * h + 1, rows1, cols1, rows0, cols0)
        step(2 * h + 2, rows0, cols0, rows1, cols1)
        return 0

    lax.fori_loop(0, octets // 2 - 1, deposit, 0)
    step(octets - 1, rows1, cols1, rows0, cols0)
    make_taps(0)
    for piece in range(PARTS):
        add_product(piece, rows1, cols1)
    high, low = split(acc[...])
    bins_high[...] = high
    bins_low[...] = low

    def fold(x):
        kept = jnp.where(lane8 < 16, x, 0.0)
        moved = pltpu.roll(kept, 0, 1, stride=16, stride_axis=0)
        return jnp.sum(moved, axis=0, keepdims=True)

    def unfold(row):
        wide = jnp.broadcast_to(row, (8, 128))
        moved = wide
        for i in range(1, 8):
            moved = jnp.where(sub8 == i, pltpu.roll(wide, 128 - 16 * i, 1), moved)
        return jnp.where(lane8 < 16, moved, 0.0)

    def convolve(p):
        own = pl.ds(pl.multiple_of(p * JW, JW), JW)
        ninth = pl.ds(POINTS * JW, JW)
        bin_high = jnp.concatenate([bins_high[own], bins_high[ninth]], axis=0)
        bin_low = jnp.concatenate([bins_low[own], bins_low[ninth]], axis=0)
        product = jnp.dot(taps_high[p], bin_high, preferred_element_type=jnp.float32)
        product += jnp.dot(taps_low[p], bin_high, preferred_element_type=jnp.float32)
        product += jnp.dot(taps_high[p], bin_low, preferred_element_type=jnp.float32)
        first, second = product[128:136, :128], product[128:136, 128:]
        outside = jnp.zeros((8, 128), jnp.float32)
        for m in range(33):
            by = m - 16
            if by == 0:
                continue
            front, back = product[8 * m : 8 * m + 8, :128], product[8 * m : 8 * m + 8, 128:]
            front = pltpu.roll(front, by % 128, 1)
            back = pltpu.roll(back, by % 128, 1)
            if by > 0:
                wraps = lane8 < by
                first += jnp.where(wraps, 0.0, front)
                second += jnp.where(wraps, front, back)
                outside += jnp.where(wraps, back, 0.0)
            else:
                wraps = lane8 >= 128 + by
                first += jnp.where(wraps, back, front)
                second += jnp.where(wraps, 0.0, back)
                outside += jnp.where(wraps, front, 0.0)
        main_send[p, 0] = first
        main_send[p, 1] = second
        left_send[p] = fold(pltpu.roll(outside, 16, 1))
        right_send[p] = fold(outside)

    def send_sums(p):
        point = lax.rem(tp + POINTS - p, POINTS)

        @pl.when(p > 0)
        def _():
            pltpu.make_async_remote_copy(
                src_ref=main_send.at[p],
                dst_ref=main_recv.at[p],
                send_sem=main_send_sem,
                recv_sem=main_sem,
                device_id=(me, point),
                device_id_type=MESH,
            ).start()

        for k, (src, dst, segment) in enumerate(
            ((left_send, left_recv, left), (right_send, right_recv, right))
        ):
            pltpu.make_async_remote_copy(
                src_ref=src.at[p],
                dst_ref=dst.at[p],
                send_sem=halo_send_sem.at[k],
                recv_sem=halo_sem.at[k],
                device_id=(segment, point),
                device_id_type=MESH,
            ).start()

    def convolve_two(h, _):
        pair = (POINTS // 2 + h, POINTS // 2 - 1 - h)
        for p in pair:
            convolve(p)
        for p in pair:
            send_sums(p)
        return 0

    lax.fori_loop(0, POINTS // 2, convolve_two, 0)

    sums = all_points(main_send, main_recv, main_send_sem, main_sem)
    halos = [
        pltpu.make_async_remote_copy(
            src_ref=src,
            dst_ref=dst,
            send_sem=halo_send_sem.at[k],
            recv_sem=halo_sem.at[k],
            device_id=(segment, tp),
            device_id_type=MESH,
        )
        for k, (src, dst, segment) in enumerate(
            ((left_send, left_recv, left), (right_send, right_recv, right))
        )
    ]
    for halo in halos:
        halo.wait_recv()
    from_right = unfold(jnp.sum(left_recv[...], axis=0))
    from_left = unfold(jnp.sum(right_recv[...], axis=0))
    from_right = jnp.where(me < n - 1, pltpu.roll(from_right, 112, 1), 0.0)
    from_left = jnp.where(me > 0, from_left, 0.0)
    first = main_send[0, 0] + from_left
    second = main_send[0, 1] + from_right
    sums.wait_recv()
    for p in range(1, POINTS):
        first += main_recv[p, 0]
        second += main_recv[p, 1]
    for k, part in enumerate((first, second)):
        tall = jnp.concatenate([part, jnp.zeros((120, 128), jnp.float32)], axis=0)
        ordered[pl.ds(128 * k, 128), :] = tall.T
    total = ordered[pl.ds(0, 16, stride=16), :]
    for k in range(1, 16):
        total += pltpu.roll(ordered[pl.ds(k, 16, stride=16), :], 8 * k, 1)
    out_ref[...] = total

    all_points(points, points, point_send_sem, point_sem).wait_send()
    all_points(shapes, shapes, shape_send_sem, shape_sem).wait_send()
    pl.when(jnp.logical_not(stays))(lambda: lines_to(0, first_sem).wait_send())
    pltpu.make_async_remote_copy(
        src_ref=send.at[pl.ds(1, octets - 1)],
        dst_ref=recv.at[pl.ds(1, octets - 1)],
        send_sem=send_sem,
        recv_sem=recv_sem.at[1],
        device_id=(partner(1), tp),
        device_id_type=MESH,
    ).wait_send()
    sums.wait_send()
    for halo in halos:
        halo.wait_send()


def body(
    natural_logged_absorbance,
    lower_state_level,
    subgrid_shift_ratio,
    local_grid_slot,
    broadening_class,
    tallies_per_shard,
    heat_levels,
    sum_over_states_ratio,
    shape_kernels,
):
    n = lax.axis_size("seg")
    lines = natural_logged_absorbance.shape[0]
    tiles = lines // 128
    hbm = pl.BlockSpec(memory_space=pl.ANY)
    vmem = pl.BlockSpec(memory_space=pltpu.VMEM)
    f32, bf16, i32 = jnp.float32, jnp.bfloat16, jnp.int32
    dma = pltpu.SemaphoreType.DMA
    result = pl.pallas_call(
        functools.partial(kernel, n),
        out_shape=jax.ShapeDtypeStruct((16, 128), f32),
        in_specs=[hbm] * 9,
        out_specs=vmem,
        scratch_shapes=[
            pltpu.SMEM((1, 1), f32),
            pltpu.SMEM((1, 1), f32),
            pltpu.SMEM((8, n), i32),
            pltpu.VMEM((tiles, 128), f32),
            pltpu.VMEM((tiles, 128), f32),
            pltpu.VMEM((tiles, 128), f32),
            pltpu.VMEM((tiles, 128), i32),
            pltpu.VMEM((tiles, 128), i32),
            pltpu.VMEM((tiles + 8, 8, 128), f32),
            pltpu.SMEM((n,), i32),
            pltpu.VMEM((n // 8, PARTS, FIELDS, 128), f32),
            pltpu.VMEM((n // 8, PARTS, FIELDS, 128), f32),
            pltpu.VMEM((POINTS, 1, 128), f32),
            pltpu.VMEM((POINTS, NW, 256), f32),
            pltpu.VMEM((CAP, BLOCKS), bf16),
            pltpu.VMEM((COLS, CAP), bf16),
            pltpu.VMEM((CAP, BLOCKS), bf16),
            pltpu.VMEM((COLS, CAP), bf16),
            pltpu.VMEM((COLS, BLOCKS), f32),
            pltpu.VMEM((POINTS, REACH, 2 * JW), bf16),
            pltpu.VMEM((POINTS, REACH, 2 * JW), bf16),
            pltpu.VMEM((COLS, BLOCKS), bf16),
            pltpu.VMEM((COLS, BLOCKS), bf16),
            pltpu.VMEM((POINTS, 2, 8, 128), f32),
            pltpu.VMEM((POINTS, 1, 128), f32),
            pltpu.VMEM((POINTS, 1, 128), f32),
            pltpu.VMEM((POINTS, 2, 8, 128), f32),
            pltpu.VMEM((POINTS, 1, 128), f32),
            pltpu.VMEM((POINTS, 1, 128), f32),
            pltpu.VMEM((BLOCKS, 128), f32),
            dma((9,)),
            dma,
            dma,
            dma((n // 8,)),
            dma,
            dma,
            dma,
            dma,
            dma,
            dma,
            dma((2,)),
            dma((2,)),
        ],
        compiler_params=pltpu.CompilerParams(
            collective_id=0, has_side_effects=True, vmem_limit_bytes=56541184
        ),
        cost_estimate=pl.CostEstimate(
            flops=2 * n * CAP // 8 * BLOCKS * COLS,
            bytes_accessed=300000,
            transcendentals=n * CAP // 8 * POINTS,
        ),
    )(
        heat_levels.reshape(1, 1),
        sum_over_states_ratio.reshape(1, 1),
        tallies_per_shard,
        natural_logged_absorbance.reshape(tiles, 128),
        lower_state_level.reshape(tiles, 128),
        subgrid_shift_ratio.reshape(tiles, 128),
        local_grid_slot.reshape(tiles, 128),
        broadening_class.reshape(tiles, 128),
        shape_kernels[0],
    )
    return result.reshape(1, G)


def solution(mesh):
    in_specs = (
        P("seg"),
        P("seg"),
        P("seg"),
        P("seg"),
        P("seg"),
        P(),
        P("tp"),
        P("tp"),
        P("tp", None, None),
    )
    out_specs = P("tp", "seg")
    return jax.shard_map(body, mesh=mesh, in_specs=in_specs, out_specs=out_specs, check_vma=False)
```

```python
import functools

import jax
import jax.numpy as jnp
from jax import lax
from jax.experimental import pallas as pl
from jax.experimental.pallas import tpu as pltpu
from jax.sharding import PartitionSpec as P

MESH = pl.DeviceIdType.MESH

G = 2048
NW = 16
POINTS = 8
CAP = 768
FIELDS = 5
J = 9
JW = 8 * NW
COLS = POINTS * JW + JW
BLOCKS = G // 8
PARTS = CAP // 128
SPAN = 384
REACH = 272
PACK = 4

planck_hc_over_boltzmann = 1.4388
baseline_heat_level = 900.0


def split(x):
    high = x.astype(jnp.bfloat16)
    return high, (x - high.astype(jnp.float32)).astype(jnp.bfloat16)


def kernel(
    n,
    heat_ref,
    ratio_ref,
    tallies_ref,
    absorb_ref,
    level_ref,
    shift_ref,
    slot_ref,
    class_ref,
    shape_ref,
    out_ref,
    heat,
    ratio,
    tallies,
    absorb,
    level,
    shift,
    slot,
    width,
    slot_value,
    width_value,
    starts,
    send,
    recv,
    points,
    shapes,
    rows0,
    cols0,
    rows1,
    cols1,
    acc,
    taps_high,
    taps_low,
    bins_high,
    bins_low,
    main_send,
    left_send,
    right_send,
    main_recv,
    left_recv,
    right_recv,
    ordered,
    in_sem,
    send_sem,
    first_sem,
    recv_sem,
    point_send_sem,
    point_sem,
    shape_send_sem,
    shape_sem,
    main_send_sem,
    main_sem,
    halo_send_sem,
    halo_sem,
):
    me = lax.axis_index("seg")
    tp = lax.axis_index("tp")
    left = lax.rem(me + n - 1, n)
    right = lax.rem(me + 1, n)

    tiles = slot.shape[0]
    eight = pl.multiple_of((me // 8) * 8, 8)
    copies = [
        pltpu.make_async_copy(src, dst, in_sem.at[k])
        for k, (src, dst) in enumerate(
            (
                (heat_ref, heat),
                (ratio_ref, ratio),
                (tallies_ref.at[pl.ds(eight, 8)], tallies),
                (absorb_ref, absorb.at[pl.ds(0, tiles)]),
                (level_ref, level.at[pl.ds(0, tiles)]),
                (shift_ref, shift.at[pl.ds(0, tiles)]),
                (slot_ref, slot),
                (class_ref, width),
                (shape_ref, shapes.at[0]),
            )
        )
    ]
    for copy in copies:
        copy.start()

    eighth = lax.rem(tp + n - lax.rem(me, 8), 8)
    stays = eighth == lax.rem(me, 8)
    octets = n // 8

    def partner(i):
        return eighth + 8 * lax.rem(me // 8 + i, octets)

    barrier = pltpu.get_barrier_semaphore()

    def greet(segment, point):
        pl.semaphore_signal(
            barrier, inc=1, device_id=(segment, point), device_id_type=MESH
        )

    for i in range(octets):
        if i == 0:
            pl.when(jnp.logical_not(stays))(lambda: greet(partner(0), tp))
        else:
            greet(partner(i), tp)
    for i in range(1, POINTS):
        for segment in (me, left, right):
            greet(segment, lax.rem(tp + i, POINTS))
    greet(left, tp)
    greet(right, tp)

    lane8 = lax.broadcasted_iota(jnp.int32, (8, 128), 1)
    sub8 = lax.broadcasted_iota(jnp.int32, (8, 128), 0)
    acc[...] = jnp.zeros_like(acc)

    for copy in copies[:3]:
        copy.wait()

    points[0] = jnp.where(lane8[:1] < 64, heat[0, 0], ratio[0, 0])

    def add_up(d, total):
        for u in range(8):
            starts[8 * d + u] = total
            total = total + tallies[lax.rem(me, 8), 8 * d + u]
        return total

    lax.fori_loop(0, octets, add_up, jnp.int32(0))

    for copy in copies[3:]:
        copy.wait()

    fields = (absorb, level, shift, slot_value, width_value)
    slot_value[pl.ds(0, tiles)] = slot[...].astype(jnp.float32)
    width_value[pl.ds(0, tiles)] = width[...].astype(jnp.float32)
    for field in fields:
        field[pl.ds(tiles, 16)] = jnp.zeros((16, 128), jnp.float32)
    position = 128 * sub8 + lane8

    def pack(target):
        begin = starts[target]
        count = tallies[lax.rem(me, 8), target]
        tile = lax.shift_right_logical(begin, 7)
        offset = jnp.full((8, 128), lax.bitwise_and(begin, 127))
        here, after = pl.ds(tile, 8), pl.ds(tile + 1, 8)
        windows = []
        for f, field in enumerate(fields):
            window = jnp.where(lane8 >= offset, field[here, :], field[after, :])
            for unit in (1, 4, 16):
                digit = lax.bitwise_and(offset, 3 * unit)
                turned = [pltpu.roll(window, 128 - k * unit, 1) for k in (1, 2, 3)]
                for k in (1, 2, 3):
                    window = jnp.where(digit == k * unit, turned[k - 1], window)
            turned = pltpu.roll(window, 64, 1)
            window = jnp.where(offset >= 64, turned, window)
            if f == FIELDS - 1:
                window = jnp.where(position >= count, float(NW), window)
            windows.append(window[:PARTS])
        return windows

    def pack_some(batch, _):
        first = batch * PACK
        packed = [pack(partner(first + u)) for u in range(PACK)]
        for u in range(PACK):
            for f in range(FIELDS):
                send[first + u, f] = packed[u][f]
        return 0

    lax.fori_loop(0, octets // PACK, pack_some, 0)

    pl.semaphore_wait(barrier, octets + 2 + 3 * (POINTS - 1) - jnp.where(stays, 1, 0))

    def share(src, dst, sem_send, sem_recv):
        for i in range(1, POINTS):
            pltpu.make_async_remote_copy(
                src_ref=src.at[0],
                dst_ref=dst.at[i],
                send_sem=sem_send,
                recv_sem=sem_recv,
                device_id=(me, lax.rem(tp + i, POINTS)),
                device_id_type=MESH,
            ).start()

    def lines_to(i, sem):
        return pltpu.make_async_remote_copy(
            src_ref=send.at[i],
            dst_ref=recv.at[i],
            send_sem=sem,
            recv_sem=recv_sem.at[i],
            device_id=(partner(i), tp),
            device_id_type=MESH,
        )

    pl.when(jnp.logical_not(stays))(lambda: lines_to(0, first_sem).start())
    pl.when(stays)(
        lambda: pltpu.make_async_copy(
            send.at[0], recv.at[0], recv_sem.at[0]
        ).start()
    )
    share(points, points, point_send_sem, point_sem)
    for i in range(1, octets):
        lines_to(i, send_sem).start()
    share(shapes, shapes, shape_send_sem, shape_sem)

    def all_points(src, dst, sem_send, sem_recv):
        return pltpu.make_async_remote_copy(
            src_ref=src.at[pl.ds(1, POINTS - 1)],
            dst_ref=dst.at[pl.ds(1, POINTS - 1)],
            send_sem=sem_send,
            recv_sem=sem_recv,
            device_id=(me, lax.rem(tp + 1, POINTS)),
            device_id_type=MESH,
        )

    all_points(points, points, point_send_sem, point_sem).wait_recv()
    both = jnp.concatenate([points[i] for i in range(POINTS)], axis=0)
    heats = jnp.where(lane8 < 64, both, pltpu.roll(both, 64, 1))
    ratios = jnp.where(lane8 < 64, pltpu.roll(both, 64, 1), both)
    inverse_gap = 1.0 / heats - 1.0 / baseline_heat_level

    block_ids = lax.broadcasted_iota(jnp.int32, (128, BLOCKS), 1).astype(jnp.float32)
    width_ids = lax.broadcasted_iota(jnp.int32, (NW, 128), 0).astype(jnp.float32)
    width_row = lax.broadcasted_iota(jnp.int32, (JW, SPAN), 0)

    def spread(row):
        return jnp.broadcast_to(row, (NW, 128)).astype(jnp.bfloat16)

    def arrived(g):
        pltpu.make_async_remote_copy(
            src_ref=send.at[g],
            dst_ref=recv.at[g],
            send_sem=send_sem,
            recv_sem=recv_sem.at[g],
            device_id=(partner(1), tp),
            device_id_type=MESH,
        ).wait_recv()

    def one_hots(g, rows, cols):
        absorbs, levels, shifts, slots, widths = (recv[g, f] for f in range(FIELDS))
        blocks = jnp.floor(slots * 0.125)
        cells = slots - 8.0 * blocks
        halves = cells * 0.5
        even_cell = jnp.where(halves == jnp.floor(halves), 1.0, 0.0)
        here = [cells == float(j) for j in range(8)]
        touched = [
            here[0],
            *(jnp.logical_or(here[j], here[j - 1]) for j in range(1, 8)),
            here[7],
        ]
        touched = [jnp.where(t, 1.0, 0.0) for t in touched]
        tall = jnp.concatenate([blocks, blocks[: 8 - PARTS]], axis=0).T
        scaled = planck_hc_over_boltzmann * levels
        below = 1.0 - shifts

        def one_hot(part):
            line = slice(part, part + 1)
            at = part * 128
            hits = jnp.broadcast_to(tall[:, line], (128, BLOCKS)) == block_ids
            rows[pl.ds(at, 128), :] = jnp.where(hits, 1.0, 0.0).astype(jnp.bfloat16)
            strength = ratios * jnp.exp(absorbs[line] - scaled[line] * inverse_gap)
            low = strength * below[line]
            high = strength * shifts[line]
            is_even = jnp.broadcast_to(even_cell[line], (POINTS, 128)) > 0.5
            evens = jnp.where(is_even, low, high)
            odds = jnp.where(is_even, high, low)
            is_width = jnp.broadcast_to(widths[line], (NW, 128)) == width_ids
            is_width = jnp.where(is_width, 1.0, 0.0).astype(jnp.bfloat16)
            cell_hits = [spread(t[line]) for t in touched]
            for p in range(POINTS):
                even = spread(evens[p : p + 1]) * is_width
                odd = spread(odds[p : p + 1]) * is_width
                for j in range(J):
                    top = p * JW + j * NW if j < 8 else POINTS * JW + p * NW
                    value = (odd if j % 2 else even) * cell_hits[j]
                    cols[pl.ds(top, NW), pl.ds(at, 128)] = value

        return [functools.partial(one_hot, part) for part in range(PARTS)]

    def add_product(piece, rows, cols):
        some = pl.ds(piece * (COLS // PARTS), COLS // PARTS)
        acc[some] += jnp.dot(
            cols[some], rows[...], preferred_element_type=jnp.float32
        )

    def make_taps(p):
        taps = jnp.concatenate([shapes[p], jnp.zeros((NW, 128), jnp.float32)], axis=1)
        moved = [taps] + [pltpu.roll(taps, j, 1) for j in range(1, J)]
        ninth = jnp.concatenate([moved[8]] * POINTS, axis=0)
        ninth = jnp.where(width_row // NW == p, ninth, 0.0)
        every = jnp.concatenate(moved[:8] + [ninth], axis=0)
        high, low = split(every.T[:REACH])
        taps_high[p] = high
        taps_low[p] = low

    def step(g, rows, cols, last_rows, last_cols):
        arrived(g)
        for part, make in enumerate(one_hots(g, rows, cols)):
            make()
            add_product(part, last_rows, last_cols)
        make_taps(g)

    arrived(0)
    for make in one_hots(0, rows0, cols0):
        make()
    all_points(shapes, shapes, shape_send_sem, shape_sem).wait_recv()

    def deposit(h, _):
        step(2 * h + 1, rows1, cols1, rows0, cols0)
        step(2 * h + 2, rows0, cols0, rows1, cols1)
        return 0

    lax.fori_loop(0, octets // 2 - 1, deposit, 0)
    step(octets - 1, rows1, cols1, rows0, cols0)
    make_taps(0)
    for piece in range(PARTS):
        add_product(piece, rows1, cols1)
    high, low = split(acc[...])
    bins_high[...] = high
    bins_low[...] = low

    def fold(x):
        kept = jnp.where(lane8 < 16, x, 0.0)
        moved = pltpu.roll(kept, 0, 1, stride=16, stride_axis=0)
        return jnp.sum(moved, axis=0, keepdims=True)

    def unfold(row):
        wide = jnp.broadcast_to(row, (8, 128))
        moved = wide
        for i in range(1, 8):
            moved = jnp.where(sub8 == i, pltpu.roll(wide, 128 - 16 * i, 1), moved)
        return jnp.where(lane8 < 16, moved, 0.0)

    def convolve(p):
        own = pl.ds(pl.multiple_of(p * JW, JW), JW)
        ninth = pl.ds(POINTS * JW, JW)
        bin_high = jnp.concatenate([bins_high[own], bins_high[ninth]], axis=0)
        bin_low = jnp.concatenate([bins_low[own], bins_low[ninth]], axis=0)
        product = jnp.dot(taps_high[p], bin_high, preferred_element_type=jnp.float32)
        product += jnp.dot(taps_low[p], bin_high, preferred_element_type=jnp.float32)
        product += jnp.dot(taps_high[p], bin_low, preferred_element_type=jnp.float32)
        first, second = product[128:136, :128], product[128:136, 128:]
        outside = jnp.zeros((8, 128), jnp.float32)
        for m in range(33):
            by = m - 16
            if by == 0:
                continue
            front, back = product[8 * m : 8 * m + 8, :128], product[8 * m : 8 * m + 8, 128:]
            front = pltpu.roll(front, by % 128, 1)
            back = pltpu.roll(back, by % 128, 1)
            if by > 0:
                wraps = lane8 < by
                first += jnp.where(wraps, 0.0, front)
                second += jnp.where(wraps, front, back)
                outside += jnp.where(wraps, back, 0.0)
            else:
                wraps = lane8 >= 128 + by
                first += jnp.where(wraps, back, front)
                second += jnp.where(wraps, 0.0, back)
                outside += jnp.where(wraps, front, 0.0)
        main_send[p, 0] = first
        main_send[p, 1] = second
        left_send[p] = fold(pltpu.roll(outside, 16, 1))
        right_send[p] = fold(outside)

    def send_sums(p):
        point = lax.rem(tp + POINTS - p, POINTS)

        @pl.when(p > 0)
        def _():
            pltpu.make_async_remote_copy(
                src_ref=main_send.at[p],
                dst_ref=main_recv.at[p],
                send_sem=main_send_sem,
                recv_sem=main_sem,
                device_id=(me, point),
                device_id_type=MESH,
            ).start()

        for k, (src, dst, segment) in enumerate(
            ((left_send, left_recv, left), (right_send, right_recv, right))
        ):
            pltpu.make_async_remote_copy(
                src_ref=src.at[p],
                dst_ref=dst.at[p],
                send_sem=halo_send_sem.at[k],
                recv_sem=halo_sem.at[k],
                device_id=(segment, point),
                device_id_type=MESH,
            ).start()

    def convolve_two(h, _):
        pair = (POINTS // 2 + h, POINTS // 2 - 1 - h)
        for p in pair:
            convolve(p)
        for p in pair:
            send_sums(p)
        return 0

    lax.fori_loop(0, POINTS // 2, convolve_two, 0)

    sums = all_points(main_send, main_recv, main_send_sem, main_sem)
    halos = [
        pltpu.make_async_remote_copy(
            src_ref=src,
            dst_ref=dst,
            send_sem=halo_send_sem.at[k],
            recv_sem=halo_sem.at[k],
            device_id=(segment, tp),
            device_id_type=MESH,
        )
        for k, (src, dst, segment) in enumerate(
            ((left_send, left_recv, left), (right_send, right_recv, right))
        )
    ]
    for halo in halos:
        halo.wait_recv()
    from_right = unfold(jnp.sum(left_recv[...], axis=0))
    from_left = unfold(jnp.sum(right_recv[...], axis=0))
    from_right = jnp.where(me < n - 1, pltpu.roll(from_right, 112, 1), 0.0)
    from_left = jnp.where(me > 0, from_left, 0.0)
    first = main_send[0, 0] + from_left
    second = main_send[0, 1] + from_right
    sums.wait_recv()
    for p in range(1, POINTS):
        first += main_recv[p, 0]
        second += main_recv[p, 1]
    for k, part in enumerate((first, second)):
        tall = jnp.concatenate([part, jnp.zeros((120, 128), jnp.float32)], axis=0)
        ordered[pl.ds(128 * k, 128), :] = tall.T
    total = ordered[pl.ds(0, 16, stride=16), :]
    for k in range(1, 16):
        total += pltpu.roll(ordered[pl.ds(k, 16, stride=16), :], 8 * k, 1)
    out_ref[...] = total

    all_points(points, points, point_send_sem, point_sem).wait_send()
    all_points(shapes, shapes, shape_send_sem, shape_sem).wait_send()
    pl.when(jnp.logical_not(stays))(lambda: lines_to(0, first_sem).wait_send())
    pltpu.make_async_remote_copy(
        src_ref=send.at[pl.ds(1, octets - 1)],
        dst_ref=recv.at[pl.ds(1, octets - 1)],
        send_sem=send_sem,
        recv_sem=recv_sem.at[1],
        device_id=(partner(1), tp),
        device_id_type=MESH,
    ).wait_send()
    sums.wait_send()
    for halo in halos:
        halo.wait_send()


def body(
    natural_logged_absorbance,
    lower_state_level,
    subgrid_shift_ratio,
    local_grid_slot,
    broadening_class,
    tallies_per_shard,
    heat_levels,
    sum_over_states_ratio,
    shape_kernels,
):
    n = lax.axis_size("seg")
    lines = natural_logged_absorbance.shape[0]
    tiles = lines // 128
    hbm = pl.BlockSpec(memory_space=pl.ANY)
    vmem = pl.BlockSpec(memory_space=pltpu.VMEM)
    f32, bf16, i32 = jnp.float32, jnp.bfloat16, jnp.int32
    dma = pltpu.SemaphoreType.DMA
    result = pl.pallas_call(
        functools.partial(kernel, n),
        out_shape=jax.ShapeDtypeStruct((16, 128), f32),
        in_specs=[hbm] * 9,
        out_specs=vmem,
        scratch_shapes=[
            pltpu.SMEM((1, 1), f32),
            pltpu.SMEM((1, 1), f32),
            pltpu.SMEM((8, n), i32),
            pltpu.VMEM((tiles + 16, 128), f32),
            pltpu.VMEM((tiles + 16, 128), f32),
            pltpu.VMEM((tiles + 16, 128), f32),
            pltpu.VMEM((tiles, 128), i32),
            pltpu.VMEM((tiles, 128), i32),
            pltpu.VMEM((tiles + 16, 128), f32),
            pltpu.VMEM((tiles + 16, 128), f32),
            pltpu.SMEM((n,), i32),
            pltpu.VMEM((n // 8, FIELDS, PARTS, 128), f32),
            pltpu.VMEM((n // 8, FIELDS, PARTS, 128), f32),
            pltpu.VMEM((POINTS, 1, 128), f32),
            pltpu.VMEM((POINTS, NW, 256), f32),
            pltpu.VMEM((CAP, BLOCKS), bf16),
            pltpu.VMEM((COLS, CAP), bf16),
            pltpu.VMEM((CAP, BLOCKS), bf16),
            pltpu.VMEM((COLS, CAP), bf16),
            pltpu.VMEM((COLS, BLOCKS), f32),
            pltpu.VMEM((POINTS, REACH, 2 * JW), bf16),
            pltpu.VMEM((POINTS, REACH, 2 * JW), bf16),
            pltpu.VMEM((COLS, BLOCKS), bf16),
            pltpu.VMEM((COLS, BLOCKS), bf16),
            pltpu.VMEM((POINTS, 2, 8, 128), f32),
            pltpu.VMEM((POINTS, 1, 128), f32),
            pltpu.VMEM((POINTS, 1, 128), f32),
            pltpu.VMEM((POINTS, 2, 8, 128), f32),
            pltpu.VMEM((POINTS, 1, 128), f32),
            pltpu.VMEM((POINTS, 1, 128), f32),
            pltpu.VMEM((BLOCKS, 128), f32),
            dma((9,)),
            dma,
            dma,
            dma((n // 8,)),
            dma,
            dma,
            dma,
            dma,
            dma,
            dma,
            dma((2,)),
            dma((2,)),
        ],
        compiler_params=pltpu.CompilerParams(
            collective_id=0, has_side_effects=True, vmem_limit_bytes=56541184
        ),
        cost_estimate=pl.CostEstimate(
            flops=2 * n * CAP // 8 * BLOCKS * COLS,
            bytes_accessed=300000,
            transcendentals=n * CAP // 8 * POINTS,
        ),
    )(
        heat_levels.reshape(1, 1),
        sum_over_states_ratio.reshape(1, 1),
        tallies_per_shard,
        natural_logged_absorbance.reshape(tiles, 128),
        lower_state_level.reshape(tiles, 128),
        subgrid_shift_ratio.reshape(tiles, 128),
        local_grid_slot.reshape(tiles, 128),
        broadening_class.reshape(tiles, 128),
        shape_kernels[0],
    )
    return result.reshape(1, G)


def solution(mesh):
    in_specs = (
        P("seg"),
        P("seg"),
        P("seg"),
        P("seg"),
        P("seg"),
        P(),
        P("tp"),
        P("tp"),
        P("tp", None, None),
    )
    out_specs = P("tp", "seg")
    return jax.shard_map(body, mesh=mesh, in_specs=in_specs, out_specs=out_specs, check_vma=False)
```

```python
import functools

import jax
import jax.numpy as jnp
from jax import lax
from jax.experimental import pallas as pl
from jax.experimental.pallas import tpu as pltpu
from jax.sharding import PartitionSpec as P

MESH = pl.DeviceIdType.MESH

G = 2048
NW = 16
POINTS = 8
CAP = 768
FIELDS = 5
J = 9
JW = 8 * NW
COLS = POINTS * JW + JW
BLOCKS = G // 8
PARTS = CAP // 128
REACH = 272
PACK = 4

planck_hc_over_boltzmann = 1.4388
baseline_heat_level = 900.0


def split(x):
    high = x.astype(jnp.bfloat16)
    return high, (x - high.astype(jnp.float32)).astype(jnp.bfloat16)


def kernel(
    n,
    heat_ref,
    ratio_ref,
    tallies_ref,
    absorb_ref,
    level_ref,
    shift_ref,
    slot_ref,
    class_ref,
    shape_ref,
    out_ref,
    heat,
    ratio,
    tallies,
    absorb,
    level,
    shift,
    slot,
    width,
    slot_value,
    width_value,
    starts,
    send,
    recv,
    points,
    shapes,
    rows0,
    cols0,
    rows1,
    cols1,
    acc,
    taps_high,
    taps_low,
    bins_high,
    bins_low,
    main_send,
    left_send,
    right_send,
    main_recv,
    left_recv,
    right_recv,
    ordered,
    in_sem,
    send_sem,
    first_sem,
    recv_sem,
    point_send_sem,
    point_sem,
    shape_send_sem,
    shape_sem,
    main_send_sem,
    main_sem,
    halo_send_sem,
    halo_sem,
):
    me = lax.axis_index("seg")
    tp = lax.axis_index("tp")
    left = lax.rem(me + n - 1, n)
    right = lax.rem(me + 1, n)

    tiles = slot.shape[0]
    eight = pl.multiple_of((me // 8) * 8, 8)
    copies = [
        pltpu.make_async_copy(src, dst, in_sem.at[k])
        for k, (src, dst) in enumerate(
            (
                (heat_ref, heat),
                (ratio_ref, ratio),
                (tallies_ref.at[pl.ds(eight, 8)], tallies),
                (absorb_ref, absorb.at[pl.ds(0, tiles)]),
                (level_ref, level.at[pl.ds(0, tiles)]),
                (shift_ref, shift.at[pl.ds(0, tiles)]),
                (slot_ref, slot),
                (class_ref, width),
                (shape_ref, shapes.at[0]),
            )
        )
    ]
    for copy in copies:
        copy.start()

    eighth = lax.rem(tp + n - lax.rem(me, 8), 8)
    stays = eighth == lax.rem(me, 8)
    octets = n // 8

    def partner(i):
        return eighth + 8 * lax.rem(me // 8 + i, octets)

    barrier = pltpu.get_barrier_semaphore()

    def greet(segment, point):
        pl.semaphore_signal(
            barrier, inc=1, device_id=(segment, point), device_id_type=MESH
        )

    for i in range(octets):
        if i == 0:
            pl.when(jnp.logical_not(stays))(lambda: greet(partner(0), tp))
        else:
            greet(partner(i), tp)
    for i in range(1, POINTS):
        for segment in (me, left, right):
            greet(segment, lax.rem(tp + i, POINTS))
    greet(left, tp)
    greet(right, tp)

    lane8 = lax.broadcasted_iota(jnp.int32, (8, 128), 1)
    sub8 = lax.broadcasted_iota(jnp.int32, (8, 128), 0)
    acc[...] = jnp.zeros_like(acc)

    for copy in copies[:3]:
        copy.wait()

    points[0] = jnp.where(lane8[:1] < 64, heat[0, 0], ratio[0, 0])

    def add_up(d, total):
        for u in range(8):
            starts[8 * d + u] = total
            total = total + tallies[lax.rem(me, 8), 8 * d + u]
        return total

    lax.fori_loop(0, octets, add_up, jnp.int32(0))

    for copy in copies[3:]:
        copy.wait()

    fields = (absorb, level, shift, slot_value, width_value)
    slot_value[pl.ds(0, tiles)] = slot[...].astype(jnp.float32)
    width_value[pl.ds(0, tiles)] = width[...].astype(jnp.float32)
    for field in fields:
        field[pl.ds(tiles, 16)] = jnp.zeros((16, 128), jnp.float32)
    position = 128 * sub8 + lane8

    def pack(target):
        begin = starts[target]
        count = tallies[lax.rem(me, 8), target]
        tile = lax.shift_right_logical(begin, 7)
        offset = jnp.full((8, 128), lax.bitwise_and(begin, 127))
        here, after = pl.ds(tile, 8), pl.ds(tile + 1, 8)
        windows = []
        for f, field in enumerate(fields):
            window = jnp.where(lane8 >= offset, field[here, :], field[after, :])
            for unit in (1, 4, 16):
                digit = lax.bitwise_and(offset, 3 * unit)
                turned = [pltpu.roll(window, 128 - k * unit, 1) for k in (1, 2, 3)]
                for k in (1, 2, 3):
                    window = jnp.where(digit == k * unit, turned[k - 1], window)
            turned = pltpu.roll(window, 64, 1)
            window = jnp.where(offset >= 64, turned, window)
            if f == FIELDS - 1:
                window = jnp.where(position >= count, float(NW), window)
            windows.append(window[:PARTS])
        return windows

    def pack_some(batch, _):
        first = batch * PACK
        packed = [pack(partner(first + u)) for u in range(PACK)]
        for u in range(PACK):
            for f in range(FIELDS):
                send[first + u, f] = packed[u][f]
        return 0

    lax.fori_loop(0, octets // PACK, pack_some, 0)

    pl.semaphore_wait(barrier, octets + 2 + 3 * (POINTS - 1) - jnp.where(stays, 1, 0))

    def share(src, dst, sem_send, sem_recv):
        for i in range(1, POINTS):
            pltpu.make_async_remote_copy(
                src_ref=src.at[0],
                dst_ref=dst.at[i],
                send_sem=sem_send,
                recv_sem=sem_recv,
                device_id=(me, lax.rem(tp + i, POINTS)),
                device_id_type=MESH,
            ).start()

    def lines_to(i, sem):
        return pltpu.make_async_remote_copy(
            src_ref=send.at[i],
            dst_ref=recv.at[i],
            send_sem=sem,
            recv_sem=recv_sem.at[i],
            device_id=(partner(i), tp),
            device_id_type=MESH,
        )

    pl.when(jnp.logical_not(stays))(lambda: lines_to(0, first_sem).start())
    pl.when(stays)(
        lambda: pltpu.make_async_copy(
            send.at[0], recv.at[0], recv_sem.at[0]
        ).start()
    )
    share(points, points, point_send_sem, point_sem)
    for i in range(1, octets):
        lines_to(i, send_sem).start()
    share(shapes, shapes, shape_send_sem, shape_sem)

    def all_points(src, dst, sem_send, sem_recv):
        return pltpu.make_async_remote_copy(
            src_ref=src.at[pl.ds(1, POINTS - 1)],
            dst_ref=dst.at[pl.ds(1, POINTS - 1)],
            send_sem=sem_send,
            recv_sem=sem_recv,
            device_id=(me, lax.rem(tp + 1, POINTS)),
            device_id_type=MESH,
        )

    all_points(points, points, point_send_sem, point_sem).wait_recv()
    both = jnp.concatenate([points[i] for i in range(POINTS)], axis=0)
    heats = jnp.where(lane8 < 64, both, pltpu.roll(both, 64, 1))
    ratios = jnp.where(lane8 < 64, pltpu.roll(both, 64, 1), both)
    inverse_gap = 1.0 / heats - 1.0 / baseline_heat_level

    block_ids = lax.broadcasted_iota(jnp.int32, (128, BLOCKS), 1).astype(jnp.float32)
    width_ids = lax.broadcasted_iota(jnp.int32, (NW, 128), 0).astype(jnp.float32)
    point_lane = lax.broadcasted_iota(jnp.int32, (REACH, JW), 1) // NW

    def spread(row):
        return jnp.broadcast_to(row, (NW, 128)).astype(jnp.bfloat16)

    def arrived(g):
        pltpu.make_async_remote_copy(
            src_ref=send.at[g],
            dst_ref=recv.at[g],
            send_sem=send_sem,
            recv_sem=recv_sem.at[g],
            device_id=(partner(1), tp),
            device_id_type=MESH,
        ).wait_recv()

    def one_hots(g, rows, cols):
        absorbs, levels, shifts, slots, widths = (recv[g, f] for f in range(FIELDS))
        blocks = jnp.floor(slots * 0.125)
        cells = slots - 8.0 * blocks
        halves = cells * 0.5
        even_cell = jnp.where(halves == jnp.floor(halves), 1.0, 0.0)
        here = [cells == float(j) for j in range(8)]
        touched = [
            here[0],
            *(jnp.logical_or(here[j], here[j - 1]) for j in range(1, 8)),
            here[7],
        ]
        touched = [jnp.where(t, 1.0, 0.0) for t in touched]
        tall = jnp.concatenate([blocks, blocks[: 8 - PARTS]], axis=0).T
        scaled = planck_hc_over_boltzmann * levels
        below = 1.0 - shifts

        def one_hot(part):
            line = slice(part, part + 1)
            at = part * 128
            hits = jnp.broadcast_to(tall[:, line], (128, BLOCKS)) == block_ids
            rows[pl.ds(at, 128), :] = jnp.where(hits, 1.0, 0.0).astype(jnp.bfloat16)
            strength = ratios * jnp.exp(absorbs[line] - scaled[line] * inverse_gap)
            low = strength * below[line]
            high = strength * shifts[line]
            is_even = jnp.broadcast_to(even_cell[line], (POINTS, 128)) > 0.5
            evens = jnp.where(is_even, low, high)
            odds = jnp.where(is_even, high, low)
            is_width = jnp.broadcast_to(widths[line], (NW, 128)) == width_ids
            is_width = jnp.where(is_width, 1.0, 0.0).astype(jnp.bfloat16)
            cell_hits = [spread(t[line]) for t in touched]
            for p in range(POINTS):
                even = spread(evens[p : p + 1]) * is_width
                odd = spread(odds[p : p + 1]) * is_width
                for j in range(J):
                    top = p * JW + j * NW if j < 8 else POINTS * JW + p * NW
                    value = (odd if j % 2 else even) * cell_hits[j]
                    cols[pl.ds(top, NW), pl.ds(at, 128)] = value

        return [functools.partial(one_hot, part) for part in range(PARTS)]

    def add_product(piece, rows, cols):
        some = pl.ds(piece * (COLS // PARTS), COLS // PARTS)
        acc[some] += jnp.dot(
            cols[some], rows[...], preferred_element_type=jnp.float32
        )

    def make_taps(p):
        taps = jnp.concatenate([shapes[p], jnp.zeros((NW, 128), jnp.float32)], axis=1)
        moved = [taps] + [pltpu.roll(taps, j, 1) for j in range(1, 8)]
        tall = jnp.concatenate(moved, axis=0).T[:REACH]
        ninth = jnp.concatenate([jnp.zeros((8, JW), jnp.float32), tall[:-8]], axis=0)
        ninth = jnp.where(point_lane == p, pltpu.roll(ninth, NW * p, 1), 0.0)
        high, low = split(jnp.concatenate([tall, ninth], axis=1))
        taps_high[p] = high
        taps_low[p] = low

    def step(g, rows, cols, last_rows, last_cols):
        arrived(g)
        for part, make in enumerate(one_hots(g, rows, cols)):
            make()
            add_product(part, last_rows, last_cols)
        make_taps(g)

    make_taps(0)
    arrived(0)
    for make in one_hots(0, rows0, cols0):
        make()
    all_points(shapes, shapes, shape_send_sem, shape_sem).wait_recv()

    def deposit(h, _):
        step(2 * h + 1, rows1, cols1, rows0, cols0)
        step(2 * h + 2, rows0, cols0, rows1, cols1)
        return 0

    lax.fori_loop(0, octets // 2 - 1, deposit, 0)
    step(octets - 1, rows1, cols1, rows0, cols0)
    for piece in range(PARTS):
        add_product(piece, rows1, cols1)
    high, low = split(acc[...])
    bins_high[...] = high
    bins_low[...] = low

    def fold(x):
        kept = jnp.where(lane8 < 16, x, 0.0)
        moved = pltpu.roll(kept, 0, 1, stride=16, stride_axis=0)
        return jnp.sum(moved, axis=0, keepdims=True)

    def unfold(row):
        wide = jnp.broadcast_to(row, (8, 128))
        moved = wide
        for i in range(1, 8):
            moved = jnp.where(sub8 == i, pltpu.roll(wide, 128 - 16 * i, 1), moved)
        return jnp.where(lane8 < 16, moved, 0.0)

    def convolve(p):
        own = pl.ds(pl.multiple_of(p * JW, JW), JW)
        ninth = pl.ds(POINTS * JW, JW)
        bin_high = jnp.concatenate([bins_high[own], bins_high[ninth]], axis=0)
        bin_low = jnp.concatenate([bins_low[own], bins_low[ninth]], axis=0)
        product = jnp.dot(taps_high[p], bin_high, preferred_element_type=jnp.float32)
        product += jnp.dot(taps_low[p], bin_high, preferred_element_type=jnp.float32)
        product += jnp.dot(taps_high[p], bin_low, preferred_element_type=jnp.float32)
        first, second = product[128:136, :128], product[128:136, 128:]
        outside = jnp.zeros((8, 128), jnp.float32)
        for m in range(33):
            by = m - 16
            if by == 0:
                continue
            front, back = product[8 * m : 8 * m + 8, :128], product[8 * m : 8 * m + 8, 128:]
            front = pltpu.roll(front, by % 128, 1)
            back = pltpu.roll(back, by % 128, 1)
            if by > 0:
                wraps = lane8 < by
                first += jnp.where(wraps, 0.0, front)
                second += jnp.where(wraps, front, back)
                outside += jnp.where(wraps, back, 0.0)
            else:
                wraps = lane8 >= 128 + by
                first += jnp.where(wraps, back, front)
                second += jnp.where(wraps, 0.0, back)
                outside += jnp.where(wraps, front, 0.0)
        main_send[p, 0] = first
        main_send[p, 1] = second
        left_send[p] = fold(pltpu.roll(outside, 16, 1))
        right_send[p] = fold(outside)

    def send_sums(p):
        point = lax.rem(tp + POINTS - p, POINTS)

        @pl.when(p > 0)
        def _():
            pltpu.make_async_remote_copy(
                src_ref=main_send.at[p],
                dst_ref=main_recv.at[p],
                send_sem=main_send_sem,
                recv_sem=main_sem,
                device_id=(me, point),
                device_id_type=MESH,
            ).start()

        for k, (src, dst, segment) in enumerate(
            ((left_send, left_recv, left), (right_send, right_recv, right))
        ):
            pltpu.make_async_remote_copy(
                src_ref=src.at[p],
                dst_ref=dst.at[p],
                send_sem=halo_send_sem.at[k],
                recv_sem=halo_sem.at[k],
                device_id=(segment, point),
                device_id_type=MESH,
            ).start()

    def convolve_two(h, _):
        pair = (POINTS // 2 + h, POINTS // 2 - 1 - h)
        for p in pair:
            convolve(p)
        for p in pair:
            send_sums(p)
        return 0

    lax.fori_loop(0, POINTS // 2, convolve_two, 0)

    sums = all_points(main_send, main_recv, main_send_sem, main_sem)
    halos = [
        pltpu.make_async_remote_copy(
            src_ref=src,
            dst_ref=dst,
            send_sem=halo_send_sem.at[k],
            recv_sem=halo_sem.at[k],
            device_id=(segment, tp),
            device_id_type=MESH,
        )
        for k, (src, dst, segment) in enumerate(
            ((left_send, left_recv, left), (right_send, right_recv, right))
        )
    ]
    for halo in halos:
        halo.wait_recv()
    from_right = unfold(jnp.sum(left_recv[...], axis=0))
    from_left = unfold(jnp.sum(right_recv[...], axis=0))
    from_right = jnp.where(me < n - 1, pltpu.roll(from_right, 112, 1), 0.0)
    from_left = jnp.where(me > 0, from_left, 0.0)
    first = main_send[0, 0] + from_left
    second = main_send[0, 1] + from_right
    sums.wait_recv()
    for p in range(1, POINTS):
        first += main_recv[p, 0]
        second += main_recv[p, 1]
    for k, part in enumerate((first, second)):
        tall = jnp.concatenate([part, jnp.zeros((120, 128), jnp.float32)], axis=0)
        ordered[pl.ds(128 * k, 128), :] = tall.T
    total = ordered[pl.ds(0, 16, stride=16), :]
    for k in range(1, 16):
        total += pltpu.roll(ordered[pl.ds(k, 16, stride=16), :], 8 * k, 1)
    out_ref[...] = total

    all_points(points, points, point_send_sem, point_sem).wait_send()
    all_points(shapes, shapes, shape_send_sem, shape_sem).wait_send()
    pl.when(jnp.logical_not(stays))(lambda: lines_to(0, first_sem).wait_send())
    pltpu.make_async_remote_copy(
        src_ref=send.at[pl.ds(1, octets - 1)],
        dst_ref=recv.at[pl.ds(1, octets - 1)],
        send_sem=send_sem,
        recv_sem=recv_sem.at[1],
        device_id=(partner(1), tp),
        device_id_type=MESH,
    ).wait_send()
    sums.wait_send()
    for halo in halos:
        halo.wait_send()


def body(
    natural_logged_absorbance,
    lower_state_level,
    subgrid_shift_ratio,
    local_grid_slot,
    broadening_class,
    tallies_per_shard,
    heat_levels,
    sum_over_states_ratio,
    shape_kernels,
):
    n = lax.axis_size("seg")
    lines = natural_logged_absorbance.shape[0]
    tiles = lines // 128
    hbm = pl.BlockSpec(memory_space=pl.ANY)
    vmem = pl.BlockSpec(memory_space=pltpu.VMEM)
    f32, bf16, i32 = jnp.float32, jnp.bfloat16, jnp.int32
    dma = pltpu.SemaphoreType.DMA
    result = pl.pallas_call(
        functools.partial(kernel, n),
        out_shape=jax.ShapeDtypeStruct((16, 128), f32),
        in_specs=[hbm] * 9,
        out_specs=vmem,
        scratch_shapes=[
            pltpu.SMEM((1, 1), f32),
            pltpu.SMEM((1, 1), f32),
            pltpu.SMEM((8, n), i32),
            pltpu.VMEM((tiles + 16, 128), f32),
            pltpu.VMEM((tiles + 16, 128), f32),
            pltpu.VMEM((tiles + 16, 128), f32),
            pltpu.VMEM((tiles, 128), i32),
            pltpu.VMEM((tiles, 128), i32),
            pltpu.VMEM((tiles + 16, 128), f32),
            pltpu.VMEM((tiles + 16, 128), f32),
            pltpu.SMEM((n,), i32),
            pltpu.VMEM((n // 8, FIELDS, PARTS, 128), f32),
            pltpu.VMEM((n // 8, FIELDS, PARTS, 128), f32),
            pltpu.VMEM((POINTS, 1, 128), f32),
            pltpu.VMEM((POINTS, NW, 256), f32),
            pltpu.VMEM((CAP, BLOCKS), bf16),
            pltpu.VMEM((COLS, CAP), bf16),
            pltpu.VMEM((CAP, BLOCKS), bf16),
            pltpu.VMEM((COLS, CAP), bf16),
            pltpu.VMEM((COLS, BLOCKS), f32),
            pltpu.VMEM((POINTS, REACH, 2 * JW), bf16),
            pltpu.VMEM((POINTS, REACH, 2 * JW), bf16),
            pltpu.VMEM((COLS, BLOCKS), bf16),
            pltpu.VMEM((COLS, BLOCKS), bf16),
            pltpu.VMEM((POINTS, 2, 8, 128), f32),
            pltpu.VMEM((POINTS, 1, 128), f32),
            pltpu.VMEM((POINTS, 1, 128), f32),
            pltpu.VMEM((POINTS, 2, 8, 128), f32),
            pltpu.VMEM((POINTS, 1, 128), f32),
            pltpu.VMEM((POINTS, 1, 128), f32),
            pltpu.VMEM((BLOCKS, 128), f32),
            dma((9,)),
            dma,
            dma,
            dma((n // 8,)),
            dma,
            dma,
            dma,
            dma,
            dma,
            dma,
            dma((2,)),
            dma((2,)),
        ],
        compiler_params=pltpu.CompilerParams(
            collective_id=0, has_side_effects=True, vmem_limit_bytes=56541184
        ),
        cost_estimate=pl.CostEstimate(
            flops=2 * n * CAP // 8 * BLOCKS * COLS,
            bytes_accessed=300000,
            transcendentals=n * CAP // 8 * POINTS,
        ),
    )(
        heat_levels.reshape(1, 1),
        sum_over_states_ratio.reshape(1, 1),
        tallies_per_shard,
        natural_logged_absorbance.reshape(tiles, 128),
        lower_state_level.reshape(tiles, 128),
        subgrid_shift_ratio.reshape(tiles, 128),
        local_grid_slot.reshape(tiles, 128),
        broadening_class.reshape(tiles, 128),
        shape_kernels[0],
    )
    return result.reshape(1, G)


def solution(mesh):
    in_specs = (
        P("seg"),
        P("seg"),
        P("seg"),
        P("seg"),
        P("seg"),
        P(),
        P("tp"),
        P("tp"),
        P("tp", None, None),
    )
    out_specs = P("tp", "seg")
    return jax.shard_map(body, mesh=mesh, in_specs=in_specs, out_specs=out_specs, check_vma=False)
```

```python
import functools

import jax
import jax.numpy as jnp
from jax import lax
from jax.experimental import pallas as pl
from jax.experimental.pallas import tpu as pltpu
from jax.sharding import PartitionSpec as P

MESH = pl.DeviceIdType.MESH

G = 2048
NW = 16
POINTS = 8
CAP = 768
FIELDS = 5
J = 9
JW = 8 * NW
COLS = POINTS * JW + JW
BLOCKS = G // 8
PARTS = CAP // 128
REACH = 272
PACK = 4

planck_hc_over_boltzmann = 1.4388
baseline_heat_level = 900.0


def split(x):
    high = x.astype(jnp.bfloat16)
    return high, (x - high.astype(jnp.float32)).astype(jnp.bfloat16)


def kernel(
    n,
    heat_ref,
    ratio_ref,
    tallies_ref,
    absorb_ref,
    level_ref,
    shift_ref,
    slot_ref,
    class_ref,
    shape_ref,
    out_ref,
    heat,
    ratio,
    tallies,
    absorb,
    level,
    shift,
    slot,
    width,
    slot_value,
    width_value,
    starts,
    send,
    recv,
    points,
    shapes,
    hits,
    weights,
    rows0,
    cols0,
    rows1,
    cols1,
    acc,
    taps_high,
    taps_low,
    bins_high,
    bins_low,
    main_send,
    left_send,
    right_send,
    main_recv,
    left_recv,
    right_recv,
    ordered,
    in_sem,
    send_sem,
    first_sem,
    recv_sem,
    point_send_sem,
    point_sem,
    shape_send_sem,
    shape_sem,
    main_send_sem,
    main_sem,
    halo_send_sem,
    halo_sem,
):
    me = lax.axis_index("seg")
    tp = lax.axis_index("tp")
    left = lax.rem(me + n - 1, n)
    right = lax.rem(me + 1, n)

    tiles = slot.shape[0]
    eight = pl.multiple_of((me // 8) * 8, 8)
    copies = [
        pltpu.make_async_copy(src, dst, in_sem.at[k])
        for k, (src, dst) in enumerate(
            (
                (heat_ref, heat),
                (ratio_ref, ratio),
                (tallies_ref.at[pl.ds(eight, 8)], tallies),
                (absorb_ref, absorb.at[pl.ds(0, tiles)]),
                (level_ref, level.at[pl.ds(0, tiles)]),
                (shift_ref, shift.at[pl.ds(0, tiles)]),
                (slot_ref, slot),
                (class_ref, width),
                (shape_ref, shapes.at[0]),
            )
        )
    ]
    for copy in copies:
        copy.start()

    eighth = lax.rem(tp + n - lax.rem(me, 8), 8)
    stays = eighth == lax.rem(me, 8)
    octets = n // 8

    def partner(i):
        return eighth + 8 * lax.rem(me // 8 + i, octets)

    barrier = pltpu.get_barrier_semaphore()

    def greet(segment, point):
        pl.semaphore_signal(
            barrier, inc=1, device_id=(segment, point), device_id_type=MESH
        )

    for i in range(octets):
        if i == 0:
            pl.when(jnp.logical_not(stays))(lambda: greet(partner(0), tp))
        else:
            greet(partner(i), tp)
    for i in range(1, POINTS):
        for segment in (me, left, right):
            greet(segment, lax.rem(tp + i, POINTS))
    greet(left, tp)
    greet(right, tp)

    lane8 = lax.broadcasted_iota(jnp.int32, (8, 128), 1)
    sub8 = lax.broadcasted_iota(jnp.int32, (8, 128), 0)
    acc[...] = jnp.zeros_like(acc)

    for copy in copies[:3]:
        copy.wait()

    points[0] = jnp.where(lane8[:1] < 64, heat[0, 0], ratio[0, 0])

    def add_up(d, total):
        for u in range(8):
            starts[8 * d + u] = total
            total = total + tallies[lax.rem(me, 8), 8 * d + u]
        return total

    lax.fori_loop(0, octets, add_up, jnp.int32(0))

    for copy in copies[3:]:
        copy.wait()

    fields = (absorb, level, shift, slot_value, width_value)
    slot_value[pl.ds(0, tiles)] = slot[...].astype(jnp.float32)
    width_value[pl.ds(0, tiles)] = width[...].astype(jnp.float32)
    for field in fields:
        field[pl.ds(tiles, 16)] = jnp.zeros((16, 128), jnp.float32)
    position = 128 * sub8 + lane8

    def pack(target):
        begin = starts[target]
        count = tallies[lax.rem(me, 8), target]
        tile = lax.shift_right_logical(begin, 7)
        offset = jnp.full((8, 128), lax.bitwise_and(begin, 127))
        here, after = pl.ds(tile, 8), pl.ds(tile + 1, 8)
        windows = []
        for f, field in enumerate(fields):
            window = jnp.where(lane8 >= offset, field[here, :], field[after, :])
            for unit in (1, 4, 16):
                digit = lax.bitwise_and(offset, 3 * unit)
                turned = [pltpu.roll(window, 128 - k * unit, 1) for k in (1, 2, 3)]
                for k in (1, 2, 3):
                    window = jnp.where(digit == k * unit, turned[k - 1], window)
            turned = pltpu.roll(window, 64, 1)
            window = jnp.where(offset >= 64, turned, window)
            if f == FIELDS - 1:
                window = jnp.where(position >= count, float(NW), window)
            windows.append(window[:PARTS])
        return windows

    def pack_some(batch, _):
        first = batch * PACK
        packed = [pack(partner(first + u)) for u in range(PACK)]
        for u in range(PACK):
            for f in range(FIELDS):
                send[first + u, f] = packed[u][f]
        return 0

    lax.fori_loop(0, octets // PACK, pack_some, 0)

    pl.semaphore_wait(barrier, octets + 2 + 3 * (POINTS - 1) - jnp.where(stays, 1, 0))

    def share(src, dst, sem_send, sem_recv):
        for i in range(1, POINTS):
            pltpu.make_async_remote_copy(
                src_ref=src.at[0],
                dst_ref=dst.at[i],
                send_sem=sem_send,
                recv_sem=sem_recv,
                device_id=(me, lax.rem(tp + i, POINTS)),
                device_id_type=MESH,
            ).start()

    def lines_to(i, sem):
        return pltpu.make_async_remote_copy(
            src_ref=send.at[i],
            dst_ref=recv.at[i],
            send_sem=sem,
            recv_sem=recv_sem.at[i],
            device_id=(partner(i), tp),
            device_id_type=MESH,
        )

    pl.when(jnp.logical_not(stays))(lambda: lines_to(0, first_sem).start())
    pl.when(stays)(
        lambda: pltpu.make_async_copy(
            send.at[0], recv.at[0], recv_sem.at[0]
        ).start()
    )
    share(points, points, point_send_sem, point_sem)
    for i in range(1, octets):
        lines_to(i, send_sem).start()
    share(shapes, shapes, shape_send_sem, shape_sem)

    def all_points(src, dst, sem_send, sem_recv):
        return pltpu.make_async_remote_copy(
            src_ref=src.at[pl.ds(1, POINTS - 1)],
            dst_ref=dst.at[pl.ds(1, POINTS - 1)],
            send_sem=sem_send,
            recv_sem=sem_recv,
            device_id=(me, lax.rem(tp + 1, POINTS)),
            device_id_type=MESH,
        )

    all_points(points, points, point_send_sem, point_sem).wait_recv()
    both = jnp.concatenate([points[i] for i in range(POINTS)], axis=0)
    heats = jnp.where(lane8 < 64, both, pltpu.roll(both, 64, 1))
    ratios = jnp.where(lane8 < 64, pltpu.roll(both, 64, 1), both)
    inverse_gap = 1.0 / heats - 1.0 / baseline_heat_level

    block_ids = lax.broadcasted_iota(jnp.int32, (128, BLOCKS), 1).astype(jnp.float32)
    width_ids = lax.broadcasted_iota(jnp.int32, (NW, 128), 0).astype(jnp.float32)
    point_lane = lax.broadcasted_iota(jnp.int32, (REACH, JW), 1) // NW

    def spread(row):
        return jnp.broadcast_to(row, (NW, 128)).astype(jnp.bfloat16)

    def arrived(g):
        pltpu.make_async_remote_copy(
            src_ref=send.at[g],
            dst_ref=recv.at[g],
            send_sem=send_sem,
            recv_sem=recv_sem.at[g],
            device_id=(partner(1), tp),
            device_id_type=MESH,
        ).wait_recv()

    def one_hots(g, rows, cols):
        blocks = jnp.floor(recv[g, 3] * 0.125)
        cells = recv[g, 3] - 8.0 * blocks
        halves = cells * 0.5
        here = [cells == float(j) for j in range(8)]
        touched = [
            here[0],
            *(jnp.logical_or(here[j], here[j - 1]) for j in range(1, 8)),
            here[7],
            halves == jnp.floor(halves),
        ]
        for j, hit in enumerate(touched):
            hits[j, pl.ds(0, PARTS)] = jnp.where(hit, 1.0, 0.0)
        tall = jnp.concatenate([blocks, blocks[: 8 - PARTS]], axis=0).T

        def one_hot(part):
            line = pl.ds(part, 1)
            at = part * 128

            def field(f, height):
                return jnp.broadcast_to(recv[g, f, line, :], (height, 128))

            in_block = jnp.broadcast_to(tall[:, part : part + 1], (128, BLOCKS)) == block_ids
            rows[pl.ds(at, 128), :] = jnp.where(in_block, 1.0, 0.0).astype(jnp.bfloat16)
            strength = ratios * jnp.exp(
                field(0, POINTS)
                - planck_hc_over_boltzmann * field(1, POINTS) * inverse_gap
            )
            low = strength * (1.0 - field(2, POINTS))
            high = strength * field(2, POINTS)
            is_even = jnp.broadcast_to(hits[J, line, :], (POINTS, 128)) > 0.5
            weights[part, 0] = jnp.where(is_even, low, high)
            weights[part, 1] = jnp.where(is_even, high, low)
            is_width = jnp.where(field(4, NW) == width_ids, 1.0, 0.0)
            is_width = is_width.astype(jnp.bfloat16)
            cell_hits = [spread(hits[j, line, :]) for j in range(J)]
            for p in range(POINTS):
                even, odd = (
                    spread(weights[part, k, pl.ds(p, 1), :]) * is_width for k in range(2)
                )
                for j in range(J):
                    top = p * JW + j * NW if j < 8 else POINTS * JW + p * NW
                    value = (odd if j % 2 else even) * cell_hits[j]
                    cols[pl.ds(top, NW), pl.ds(at, 128)] = value

        return [functools.partial(one_hot, part) for part in range(PARTS)]

    def add_product(piece, rows, cols):
        some = pl.ds(piece * (COLS // PARTS), COLS // PARTS)
        acc[some] += jnp.dot(
            cols[some], rows[...], preferred_element_type=jnp.float32
        )

    def make_taps(p):
        taps = jnp.concatenate([shapes[p], jnp.zeros((NW, 128), jnp.float32)], axis=1)
        moved = [taps] + [pltpu.roll(taps, j, 1) for j in range(1, 8)]
        tall = jnp.concatenate(moved, axis=0).T[:REACH]
        ninth = jnp.concatenate([jnp.zeros((8, JW), jnp.float32), tall[:-8]], axis=0)
        ninth = jnp.where(point_lane == p, pltpu.roll(ninth, NW * p, 1), 0.0)
        high, low = split(jnp.concatenate([tall, ninth], axis=1))
        taps_high[p] = high
        taps_low[p] = low

    def step(g, rows, cols, last_rows, last_cols):
        arrived(g)
        for part, make in enumerate(one_hots(g, rows, cols)):
            make()
            add_product(part, last_rows, last_cols)
        make_taps(g)

    make_taps(0)
    arrived(0)
    for make in one_hots(0, rows0, cols0):
        make()
    all_points(shapes, shapes, shape_send_sem, shape_sem).wait_recv()

    def deposit(h, _):
        step(2 * h + 1, rows1, cols1, rows0, cols0)
        step(2 * h + 2, rows0, cols0, rows1, cols1)
        return 0

    lax.fori_loop(0, octets // 2 - 1, deposit, 0)
    step(octets - 1, rows1, cols1, rows0, cols0)
    for piece in range(PARTS):
        add_product(piece, rows1, cols1)
    high, low = split(acc[...])
    bins_high[...] = high
    bins_low[...] = low

    def fold(x):
        kept = jnp.where(lane8 < 16, x, 0.0)
        moved = pltpu.roll(kept, 0, 1, stride=16, stride_axis=0)
        return jnp.sum(moved, axis=0, keepdims=True)

    def unfold(row):
        wide = jnp.broadcast_to(row, (8, 128))
        moved = wide
        for i in range(1, 8):
            moved = jnp.where(sub8 == i, pltpu.roll(wide, 128 - 16 * i, 1), moved)
        return jnp.where(lane8 < 16, moved, 0.0)

    def convolve(p):
        own = pl.ds(pl.multiple_of(p * JW, JW), JW)
        ninth = pl.ds(POINTS * JW, JW)
        bin_high = jnp.concatenate([bins_high[own], bins_high[ninth]], axis=0)
        bin_low = jnp.concatenate([bins_low[own], bins_low[ninth]], axis=0)
        product = jnp.dot(taps_high[p], bin_high, preferred_element_type=jnp.float32)
        product += jnp.dot(taps_low[p], bin_high, preferred_element_type=jnp.float32)
        product += jnp.dot(taps_high[p], bin_low, preferred_element_type=jnp.float32)
        first, second = product[128:136, :128], product[128:136, 128:]
        outside = jnp.zeros((8, 128), jnp.float32)
        for m in range(33):
            by = m - 16
            if by == 0:
                continue
            front, back = product[8 * m : 8 * m + 8, :128], product[8 * m : 8 * m + 8, 128:]
            front = pltpu.roll(front, by % 128, 1)
            back = pltpu.roll(back, by % 128, 1)
            if by > 0:
                wraps = lane8 < by
                first += jnp.where(wraps, 0.0, front)
                second += jnp.where(wraps, front, back)
                outside += jnp.where(wraps, back, 0.0)
            else:
                wraps = lane8 >= 128 + by
                first += jnp.where(wraps, back, front)
                second += jnp.where(wraps, 0.0, back)
                outside += jnp.where(wraps, front, 0.0)
        main_send[p, 0] = first
        main_send[p, 1] = second
        left_send[p] = fold(pltpu.roll(outside, 16, 1))
        right_send[p] = fold(outside)

    def send_sums(p):
        point = lax.rem(tp + POINTS - p, POINTS)

        @pl.when(p > 0)
        def _():
            pltpu.make_async_remote_copy(
                src_ref=main_send.at[p],
                dst_ref=main_recv.at[p],
                send_sem=main_send_sem,
                recv_sem=main_sem,
                device_id=(me, point),
                device_id_type=MESH,
            ).start()

        for k, (src, dst, segment) in enumerate(
            ((left_send, left_recv, left), (right_send, right_recv, right))
        ):
            pltpu.make_async_remote_copy(
                src_ref=src.at[p],
                dst_ref=dst.at[p],
                send_sem=halo_send_sem.at[k],
                recv_sem=halo_sem.at[k],
                device_id=(segment, point),
                device_id_type=MESH,
            ).start()

    def convolve_two(h, _):
        pair = (POINTS // 2 + h, POINTS // 2 - 1 - h)
        for p in pair:
            convolve(p)
        for p in pair:
            send_sums(p)
        return 0

    lax.fori_loop(0, POINTS // 2, convolve_two, 0)

    sums = all_points(main_send, main_recv, main_send_sem, main_sem)
    halos = [
        pltpu.make_async_remote_copy(
            src_ref=src,
            dst_ref=dst,
            send_sem=halo_send_sem.at[k],
            recv_sem=halo_sem.at[k],
            device_id=(segment, tp),
            device_id_type=MESH,
        )
        for k, (src, dst, segment) in enumerate(
            ((left_send, left_recv, left), (right_send, right_recv, right))
        )
    ]
    for halo in halos:
        halo.wait_recv()
    from_right = unfold(jnp.sum(left_recv[...], axis=0))
    from_left = unfold(jnp.sum(right_recv[...], axis=0))
    from_right = jnp.where(me < n - 1, pltpu.roll(from_right, 112, 1), 0.0)
    from_left = jnp.where(me > 0, from_left, 0.0)
    first = main_send[0, 0] + from_left
    second = main_send[0, 1] + from_right
    sums.wait_recv()
    for p in range(1, POINTS):
        first += main_recv[p, 0]
        second += main_recv[p, 1]
    for k, part in enumerate((first, second)):
        tall = jnp.concatenate([part, jnp.zeros((120, 128), jnp.float32)], axis=0)
        ordered[pl.ds(128 * k, 128), :] = tall.T
    total = ordered[pl.ds(0, 16, stride=16), :]
    for k in range(1, 16):
        total += pltpu.roll(ordered[pl.ds(k, 16, stride=16), :], 8 * k, 1)
    out_ref[...] = total

    all_points(points, points, point_send_sem, point_sem).wait_send()
    all_points(shapes, shapes, shape_send_sem, shape_sem).wait_send()
    pl.when(jnp.logical_not(stays))(lambda: lines_to(0, first_sem).wait_send())
    pltpu.make_async_remote_copy(
        src_ref=send.at[pl.ds(1, octets - 1)],
        dst_ref=recv.at[pl.ds(1, octets - 1)],
        send_sem=send_sem,
        recv_sem=recv_sem.at[1],
        device_id=(partner(1), tp),
        device_id_type=MESH,
    ).wait_send()
    sums.wait_send()
    for halo in halos:
        halo.wait_send()


def body(
    natural_logged_absorbance,
    lower_state_level,
    subgrid_shift_ratio,
    local_grid_slot,
    broadening_class,
    tallies_per_shard,
    heat_levels,
    sum_over_states_ratio,
    shape_kernels,
):
    n = lax.axis_size("seg")
    lines = natural_logged_absorbance.shape[0]
    tiles = lines // 128
    hbm = pl.BlockSpec(memory_space=pl.ANY)
    vmem = pl.BlockSpec(memory_space=pltpu.VMEM)
    f32, bf16, i32 = jnp.float32, jnp.bfloat16, jnp.int32
    dma = pltpu.SemaphoreType.DMA
    result = pl.pallas_call(
        functools.partial(kernel, n),
        out_shape=jax.ShapeDtypeStruct((16, 128), f32),
        in_specs=[hbm] * 9,
        out_specs=vmem,
        scratch_shapes=[
            pltpu.SMEM((1, 1), f32),
            pltpu.SMEM((1, 1), f32),
            pltpu.SMEM((8, n), i32),
            pltpu.VMEM((tiles + 16, 128), f32),
            pltpu.VMEM((tiles + 16, 128), f32),
            pltpu.VMEM((tiles + 16, 128), f32),
            pltpu.VMEM((tiles, 128), i32),
            pltpu.VMEM((tiles, 128), i32),
            pltpu.VMEM((tiles + 16, 128), f32),
            pltpu.VMEM((tiles + 16, 128), f32),
            pltpu.SMEM((n,), i32),
            pltpu.VMEM((n // 8, FIELDS, PARTS, 128), f32),
            pltpu.VMEM((n // 8, FIELDS, PARTS, 128), f32),
            pltpu.VMEM((POINTS, 1, 128), f32),
            pltpu.VMEM((POINTS, NW, 256), f32),
            pltpu.VMEM((J + 1, 8, 128), f32),
            pltpu.VMEM((PARTS, 2, POINTS, 128), f32),
            pltpu.VMEM((CAP, BLOCKS), bf16),
            pltpu.VMEM((COLS, CAP), bf16),
            pltpu.VMEM((CAP, BLOCKS), bf16),
            pltpu.VMEM((COLS, CAP), bf16),
            pltpu.VMEM((COLS, BLOCKS), f32),
            pltpu.VMEM((POINTS, REACH, 2 * JW), bf16),
            pltpu.VMEM((POINTS, REACH, 2 * JW), bf16),
            pltpu.VMEM((COLS, BLOCKS), bf16),
            pltpu.VMEM((COLS, BLOCKS), bf16),
            pltpu.VMEM((POINTS, 2, 8, 128), f32),
            pltpu.VMEM((POINTS, 1, 128), f32),
            pltpu.VMEM((POINTS, 1, 128), f32),
            pltpu.VMEM((POINTS, 2, 8, 128), f32),
            pltpu.VMEM((POINTS, 1, 128), f32),
            pltpu.VMEM((POINTS, 1, 128), f32),
            pltpu.VMEM((BLOCKS, 128), f32),
            dma((9,)),
            dma,
            dma,
            dma((n // 8,)),
            dma,
            dma,
            dma,
            dma,
            dma,
            dma,
            dma((2,)),
            dma((2,)),
        ],
        compiler_params=pltpu.CompilerParams(
            collective_id=0, has_side_effects=True, vmem_limit_bytes=56541184
        ),
        cost_estimate=pl.CostEstimate(
            flops=2 * n * CAP // 8 * BLOCKS * COLS,
            bytes_accessed=300000,
            transcendentals=n * CAP // 8 * POINTS,
        ),
    )(
        heat_levels.reshape(1, 1),
        sum_over_states_ratio.reshape(1, 1),
        tallies_per_shard,
        natural_logged_absorbance.reshape(tiles, 128),
        lower_state_level.reshape(tiles, 128),
        subgrid_shift_ratio.reshape(tiles, 128),
        local_grid_slot.reshape(tiles, 128),
        broadening_class.reshape(tiles, 128),
        shape_kernels[0],
    )
    return result.reshape(1, G)


def solution(mesh):
    in_specs = (
        P("seg"),
        P("seg"),
        P("seg"),
        P("seg"),
        P("seg"),
        P(),
        P("tp"),
        P("tp"),
        P("tp", None, None),
    )
    out_specs = P("tp", "seg")
    return jax.shard_map(body, mesh=mesh, in_specs=in_specs, out_specs=out_specs, check_vma=False)
```

```python
import functools

import jax
import jax.numpy as jnp
from jax import lax
from jax.experimental import pallas as pl
from jax.experimental.pallas import tpu as pltpu
from jax.sharding import PartitionSpec as P

MESH = pl.DeviceIdType.MESH

G = 2048
NW = 16
POINTS = 8
CAP = 768
FIELDS = 5
J = 9
JW = 8 * NW
COLS = POINTS * JW + JW
BLOCKS = G // 8
PARTS = CAP // 128
REACH = 272
PACK = 4

planck_hc_over_boltzmann = 1.4388
baseline_heat_level = 900.0


def split(x):
    high = x.astype(jnp.bfloat16)
    return high, (x - high.astype(jnp.float32)).astype(jnp.bfloat16)


def kernel(
    n,
    heat_ref,
    ratio_ref,
    tallies_ref,
    absorb_ref,
    level_ref,
    shift_ref,
    slot_ref,
    class_ref,
    shape_ref,
    out_ref,
    heat,
    ratio,
    tallies,
    absorb,
    level,
    shift,
    slot,
    width,
    slot_value,
    width_value,
    starts,
    send,
    recv,
    points,
    shapes,
    rows0,
    cols0,
    rows1,
    cols1,
    acc,
    taps_high,
    taps_low,
    bins_high,
    bins_low,
    main_send,
    left_send,
    right_send,
    main_recv,
    left_recv,
    right_recv,
    ordered,
    in_sem,
    send_sem,
    first_sem,
    recv_sem,
    point_send_sem,
    point_sem,
    shape_send_sem,
    shape_sem,
    main_send_sem,
    main_sem,
    halo_send_sem,
    halo_sem,
):
    me = lax.axis_index("seg")
    tp = lax.axis_index("tp")
    left = lax.rem(me + n - 1, n)
    right = lax.rem(me + 1, n)

    tiles = slot.shape[0]
    eight = pl.multiple_of((me // 8) * 8, 8)
    copies = [
        pltpu.make_async_copy(src, dst, in_sem.at[k])
        for k, (src, dst) in enumerate(
            (
                (heat_ref, heat),
                (ratio_ref, ratio),
                (tallies_ref.at[pl.ds(eight, 8)], tallies),
                (absorb_ref, absorb.at[pl.ds(0, tiles)]),
                (level_ref, level.at[pl.ds(0, tiles)]),
                (shift_ref, shift.at[pl.ds(0, tiles)]),
                (slot_ref, slot),
                (class_ref, width),
                (shape_ref, shapes.at[0]),
            )
        )
    ]
    for copy in copies:
        copy.start()

    eighth = lax.rem(tp + n - lax.rem(me, 8), 8)
    stays = eighth == lax.rem(me, 8)
    octets = n // 8

    def partner(i):
        return eighth + 8 * lax.rem(me // 8 + i, octets)

    barrier = pltpu.get_barrier_semaphore()

    def greet(segment, point):
        pl.semaphore_signal(
            barrier, inc=1, device_id=(segment, point), device_id_type=MESH
        )

    for i in range(octets):
        if i == 0:
            pl.when(jnp.logical_not(stays))(lambda: greet(partner(0), tp))
        else:
            greet(partner(i), tp)
    for i in range(1, POINTS):
        for segment in (me, left, right):
            greet(segment, lax.rem(tp + i, POINTS))
    greet(left, tp)
    greet(right, tp)

    lane8 = lax.broadcasted_iota(jnp.int32, (8, 128), 1)
    sub8 = lax.broadcasted_iota(jnp.int32, (8, 128), 0)
    acc[...] = jnp.zeros_like(acc)

    for copy in copies[:3]:
        copy.wait()

    points[0] = jnp.where(lane8[:1] < 64, heat[0, 0], ratio[0, 0])

    def add_up(d, total):
        for u in range(8):
            starts[8 * d + u] = total
            total = total + tallies[lax.rem(me, 8), 8 * d + u]
        return total

    lax.fori_loop(0, octets, add_up, jnp.int32(0))

    for copy in copies[3:]:
        copy.wait()

    fields = (absorb, level, shift, slot_value, width_value)
    slot_value[pl.ds(0, tiles)] = slot[...].astype(jnp.float32)
    width_value[pl.ds(0, tiles)] = width[...].astype(jnp.float32)
    for field in fields:
        field[pl.ds(tiles, 16)] = jnp.zeros((16, 128), jnp.float32)
    position = 128 * sub8 + lane8

    def pack(target):
        begin = starts[target]
        count = tallies[lax.rem(me, 8), target]
        tile = lax.shift_right_logical(begin, 7)
        offset = jnp.full((8, 128), lax.bitwise_and(begin, 127))
        here, after = pl.ds(tile, 8), pl.ds(tile + 1, 8)
        windows = []
        for f, field in enumerate(fields):
            window = jnp.where(lane8 >= offset, field[here, :], field[after, :])
            for unit in (1, 4, 16):
                digit = lax.bitwise_and(offset, 3 * unit)
                turned = [pltpu.roll(window, 128 - k * unit, 1) for k in (1, 2, 3)]
                for k in (1, 2, 3):
                    window = jnp.where(digit == k * unit, turned[k - 1], window)
            turned = pltpu.roll(window, 64, 1)
            window = jnp.where(offset >= 64, turned, window)
            if f == FIELDS - 1:
                window = jnp.where(position >= count, float(NW), window)
            windows.append(window[:PARTS])
        return windows

    def pack_some(batch, _):
        first = batch * PACK
        packed = [pack(partner(first + u)) for u in range(PACK)]
        for u in range(PACK):
            for f in range(FIELDS):
                send[first + u, f] = packed[u][f]
        return 0

    lax.fori_loop(0, octets // PACK, pack_some, 0)

    pl.semaphore_wait(barrier, octets + 2 + 3 * (POINTS - 1) - jnp.where(stays, 1, 0))

    def share(src, dst, sem_send, sem_recv):
        for i in range(1, POINTS):
            pltpu.make_async_remote_copy(
                src_ref=src.at[0],
                dst_ref=dst.at[i],
                send_sem=sem_send,
                recv_sem=sem_recv,
                device_id=(me, lax.rem(tp + i, POINTS)),
                device_id_type=MESH,
            ).start()

    def lines_to(i, sem):
        return pltpu.make_async_remote_copy(
            src_ref=send.at[i],
            dst_ref=recv.at[i],
            send_sem=sem,
            recv_sem=recv_sem.at[i],
            device_id=(partner(i), tp),
            device_id_type=MESH,
        )

    pl.when(jnp.logical_not(stays))(lambda: lines_to(0, first_sem).start())
    pl.when(stays)(
        lambda: pltpu.make_async_copy(
            send.at[0], recv.at[0], recv_sem.at[0]
        ).start()
    )
    share(points, points, point_send_sem, point_sem)
    for i in range(1, octets):
        lines_to(i, send_sem).start()
    share(shapes, shapes, shape_send_sem, shape_sem)

    def all_points(src, dst, sem_send, sem_recv):
        return pltpu.make_async_remote_copy(
            src_ref=src.at[pl.ds(1, POINTS - 1)],
            dst_ref=dst.at[pl.ds(1, POINTS - 1)],
            send_sem=sem_send,
            recv_sem=sem_recv,
            device_id=(me, lax.rem(tp + 1, POINTS)),
            device_id_type=MESH,
        )

    all_points(points, points, point_send_sem, point_sem).wait_recv()
    both = jnp.concatenate([points[i] for i in range(POINTS)], axis=0)
    heats = jnp.where(lane8 < 64, both, pltpu.roll(both, 64, 1))
    ratios = jnp.where(lane8 < 64, pltpu.roll(both, 64, 1), both)
    inverse_gap = 1.0 / heats - 1.0 / baseline_heat_level

    block_ids = lax.broadcasted_iota(jnp.int32, (128, BLOCKS), 1).astype(jnp.float32)
    width_ids = lax.broadcasted_iota(jnp.int32, (NW, 128), 0).astype(jnp.float32)
    point_lane = lax.broadcasted_iota(jnp.int32, (REACH, JW), 1) // NW

    def spread(row):
        return jnp.broadcast_to(row, (NW, 128)).astype(jnp.bfloat16)

    def arrived(g):
        pltpu.make_async_remote_copy(
            src_ref=send.at[g],
            dst_ref=recv.at[g],
            send_sem=send_sem,
            recv_sem=recv_sem.at[g],
            device_id=(partner(1), tp),
            device_id_type=MESH,
        ).wait_recv()

    def one_hots(g, rows, cols):
        absorbs, levels, shifts, slots, widths = (recv[g, f] for f in range(FIELDS))
        blocks = jnp.floor(slots * 0.125)
        cells = slots - 8.0 * blocks
        halves = cells * 0.5
        even_cell = jnp.where(halves == jnp.floor(halves), 1.0, 0.0)
        here = [cells == float(j) for j in range(8)]
        touched = [
            here[0],
            *(jnp.logical_or(here[j], here[j - 1]) for j in range(1, 8)),
            here[7],
        ]
        touched = [jnp.where(t, 1.0, 0.0) for t in touched]
        tall = jnp.concatenate([blocks, blocks[: 8 - PARTS]], axis=0).T
        scaled = planck_hc_over_boltzmann * levels
        below = 1.0 - shifts

        def one_hot(part):
            line = slice(part, part + 1)
            at = part * 128
            hits = jnp.broadcast_to(tall[:, line], (128, BLOCKS)) == block_ids
            rows[pl.ds(at, 128), :] = jnp.where(hits, 1.0, 0.0).astype(jnp.bfloat16)
            strength = ratios * jnp.exp(absorbs[line] - scaled[line] * inverse_gap)
            low = strength * below[line]
            high = strength * shifts[line]
            is_even = jnp.broadcast_to(even_cell[line], (POINTS, 128)) > 0.5
            evens = jnp.where(is_even, low, high)
            odds = jnp.where(is_even, high, low)
            is_width = jnp.broadcast_to(widths[line], (NW, 128)) == width_ids
            is_width = jnp.where(is_width, 1.0, 0.0).astype(jnp.bfloat16)
            cell_hits = [spread(t[line]) for t in touched]
            for p in range(POINTS):
                even = spread(evens[p : p + 1]) * is_width
                odd = spread(odds[p : p + 1]) * is_width
                for j in range(J):
                    top = p * JW + j * NW if j < 8 else POINTS * JW + p * NW
                    value = (odd if j % 2 else even) * cell_hits[j]
                    cols[pl.ds(top, NW), pl.ds(at, 128)] = value

        return [functools.partial(one_hot, part) for part in range(PARTS)]

    def rows_of(piece):
        return pl.ds(piece * (COLS // PARTS), COLS // PARTS)

    def added(piece, rows, cols):
        some = rows_of(piece)
        return acc[some] + jnp.dot(
            cols[some], rows[...], preferred_element_type=jnp.float32
        )

    def add_product(piece, rows, cols):
        acc[rows_of(piece)] = added(piece, rows, cols)

    def make_taps(p):
        taps = jnp.concatenate([shapes[p], jnp.zeros((NW, 128), jnp.float32)], axis=1)
        moved = [taps] + [pltpu.roll(taps, j, 1) for j in range(1, 8)]
        tall = jnp.concatenate(moved, axis=0).T[:REACH]
        ninth = jnp.concatenate([jnp.zeros((8, JW), jnp.float32), tall[:-8]], axis=0)
        ninth = jnp.where(point_lane == p, pltpu.roll(ninth, NW * p, 1), 0.0)
        high, low = split(jnp.concatenate([tall, ninth], axis=1))
        taps_high[p] = high
        taps_low[p] = low

    def step(g, rows, cols, last_rows, last_cols):
        arrived(g)
        for part, make in enumerate(one_hots(g, rows, cols)):
            make()
            add_product(part, last_rows, last_cols)
        make_taps(g)

    make_taps(0)
    arrived(0)
    for make in one_hots(0, rows0, cols0):
        make()
    all_points(shapes, shapes, shape_send_sem, shape_sem).wait_recv()

    def deposit(h, _):
        step(2 * h + 1, rows1, cols1, rows0, cols0)
        step(2 * h + 2, rows0, cols0, rows1, cols1)
        return 0

    lax.fori_loop(0, octets // 2 - 1, deposit, 0)
    step(octets - 1, rows1, cols1, rows0, cols0)
    for piece in range(PARTS):
        high, low = split(added(piece, rows1, cols1))
        bins_high[rows_of(piece)] = high
        bins_low[rows_of(piece)] = low

    def fold(x):
        kept = jnp.where(lane8 < 16, x, 0.0)
        moved = pltpu.roll(kept, 0, 1, stride=16, stride_axis=0)
        return jnp.sum(moved, axis=0, keepdims=True)

    def unfold(row):
        wide = jnp.broadcast_to(row, (8, 128))
        moved = wide
        for i in range(1, 8):
            moved = jnp.where(sub8 == i, pltpu.roll(wide, 128 - 16 * i, 1), moved)
        return jnp.where(lane8 < 16, moved, 0.0)

    def convolve(p):
        own = pl.ds(pl.multiple_of(p * JW, JW), JW)
        ninth = pl.ds(POINTS * JW, JW)
        bin_high = jnp.concatenate([bins_high[own], bins_high[ninth]], axis=0)
        bin_low = jnp.concatenate([bins_low[own], bins_low[ninth]], axis=0)
        product = jnp.dot(taps_high[p], bin_high, preferred_element_type=jnp.float32)
        product += jnp.dot(taps_low[p], bin_high, preferred_element_type=jnp.float32)
        product += jnp.dot(taps_high[p], bin_low, preferred_element_type=jnp.float32)
        first, second = product[128:136, :128], product[128:136, 128:]
        outside = jnp.zeros((8, 128), jnp.float32)
        for m in range(33):
            by = m - 16
            if by == 0:
                continue
            front, back = product[8 * m : 8 * m + 8, :128], product[8 * m : 8 * m + 8, 128:]
            front = pltpu.roll(front, by % 128, 1)
            back = pltpu.roll(back, by % 128, 1)
            if by > 0:
                wraps = lane8 < by
                first += jnp.where(wraps, 0.0, front)
                second += jnp.where(wraps, front, back)
                outside += jnp.where(wraps, back, 0.0)
            else:
                wraps = lane8 >= 128 + by
                first += jnp.where(wraps, back, front)
                second += jnp.where(wraps, 0.0, back)
                outside += jnp.where(wraps, front, 0.0)
        main_send[p, 0] = first
        main_send[p, 1] = second
        left_send[p] = fold(pltpu.roll(outside, 16, 1))
        right_send[p] = fold(outside)

    def send_sums(p):
        point = lax.rem(tp + POINTS - p, POINTS)

        if p > 0:
            pltpu.make_async_remote_copy(
                src_ref=main_send.at[p],
                dst_ref=main_recv.at[p],
                send_sem=main_send_sem,
                recv_sem=main_sem,
                device_id=(me, point),
                device_id_type=MESH,
            ).start()

        for k, (src, dst, segment) in enumerate(
            ((left_send, left_recv, left), (right_send, right_recv, right))
        ):
            pltpu.make_async_remote_copy(
                src_ref=src.at[p],
                dst_ref=dst.at[p],
                send_sem=halo_send_sem.at[k],
                recv_sem=halo_sem.at[k],
                device_id=(segment, point),
                device_id_type=MESH,
            ).start()

    pairs = [(POINTS // 2 + h, POINTS // 2 - 1 - h) for h in range(POINTS // 2)]
    for h, pair in enumerate(pairs):
        for p in pair:
            convolve(p)
        if h > 0:
            for p in pairs[h - 1]:
                send_sums(p)
    for p in pairs[-1]:
        send_sums(p)

    sums = all_points(main_send, main_recv, main_send_sem, main_sem)
    halos = [
        pltpu.make_async_remote_copy(
            src_ref=src,
            dst_ref=dst,
            send_sem=halo_send_sem.at[k],
            recv_sem=halo_sem.at[k],
            device_id=(segment, tp),
            device_id_type=MESH,
        )
        for k, (src, dst, segment) in enumerate(
            ((left_send, left_recv, left), (right_send, right_recv, right))
        )
    ]
    for halo in halos:
        halo.wait_recv()
    from_right = unfold(jnp.sum(left_recv[...], axis=0))
    from_left = unfold(jnp.sum(right_recv[...], axis=0))
    from_right = jnp.where(me < n - 1, pltpu.roll(from_right, 112, 1), 0.0)
    from_left = jnp.where(me > 0, from_left, 0.0)
    first = main_send[0, 0] + from_left
    second = main_send[0, 1] + from_right
    sums.wait_recv()
    for p in range(1, POINTS):
        first += main_recv[p, 0]
        second += main_recv[p, 1]
    for k, part in enumerate((first, second)):
        tall = jnp.concatenate([part, jnp.zeros((120, 128), jnp.float32)], axis=0)
        ordered[pl.ds(128 * k, 128), :] = tall.T
    total = ordered[pl.ds(0, 16, stride=16), :]
    for k in range(1, 16):
        total += pltpu.roll(ordered[pl.ds(k, 16, stride=16), :], 8 * k, 1)
    out_ref[...] = total

    all_points(points, points, point_send_sem, point_sem).wait_send()
    all_points(shapes, shapes, shape_send_sem, shape_sem).wait_send()
    pl.when(jnp.logical_not(stays))(lambda: lines_to(0, first_sem).wait_send())
    pltpu.make_async_remote_copy(
        src_ref=send.at[pl.ds(1, octets - 1)],
        dst_ref=recv.at[pl.ds(1, octets - 1)],
        send_sem=send_sem,
        recv_sem=recv_sem.at[1],
        device_id=(partner(1), tp),
        device_id_type=MESH,
    ).wait_send()
    sums.wait_send()
    for halo in halos:
        halo.wait_send()


def body(
    natural_logged_absorbance,
    lower_state_level,
    subgrid_shift_ratio,
    local_grid_slot,
    broadening_class,
    tallies_per_shard,
    heat_levels,
    sum_over_states_ratio,
    shape_kernels,
):
    n = lax.axis_size("seg")
    lines = natural_logged_absorbance.shape[0]
    tiles = lines // 128
    hbm = pl.BlockSpec(memory_space=pl.ANY)
    vmem = pl.BlockSpec(memory_space=pltpu.VMEM)
    f32, bf16, i32 = jnp.float32, jnp.bfloat16, jnp.int32
    dma = pltpu.SemaphoreType.DMA
    result = pl.pallas_call(
        functools.partial(kernel, n),
        out_shape=jax.ShapeDtypeStruct((16, 128), f32),
        in_specs=[hbm] * 9,
        out_specs=vmem,
        scratch_shapes=[
            pltpu.SMEM((1, 1), f32),
            pltpu.SMEM((1, 1), f32),
            pltpu.SMEM((8, n), i32),
            pltpu.VMEM((tiles + 16, 128), f32),
            pltpu.VMEM((tiles + 16, 128), f32),
            pltpu.VMEM((tiles + 16, 128), f32),
            pltpu.VMEM((tiles, 128), i32),
            pltpu.VMEM((tiles, 128), i32),
            pltpu.VMEM((tiles + 16, 128), f32),
            pltpu.VMEM((tiles + 16, 128), f32),
            pltpu.SMEM((n,), i32),
            pltpu.VMEM((n // 8, FIELDS, PARTS, 128), f32),
            pltpu.VMEM((n // 8, FIELDS, PARTS, 128), f32),
            pltpu.VMEM((POINTS, 1, 128), f32),
            pltpu.VMEM((POINTS, NW, 256), f32),
            pltpu.VMEM((CAP, BLOCKS), bf16),
            pltpu.VMEM((COLS, CAP), bf16),
            pltpu.VMEM((CAP, BLOCKS), bf16),
            pltpu.VMEM((COLS, CAP), bf16),
            pltpu.VMEM((COLS, BLOCKS), f32),
            pltpu.VMEM((POINTS, REACH, 2 * JW), bf16),
            pltpu.VMEM((POINTS, REACH, 2 * JW), bf16),
            pltpu.VMEM((COLS, BLOCKS), bf16),
            pltpu.VMEM((COLS, BLOCKS), bf16),
            pltpu.VMEM((POINTS, 2, 8, 128), f32),
            pltpu.VMEM((POINTS, 1, 128), f32),
            pltpu.VMEM((POINTS, 1, 128), f32),
            pltpu.VMEM((POINTS, 2, 8, 128), f32),
            pltpu.VMEM((POINTS, 1, 128), f32),
            pltpu.VMEM((POINTS, 1, 128), f32),
            pltpu.VMEM((BLOCKS, 128), f32),
            dma((9,)),
            dma,
            dma,
            dma((n // 8,)),
            dma,
            dma,
            dma,
            dma,
            dma,
            dma,
            dma((2,)),
            dma((2,)),
        ],
        compiler_params=pltpu.CompilerParams(
            collective_id=0, has_side_effects=True, vmem_limit_bytes=56541184
        ),
        cost_estimate=pl.CostEstimate(
            flops=2 * n * CAP // 8 * BLOCKS * COLS,
            bytes_accessed=300000,
            transcendentals=n * CAP // 8 * POINTS,
        ),
    )(
        heat_levels.reshape(1, 1),
        sum_over_states_ratio.reshape(1, 1),
        tallies_per_shard,
        natural_logged_absorbance.reshape(tiles, 128),
        lower_state_level.reshape(tiles, 128),
        subgrid_shift_ratio.reshape(tiles, 128),
        local_grid_slot.reshape(tiles, 128),
        broadening_class.reshape(tiles, 128),
        shape_kernels[0],
    )
    return result.reshape(1, G)


def solution(mesh):
    in_specs = (
        P("seg"),
        P("seg"),
        P("seg"),
        P("seg"),
        P("seg"),
        P(),
        P("tp"),
        P("tp"),
        P("tp", None, None),
    )
    out_specs = P("tp", "seg")
    return jax.shard_map(body, mesh=mesh, in_specs=in_specs, out_specs=out_specs, check_vma=False)
```

```python
import functools

import jax
import jax.numpy as jnp
from jax import lax
from jax.experimental import pallas as pl
from jax.experimental.pallas import tpu as pltpu
from jax.sharding import PartitionSpec as P

MESH = pl.DeviceIdType.MESH

G = 2048
NW = 16
POINTS = 8
CAP = 768
FIELDS = 5
J = 9
JW = 8 * NW
COLS = POINTS * JW + JW
BLOCKS = G // 8
PARTS = CAP // 128
REACH = 272
PACK = 4

planck_hc_over_boltzmann = 1.4388
baseline_heat_level = 900.0


def split(x):
    high = x.astype(jnp.bfloat16)
    return high, (x - high.astype(jnp.float32)).astype(jnp.bfloat16)


def kernel(
    n,
    heat_ref,
    ratio_ref,
    tallies_ref,
    absorb_ref,
    level_ref,
    shift_ref,
    slot_ref,
    class_ref,
    shape_ref,
    out_ref,
    heat,
    ratio,
    tallies,
    absorb,
    level,
    shift,
    slot,
    width,
    slot_value,
    width_value,
    starts,
    send,
    recv,
    points,
    shapes,
    rows0,
    cols0,
    rows1,
    cols1,
    acc,
    taps_high,
    taps_low,
    bins_high,
    bins_low,
    main_send,
    left_send,
    right_send,
    main_recv,
    left_recv,
    right_recv,
    ordered,
    in_sem,
    send_sem,
    first_sem,
    recv_sem,
    point_send_sem,
    point_sem,
    shape_send_sem,
    shape_sem,
    main_send_sem,
    main_sem,
    halo_send_sem,
    halo_sem,
):
    me = lax.axis_index("seg")
    tp = lax.axis_index("tp")
    left = lax.rem(me + n - 1, n)
    right = lax.rem(me + 1, n)

    tiles = slot.shape[0]
    eight = pl.multiple_of((me // 8) * 8, 8)
    copies = [
        pltpu.make_async_copy(src, dst, in_sem.at[k])
        for k, (src, dst) in enumerate(
            (
                (heat_ref, heat),
                (ratio_ref, ratio),
                (tallies_ref.at[pl.ds(eight, 8)], tallies),
                (absorb_ref, absorb.at[pl.ds(0, tiles)]),
                (level_ref, level.at[pl.ds(0, tiles)]),
                (shift_ref, shift.at[pl.ds(0, tiles)]),
                (slot_ref, slot),
                (class_ref, width),
                (shape_ref, shapes.at[0]),
            )
        )
    ]
    for copy in copies:
        copy.start()

    eighth = lax.rem(tp + n - lax.rem(me, 8), 8)
    stays = eighth == lax.rem(me, 8)
    octets = n // 8

    def partner(i):
        return eighth + 8 * lax.rem(me // 8 + i, octets)

    barrier = pltpu.get_barrier_semaphore()

    def greet(segment, point):
        pl.semaphore_signal(
            barrier, inc=1, device_id=(segment, point), device_id_type=MESH
        )

    for i in range(octets):
        if i == 0:
            pl.when(jnp.logical_not(stays))(lambda: greet(partner(0), tp))
        else:
            greet(partner(i), tp)
    for i in range(1, POINTS):
        for segment in (me, left, right):
            greet(segment, lax.rem(tp + i, POINTS))
    greet(left, tp)
    greet(right, tp)

    lane8 = lax.broadcasted_iota(jnp.int32, (8, 128), 1)
    sub8 = lax.broadcasted_iota(jnp.int32, (8, 128), 0)
    acc[...] = jnp.zeros_like(acc)

    for copy in copies[:3]:
        copy.wait()

    points[0] = jnp.where(lane8[:1] < 64, heat[0, 0], ratio[0, 0])

    def add_up(d, total):
        for u in range(8):
            starts[8 * d + u] = total
            total = total + tallies[lax.rem(me, 8), 8 * d + u]
        return total

    lax.fori_loop(0, octets, add_up, jnp.int32(0))

    for copy in copies[3:]:
        copy.wait()

    fields = (absorb, level, shift, slot_value, width_value)
    slot_value[pl.ds(0, tiles)] = slot[...].astype(jnp.float32)
    width_value[pl.ds(0, tiles)] = width[...].astype(jnp.float32)
    for field in fields:
        field[pl.ds(tiles, 16)] = jnp.zeros((16, 128), jnp.float32)
    position = 128 * sub8 + lane8

    def pack(target):
        begin = starts[target]
        count = tallies[lax.rem(me, 8), target]
        tile = lax.shift_right_logical(begin, 7)
        offset = jnp.full((8, 128), lax.bitwise_and(begin, 127))
        here, after = pl.ds(tile, 8), pl.ds(tile + 1, 8)
        windows = []
        for f, field in enumerate(fields):
            window = jnp.where(lane8 >= offset, field[here, :], field[after, :])
            for unit in (1, 4, 16):
                digit = lax.bitwise_and(offset, 3 * unit)
                turned = [pltpu.roll(window, 128 - k * unit, 1) for k in (1, 2, 3)]
                for k in (1, 2, 3):
                    window = jnp.where(digit == k * unit, turned[k - 1], window)
            turned = pltpu.roll(window, 64, 1)
            window = jnp.where(offset >= 64, turned, window)
            if f == FIELDS - 1:
                window = jnp.where(position >= count, float(NW), window)
            windows.append(window[:PARTS])
        return windows

    def pack_some(batch, _):
        first = batch * PACK
        packed = [pack(partner(first + u)) for u in range(PACK)]
        for u in range(PACK):
            for f in range(FIELDS):
                send[first + u, f] = packed[u][f]
        return 0

    lax.fori_loop(0, octets // PACK, pack_some, 0)

    pl.semaphore_wait(barrier, octets + 2 + 3 * (POINTS - 1) - jnp.where(stays, 1, 0))

    def share(src, dst, sem_send, sem_recv):
        for i in range(1, POINTS):
            pltpu.make_async_remote_copy(
                src_ref=src.at[0],
                dst_ref=dst.at[i],
                send_sem=sem_send,
                recv_sem=sem_recv,
                device_id=(me, lax.rem(tp + i, POINTS)),
                device_id_type=MESH,
            ).start()

    def lines_to(i, sem):
        return pltpu.make_async_remote_copy(
            src_ref=send.at[i],
            dst_ref=recv.at[i],
            send_sem=sem,
            recv_sem=recv_sem.at[i],
            device_id=(partner(i), tp),
            device_id_type=MESH,
        )

    pl.when(jnp.logical_not(stays))(lambda: lines_to(0, first_sem).start())
    pl.when(stays)(
        lambda: pltpu.make_async_copy(
            send.at[0], recv.at[0], recv_sem.at[0]
        ).start()
    )
    share(points, points, point_send_sem, point_sem)
    for i in range(1, octets):
        lines_to(i, send_sem).start()
    share(shapes, shapes, shape_send_sem, shape_sem)

    def all_points(src, dst, sem_send, sem_recv):
        return pltpu.make_async_remote_copy(
            src_ref=src.at[pl.ds(1, POINTS - 1)],
            dst_ref=dst.at[pl.ds(1, POINTS - 1)],
            send_sem=sem_send,
            recv_sem=sem_recv,
            device_id=(me, lax.rem(tp + 1, POINTS)),
            device_id_type=MESH,
        )

    all_points(points, points, point_send_sem, point_sem).wait_recv()
    both = jnp.concatenate([points[i] for i in range(POINTS)], axis=0)
    heats = jnp.where(lane8 < 64, both, pltpu.roll(both, 64, 1))
    ratios = jnp.where(lane8 < 64, pltpu.roll(both, 64, 1), both)
    inverse_gap = 1.0 / heats - 1.0 / baseline_heat_level

    block_ids = lax.broadcasted_iota(jnp.int32, (128, BLOCKS), 1).astype(jnp.float32)
    width_ids = lax.broadcasted_iota(jnp.int32, (NW, 128), 0).astype(jnp.float32)
    point_lane = lax.broadcasted_iota(jnp.int32, (REACH, JW), 1) // NW

    def spread(row):
        return jnp.broadcast_to(row, (NW, 128)).astype(jnp.bfloat16)

    def arrived(g):
        pltpu.make_async_remote_copy(
            src_ref=send.at[g],
            dst_ref=recv.at[g],
            send_sem=send_sem,
            recv_sem=recv_sem.at[g],
            device_id=(partner(1), tp),
            device_id_type=MESH,
        ).wait_recv()

    def one_hots(g, rows, cols):
        absorbs, levels, shifts, slots, widths = (recv[g, f] for f in range(FIELDS))
        blocks = jnp.floor(slots * 0.125)
        cells = slots - 8.0 * blocks
        halves = cells * 0.5
        even_cell = jnp.where(halves == jnp.floor(halves), 1.0, 0.0)
        here = [cells == float(j) for j in range(8)]
        touched = [
            here[0],
            *(jnp.logical_or(here[j], here[j - 1]) for j in range(1, 8)),
            here[7],
        ]
        touched = [jnp.where(t, 1.0, 0.0) for t in touched]
        tall = jnp.concatenate([blocks, blocks[: 8 - PARTS]], axis=0).T
        scaled = planck_hc_over_boltzmann * levels
        below = 1.0 - shifts

        def one_hot(part):
            line = slice(part, part + 1)
            at = part * 128
            hits = jnp.broadcast_to(tall[:, line], (128, BLOCKS)) == block_ids
            rows[pl.ds(at, 128), :] = jnp.where(hits, 1.0, 0.0).astype(jnp.bfloat16)
            strength = ratios * jnp.exp(absorbs[line] - scaled[line] * inverse_gap)
            low = strength * below[line]
            high = strength * shifts[line]
            is_even = jnp.broadcast_to(even_cell[line], (POINTS, 128)) > 0.5
            evens = jnp.where(is_even, low, high)
            odds = jnp.where(is_even, high, low)
            is_width = jnp.broadcast_to(widths[line], (NW, 128)) == width_ids
            is_width = jnp.where(is_width, 1.0, 0.0).astype(jnp.bfloat16)
            cell_hits = [spread(t[line]) for t in touched]
            for p in range(POINTS):
                even = spread(evens[p : p + 1]) * is_width
                odd = spread(odds[p : p + 1]) * is_width
                for j in range(J):
                    top = p * JW + j * NW if j < 8 else POINTS * JW + p * NW
                    value = (odd if j % 2 else even) * cell_hits[j]
                    cols[pl.ds(top, NW), pl.ds(at, 128)] = value

        return [functools.partial(one_hot, part) for part in range(PARTS)]

    def add_product(piece, rows, cols):
        some = pl.ds(piece * (COLS // PARTS), COLS // PARTS)
        acc[some] += jnp.dot(
            cols[some], rows[...], preferred_element_type=jnp.float32
        )

    def make_taps(p):
        taps = jnp.concatenate([shapes[p], jnp.zeros((NW, 128), jnp.float32)], axis=1)
        moved = [taps] + [pltpu.roll(taps, j, 1) for j in range(1, 8)]
        tall = jnp.concatenate(moved, axis=0).T[:REACH]
        ninth = jnp.concatenate([jnp.zeros((8, JW), jnp.float32), tall[:-8]], axis=0)
        ninth = jnp.where(point_lane == p, pltpu.roll(ninth, NW * p, 1), 0.0)
        high, low = split(jnp.concatenate([tall, ninth], axis=1))
        taps_high[p] = high
        taps_low[p] = low

    def step(g, rows, cols, last_rows, last_cols):
        for part, make in enumerate(one_hots(g, rows, cols)):
            add_product(part, last_rows, last_cols)
            make()
        make_taps(g)

    make_taps(0)
    arrived(0)
    for make in one_hots(0, rows0, cols0):
        make()
    all_points(shapes, shapes, shape_send_sem, shape_sem).wait_recv()

    def deposit(h, _):
        arrived(2 * h + 1)
        arrived(2 * h + 2)
        step(2 * h + 1, rows1, cols1, rows0, cols0)
        step(2 * h + 2, rows0, cols0, rows1, cols1)
        return 0

    lax.fori_loop(0, octets // 2 - 1, deposit, 0)
    arrived(octets - 1)
    step(octets - 1, rows1, cols1, rows0, cols0)
    for piece in range(PARTS):
        add_product(piece, rows1, cols1)
    high, low = split(acc[...])
    bins_high[...] = high
    bins_low[...] = low

    def fold(x):
        kept = jnp.where(lane8 < 16, x, 0.0)
        moved = pltpu.roll(kept, 0, 1, stride=16, stride_axis=0)
        return jnp.sum(moved, axis=0, keepdims=True)

    def unfold(row):
        wide = jnp.broadcast_to(row, (8, 128))
        moved = wide
        for i in range(1, 8):
            moved = jnp.where(sub8 == i, pltpu.roll(wide, 128 - 16 * i, 1), moved)
        return jnp.where(lane8 < 16, moved, 0.0)

    def convolve(p):
        own = pl.ds(pl.multiple_of(p * JW, JW), JW)
        ninth = pl.ds(POINTS * JW, JW)
        bin_high = jnp.concatenate([bins_high[own], bins_high[ninth]], axis=0)
        bin_low = jnp.concatenate([bins_low[own], bins_low[ninth]], axis=0)
        product = jnp.dot(taps_high[p], bin_high, preferred_element_type=jnp.float32)
        product += jnp.dot(taps_low[p], bin_high, preferred_element_type=jnp.float32)
        product += jnp.dot(taps_high[p], bin_low, preferred_element_type=jnp.float32)
        first, second = product[128:136, :128], product[128:136, 128:]
        outside = jnp.zeros((8, 128), jnp.float32)
        for m in range(33):
            by = m - 16
            if by == 0:
                continue
            front, back = product[8 * m : 8 * m + 8, :128], product[8 * m : 8 * m + 8, 128:]
            front = pltpu.roll(front, by % 128, 1)
            back = pltpu.roll(back, by % 128, 1)
            if by > 0:
                wraps = lane8 < by
                first += jnp.where(wraps, 0.0, front)
                second += jnp.where(wraps, front, back)
                outside += jnp.where(wraps, back, 0.0)
            else:
                wraps = lane8 >= 128 + by
                first += jnp.where(wraps, back, front)
                second += jnp.where(wraps, 0.0, back)
                outside += jnp.where(wraps, front, 0.0)
        main_send[p, 0] = first
        main_send[p, 1] = second
        left_send[p] = fold(pltpu.roll(outside, 16, 1))
        right_send[p] = fold(outside)

    def send_sums(p):
        point = lax.rem(tp + POINTS - p, POINTS)

        @pl.when(p > 0)
        def _():
            pltpu.make_async_remote_copy(
                src_ref=main_send.at[p],
                dst_ref=main_recv.at[p],
                send_sem=main_send_sem,
                recv_sem=main_sem,
                device_id=(me, point),
                device_id_type=MESH,
            ).start()

        for k, (src, dst, segment) in enumerate(
            ((left_send, left_recv, left), (right_send, right_recv, right))
        ):
            pltpu.make_async_remote_copy(
                src_ref=src.at[p],
                dst_ref=dst.at[p],
                send_sem=halo_send_sem.at[k],
                recv_sem=halo_sem.at[k],
                device_id=(segment, point),
                device_id_type=MESH,
            ).start()

    def convolve_two(h, _):
        pair = (POINTS // 2 + h, POINTS // 2 - 1 - h)
        for p in pair:
            convolve(p)
        for p in pair:
            send_sums(p)
        return 0

    lax.fori_loop(0, POINTS // 2, convolve_two, 0)

    sums = all_points(main_send, main_recv, main_send_sem, main_sem)
    halos = [
        pltpu.make_async_remote_copy(
            src_ref=src,
            dst_ref=dst,
            send_sem=halo_send_sem.at[k],
            recv_sem=halo_sem.at[k],
            device_id=(segment, tp),
            device_id_type=MESH,
        )
        for k, (src, dst, segment) in enumerate(
            ((left_send, left_recv, left), (right_send, right_recv, right))
        )
    ]
    for halo in halos:
        halo.wait_recv()
    from_right = unfold(jnp.sum(left_recv[...], axis=0))
    from_left = unfold(jnp.sum(right_recv[...], axis=0))
    from_right = jnp.where(me < n - 1, pltpu.roll(from_right, 112, 1), 0.0)
    from_left = jnp.where(me > 0, from_left, 0.0)
    first = main_send[0, 0] + from_left
    second = main_send[0, 1] + from_right
    sums.wait_recv()
    for p in range(1, POINTS):
        first += main_recv[p, 0]
        second += main_recv[p, 1]
    for k, part in enumerate((first, second)):
        tall = jnp.concatenate([part, jnp.zeros((120, 128), jnp.float32)], axis=0)
        ordered[pl.ds(128 * k, 128), :] = tall.T
    total = ordered[pl.ds(0, 16, stride=16), :]
    for k in range(1, 16):
        total += pltpu.roll(ordered[pl.ds(k, 16, stride=16), :], 8 * k, 1)
    out_ref[...] = total

    all_points(points, points, point_send_sem, point_sem).wait_send()
    all_points(shapes, shapes, shape_send_sem, shape_sem).wait_send()
    pl.when(jnp.logical_not(stays))(lambda: lines_to(0, first_sem).wait_send())
    pltpu.make_async_remote_copy(
        src_ref=send.at[pl.ds(1, octets - 1)],
        dst_ref=recv.at[pl.ds(1, octets - 1)],
        send_sem=send_sem,
        recv_sem=recv_sem.at[1],
        device_id=(partner(1), tp),
        device_id_type=MESH,
    ).wait_send()
    sums.wait_send()
    for halo in halos:
        halo.wait_send()


def body(
    natural_logged_absorbance,
    lower_state_level,
    subgrid_shift_ratio,
    local_grid_slot,
    broadening_class,
    tallies_per_shard,
    heat_levels,
    sum_over_states_ratio,
    shape_kernels,
):
    n = lax.axis_size("seg")
    lines = natural_logged_absorbance.shape[0]
    tiles = lines // 128
    hbm = pl.BlockSpec(memory_space=pl.ANY)
    vmem = pl.BlockSpec(memory_space=pltpu.VMEM)
    f32, bf16, i32 = jnp.float32, jnp.bfloat16, jnp.int32
    dma = pltpu.SemaphoreType.DMA
    result = pl.pallas_call(
        functools.partial(kernel, n),
        out_shape=jax.ShapeDtypeStruct((16, 128), f32),
        in_specs=[hbm] * 9,
        out_specs=vmem,
        scratch_shapes=[
            pltpu.SMEM((1, 1), f32),
            pltpu.SMEM((1, 1), f32),
            pltpu.SMEM((8, n), i32),
            pltpu.VMEM((tiles + 16, 128), f32),
            pltpu.VMEM((tiles + 16, 128), f32),
            pltpu.VMEM((tiles + 16, 128), f32),
            pltpu.VMEM((tiles, 128), i32),
            pltpu.VMEM((tiles, 128), i32),
            pltpu.VMEM((tiles + 16, 128), f32),
            pltpu.VMEM((tiles + 16, 128), f32),
            pltpu.SMEM((n,), i32),
            pltpu.VMEM((n // 8, FIELDS, PARTS, 128), f32),
            pltpu.VMEM((n // 8, FIELDS, PARTS, 128), f32),
            pltpu.VMEM((POINTS, 1, 128), f32),
            pltpu.VMEM((POINTS, NW, 256), f32),
            pltpu.VMEM((CAP, BLOCKS), bf16),
            pltpu.VMEM((COLS, CAP), bf16),
            pltpu.VMEM((CAP, BLOCKS), bf16),
            pltpu.VMEM((COLS, CAP), bf16),
            pltpu.VMEM((COLS, BLOCKS), f32),
            pltpu.VMEM((POINTS, REACH, 2 * JW), bf16),
            pltpu.VMEM((POINTS, REACH, 2 * JW), bf16),
            pltpu.VMEM((COLS, BLOCKS), bf16),
            pltpu.VMEM((COLS, BLOCKS), bf16),
            pltpu.VMEM((POINTS, 2, 8, 128), f32),
            pltpu.VMEM((POINTS, 1, 128), f32),
            pltpu.VMEM((POINTS, 1, 128), f32),
            pltpu.VMEM((POINTS, 2, 8, 128), f32),
            pltpu.VMEM((POINTS, 1, 128), f32),
            pltpu.VMEM((POINTS, 1, 128), f32),
            pltpu.VMEM((BLOCKS, 128), f32),
            dma((9,)),
            dma,
            dma,
            dma((n // 8,)),
            dma,
            dma,
            dma,
            dma,
            dma,
            dma,
            dma((2,)),
            dma((2,)),
        ],
        compiler_params=pltpu.CompilerParams(
            collective_id=0, has_side_effects=True, vmem_limit_bytes=56541184
        ),
        cost_estimate=pl.CostEstimate(
            flops=2 * n * CAP // 8 * BLOCKS * COLS,
            bytes_accessed=300000,
            transcendentals=n * CAP // 8 * POINTS,
        ),
    )(
        heat_levels.reshape(1, 1),
        sum_over_states_ratio.reshape(1, 1),
        tallies_per_shard,
        natural_logged_absorbance.reshape(tiles, 128),
        lower_state_level.reshape(tiles, 128),
        subgrid_shift_ratio.reshape(tiles, 128),
        local_grid_slot.reshape(tiles, 128),
        broadening_class.reshape(tiles, 128),
        shape_kernels[0],
    )
    return result.reshape(1, G)


def solution(mesh):
    in_specs = (
        P("seg"),
        P("seg"),
        P("seg"),
        P("seg"),
        P("seg"),
        P(),
        P("tp"),
        P("tp"),
        P("tp", None, None),
    )
    out_specs = P("tp", "seg")
    return jax.shard_map(body, mesh=mesh, in_specs=in_specs, out_specs=out_specs, check_vma=False)
```

```python
import functools

import jax
import jax.numpy as jnp
from jax import lax
from jax.experimental import pallas as pl
from jax.experimental.pallas import tpu as pltpu
from jax.sharding import PartitionSpec as P

MESH = pl.DeviceIdType.MESH

G = 2048
NW = 16
POINTS = 8
CAP = 768
FIELDS = 5
J = 9
JW = 8 * NW
COLS = POINTS * JW + JW
BLOCKS = G // 8
PARTS = CAP // 128
REACH = 272
PACK = 4

planck_hc_over_boltzmann = 1.4388
baseline_heat_level = 900.0


def split(x):
    high = x.astype(jnp.bfloat16)
    return high, (x - high.astype(jnp.float32)).astype(jnp.bfloat16)


def kernel(
    n,
    heat_ref,
    ratio_ref,
    tallies_ref,
    absorb_ref,
    level_ref,
    shift_ref,
    slot_ref,
    class_ref,
    shape_ref,
    out_ref,
    heat,
    ratio,
    tallies,
    absorb,
    level,
    shift,
    slot,
    width,
    slot_value,
    width_value,
    starts,
    send,
    recv,
    points,
    shapes,
    rows0,
    cols0,
    rows1,
    cols1,
    acc,
    taps_high,
    taps_low,
    bins_high,
    bins_low,
    main_send,
    left_send,
    right_send,
    main_recv,
    left_recv,
    right_recv,
    ordered,
    in_sem,
    send_sem,
    first_sem,
    recv_sem,
    point_send_sem,
    point_sem,
    shape_send_sem,
    shape_sem,
    main_send_sem,
    main_sem,
    halo_send_sem,
    halo_sem,
):
    me = lax.axis_index("seg")
    tp = lax.axis_index("tp")
    left = lax.rem(me + n - 1, n)
    right = lax.rem(me + 1, n)

    tiles = slot.shape[0]
    eight = pl.multiple_of((me // 8) * 8, 8)
    copies = [
        pltpu.make_async_copy(src, dst, in_sem.at[k])
        for k, (src, dst) in enumerate(
            (
                (heat_ref, heat),
                (ratio_ref, ratio),
                (tallies_ref.at[pl.ds(eight, 8)], tallies),
                (absorb_ref, absorb.at[pl.ds(0, tiles)]),
                (level_ref, level.at[pl.ds(0, tiles)]),
                (shift_ref, shift.at[pl.ds(0, tiles)]),
                (slot_ref, slot),
                (class_ref, width),
                (shape_ref, shapes.at[0]),
            )
        )
    ]
    for copy in copies:
        copy.start()

    eighth = lax.rem(tp + n - lax.rem(me, 8), 8)
    stays = eighth == lax.rem(me, 8)
    octets = n // 8

    def partner(i):
        return eighth + 8 * lax.rem(me // 8 + i, octets)

    barrier = pltpu.get_barrier_semaphore()

    def greet(segment, point):
        pl.semaphore_signal(
            barrier, inc=1, device_id=(segment, point), device_id_type=MESH
        )

    for i in range(octets):
        if i == 0:
            pl.when(jnp.logical_not(stays))(lambda: greet(partner(0), tp))
        else:
            greet(partner(i), tp)
    for i in range(1, POINTS):
        for segment in (me, left, right):
            greet(segment, lax.rem(tp + i, POINTS))
    greet(left, tp)
    greet(right, tp)

    lane8 = lax.broadcasted_iota(jnp.int32, (8, 128), 1)
    sub8 = lax.broadcasted_iota(jnp.int32, (8, 128), 0)
    acc[...] = jnp.zeros_like(acc)

    for copy in copies[:3]:
        copy.wait()

    points[0] = jnp.where(lane8[:1] < 64, heat[0, 0], ratio[0, 0])

    def add_up(d, total):
        for u in range(8):
            starts[8 * d + u] = total
            total = total + tallies[lax.rem(me, 8), 8 * d + u]
        return total

    lax.fori_loop(0, octets, add_up, jnp.int32(0))

    for copy in copies[3:]:
        copy.wait()

    fields = (absorb, level, shift, slot_value, width_value)
    slot_value[pl.ds(0, tiles)] = slot[...].astype(jnp.float32)
    width_value[pl.ds(0, tiles)] = width[...].astype(jnp.float32)
    for field in fields:
        field[pl.ds(tiles, 16)] = jnp.zeros((16, 128), jnp.float32)
    position = 128 * sub8 + lane8

    def pack(target):
        begin = starts[target]
        count = tallies[lax.rem(me, 8), target]
        tile = lax.shift_right_logical(begin, 7)
        offset = jnp.full((8, 128), lax.bitwise_and(begin, 127))
        here, after = pl.ds(tile, 8), pl.ds(tile + 1, 8)
        windows = []
        for f, field in enumerate(fields):
            window = jnp.where(lane8 >= offset, field[here, :], field[after, :])
            for unit in (1, 4, 16):
                digit = lax.bitwise_and(offset, 3 * unit)
                turned = [pltpu.roll(window, 128 - k * unit, 1) for k in (1, 2, 3)]
                for k in (1, 2, 3):
                    window = jnp.where(digit == k * unit, turned[k - 1], window)
            turned = pltpu.roll(window, 64, 1)
            window = jnp.where(offset >= 64, turned, window)
            if f == FIELDS - 1:
                window = jnp.where(position >= count, float(NW), window)
            windows.append(window[:PARTS])
        return windows

    def pack_some(batch, _):
        first = batch * PACK
        packed = [pack(partner(first + u)) for u in range(PACK)]
        for u in range(PACK):
            for f in range(FIELDS):
                send[first + u, f] = packed[u][f]
        return 0

    lax.fori_loop(0, octets // PACK, pack_some, 0)

    pl.semaphore_wait(barrier, octets + 2 + 3 * (POINTS - 1) - jnp.where(stays, 1, 0))

    def share(src, dst, sem_send, sem_recv):
        for i in range(1, POINTS):
            pltpu.make_async_remote_copy(
                src_ref=src.at[0],
                dst_ref=dst.at[i],
                send_sem=sem_send,
                recv_sem=sem_recv,
                device_id=(me, lax.rem(tp + i, POINTS)),
                device_id_type=MESH,
            ).start()

    def lines_to(i, sem):
        return pltpu.make_async_remote_copy(
            src_ref=send.at[i],
            dst_ref=recv.at[i],
            send_sem=sem,
            recv_sem=recv_sem.at[i],
            device_id=(partner(i), tp),
            device_id_type=MESH,
        )

    pl.when(jnp.logical_not(stays))(lambda: lines_to(0, first_sem).start())
    pl.when(stays)(
        lambda: pltpu.make_async_copy(
            send.at[0], recv.at[0], recv_sem.at[0]
        ).start()
    )
    share(points, points, point_send_sem, point_sem)
    for i in range(1, octets):
        lines_to(i, send_sem).start()
    share(shapes, shapes, shape_send_sem, shape_sem)

    def all_points(src, dst, sem_send, sem_recv):
        return pltpu.make_async_remote_copy(
            src_ref=src.at[pl.ds(1, POINTS - 1)],
            dst_ref=dst.at[pl.ds(1, POINTS - 1)],
            send_sem=sem_send,
            recv_sem=sem_recv,
            device_id=(me, lax.rem(tp + 1, POINTS)),
            device_id_type=MESH,
        )

    all_points(points, points, point_send_sem, point_sem).wait_recv()
    both = jnp.concatenate([points[i] for i in range(POINTS)], axis=0)
    heats = jnp.where(lane8 < 64, both, pltpu.roll(both, 64, 1))
    ratios = jnp.where(lane8 < 64, pltpu.roll(both, 64, 1), both)
    inverse_gap = 1.0 / heats - 1.0 / baseline_heat_level

    block_ids = lax.broadcasted_iota(jnp.int32, (128, BLOCKS), 1).astype(jnp.float32)
    width_ids = lax.broadcasted_iota(jnp.int32, (NW, 128), 0).astype(jnp.float32)
    point_lane = lax.broadcasted_iota(jnp.int32, (REACH, JW), 1) // NW

    def spread(row):
        return jnp.broadcast_to(row, (NW, 128)).astype(jnp.bfloat16)

    def arrived(g):
        pltpu.make_async_remote_copy(
            src_ref=send.at[g],
            dst_ref=recv.at[g],
            send_sem=send_sem,
            recv_sem=recv_sem.at[g],
            device_id=(partner(1), tp),
            device_id_type=MESH,
        ).wait_recv()

    def one_hots(g, rows, cols):
        absorbs, levels, shifts, slots, widths = (recv[g, f] for f in range(FIELDS))
        blocks = jnp.floor(slots * 0.125)
        cells = slots - 8.0 * blocks
        halves = cells * 0.5
        even_cell = jnp.where(halves == jnp.floor(halves), 1.0, 0.0)
        here = [cells == float(j) for j in range(8)]
        touched = [
            here[0],
            *(jnp.logical_or(here[j], here[j - 1]) for j in range(1, 8)),
            here[7],
        ]
        touched = [jnp.where(t, 1.0, 0.0) for t in touched]
        tall = jnp.concatenate([blocks, blocks[: 8 - PARTS]], axis=0).T
        scaled = planck_hc_over_boltzmann * levels
        below = 1.0 - shifts

        def one_hot(part):
            line = slice(part, part + 1)
            at = part * 128
            hits = jnp.broadcast_to(tall[:, line], (128, BLOCKS)) == block_ids
            rows[pl.ds(at, 128), :] = jnp.where(hits, 1.0, 0.0).astype(jnp.bfloat16)
            strength = ratios * jnp.exp(absorbs[line] - scaled[line] * inverse_gap)
            low = strength * below[line]
            high = strength * shifts[line]
            is_even = jnp.broadcast_to(even_cell[line], (POINTS, 128)) > 0.5
            evens = jnp.where(is_even, low, high)
            odds = jnp.where(is_even, high, low)
            is_width = jnp.broadcast_to(widths[line], (NW, 128)) == width_ids
            is_width = jnp.where(is_width, 1.0, 0.0).astype(jnp.bfloat16)
            cell_hits = [spread(t[line]) for t in touched]
            for p in range(POINTS):
                even = spread(evens[p : p + 1]) * is_width
                odd = spread(odds[p : p + 1]) * is_width
                for j in range(J):
                    top = p * JW + j * NW if j < 8 else POINTS * JW + p * NW
                    value = (odd if j % 2 else even) * cell_hits[j]
                    cols[pl.ds(top, NW), pl.ds(at, 128)] = value

        return [functools.partial(one_hot, part) for part in range(PARTS)]

    def add_product(piece, rows, cols):
        some = pl.ds(piece * (COLS // PARTS), COLS // PARTS)
        acc[some] += jnp.dot(
            cols[some], rows[...], preferred_element_type=jnp.float32
        )

    def make_taps(p):
        taps = jnp.concatenate([shapes[p], jnp.zeros((NW, 128), jnp.float32)], axis=1)
        moved = [taps] + [pltpu.roll(taps, j, 1) for j in range(1, 8)]
        tall = jnp.concatenate(moved, axis=0).T[:REACH]
        ninth = jnp.concatenate([jnp.zeros((8, JW), jnp.float32), tall[:-8]], axis=0)
        ninth = jnp.where(point_lane == p, pltpu.roll(ninth, NW * p, 1), 0.0)
        high, low = split(jnp.concatenate([tall, ninth], axis=1))
        taps_high[p] = high
        taps_low[p] = low

    def step(g, rows, cols, last_rows, last_cols):
        for part, make in enumerate(one_hots(g, rows, cols)):
            add_product(part, last_rows, last_cols)
            make()

    make_taps(0)
    arrived(0)
    for make in one_hots(0, rows0, cols0):
        make()
    arrived(1)
    arrived(2)
    step(1, rows1, cols1, rows0, cols0)
    step(2, rows0, cols0, rows1, cols1)
    all_points(shapes, shapes, shape_send_sem, shape_sem).wait_recv()

    def deposit(h, _):
        arrived(2 * h + 1)
        arrived(2 * h + 2)
        step(2 * h + 1, rows1, cols1, rows0, cols0)
        make_taps(3 * h - 2)
        step(2 * h + 2, rows0, cols0, rows1, cols1)
        make_taps(3 * h - 1)
        make_taps(3 * h)
        return 0

    lax.fori_loop(1, octets // 2 - 1, deposit, 0)
    arrived(octets - 1)
    step(octets - 1, rows1, cols1, rows0, cols0)
    make_taps(octets - 1)
    for piece in range(PARTS):
        add_product(piece, rows1, cols1)
    high, low = split(acc[...])
    bins_high[...] = high
    bins_low[...] = low

    def fold(x):
        kept = jnp.where(lane8 < 16, x, 0.0)
        moved = pltpu.roll(kept, 0, 1, stride=16, stride_axis=0)
        return jnp.sum(moved, axis=0, keepdims=True)

    def unfold(row):
        wide = jnp.broadcast_to(row, (8, 128))
        moved = wide
        for i in range(1, 8):
            moved = jnp.where(sub8 == i, pltpu.roll(wide, 128 - 16 * i, 1), moved)
        return jnp.where(lane8 < 16, moved, 0.0)

    def convolve(p):
        own = pl.ds(pl.multiple_of(p * JW, JW), JW)
        ninth = pl.ds(POINTS * JW, JW)
        bin_high = jnp.concatenate([bins_high[own], bins_high[ninth]], axis=0)
        bin_low = jnp.concatenate([bins_low[own], bins_low[ninth]], axis=0)
        product = jnp.dot(taps_high[p], bin_high, preferred_element_type=jnp.float32)
        product += jnp.dot(taps_low[p], bin_high, preferred_element_type=jnp.float32)
        product += jnp.dot(taps_high[p], bin_low, preferred_element_type=jnp.float32)
        first, second = product[128:136, :128], product[128:136, 128:]
        outside = jnp.zeros((8, 128), jnp.float32)
        for m in range(33):
            by = m - 16
            if by == 0:
                continue
            front, back = product[8 * m : 8 * m + 8, :128], product[8 * m : 8 * m + 8, 128:]
            front = pltpu.roll(front, by % 128, 1)
            back = pltpu.roll(back, by % 128, 1)
            if by > 0:
                wraps = lane8 < by
                first += jnp.where(wraps, 0.0, front)
                second += jnp.where(wraps, front, back)
                outside += jnp.where(wraps, back, 0.0)
            else:
                wraps = lane8 >= 128 + by
                first += jnp.where(wraps, back, front)
                second += jnp.where(wraps, 0.0, back)
                outside += jnp.where(wraps, front, 0.0)
        main_send[p, 0] = first
        main_send[p, 1] = second
        left_send[p] = fold(pltpu.roll(outside, 16, 1))
        right_send[p] = fold(outside)

    def send_sums(p):
        point = lax.rem(tp + POINTS - p, POINTS)

        @pl.when(p > 0)
        def _():
            pltpu.make_async_remote_copy(
                src_ref=main_send.at[p],
                dst_ref=main_recv.at[p],
                send_sem=main_send_sem,
                recv_sem=main_sem,
                device_id=(me, point),
                device_id_type=MESH,
            ).start()

        for k, (src, dst, segment) in enumerate(
            ((left_send, left_recv, left), (right_send, right_recv, right))
        ):
            pltpu.make_async_remote_copy(
                src_ref=src.at[p],
                dst_ref=dst.at[p],
                send_sem=halo_send_sem.at[k],
                recv_sem=halo_sem.at[k],
                device_id=(segment, point),
                device_id_type=MESH,
            ).start()

    def convolve_two(h, _):
        pair = (POINTS // 2 + h, POINTS // 2 - 1 - h)
        for p in pair:
            convolve(p)
        for p in pair:
            send_sums(p)
        return 0

    lax.fori_loop(0, POINTS // 2, convolve_two, 0)

    sums = all_points(main_send, main_recv, main_send_sem, main_sem)
    halos = [
        pltpu.make_async_remote_copy(
            src_ref=src,
            dst_ref=dst,
            send_sem=halo_send_sem.at[k],
            recv_sem=halo_sem.at[k],
            device_id=(segment, tp),
            device_id_type=MESH,
        )
        for k, (src, dst, segment) in enumerate(
            ((left_send, left_recv, left), (right_send, right_recv, right))
        )
    ]
    for halo in halos:
        halo.wait_recv()
    from_right = unfold(jnp.sum(left_recv[...], axis=0))
    from_left = unfold(jnp.sum(right_recv[...], axis=0))
    from_right = jnp.where(me < n - 1, pltpu.roll(from_right, 112, 1), 0.0)
    from_left = jnp.where(me > 0, from_left, 0.0)
    first = main_send[0, 0] + from_left
    second = main_send[0, 1] + from_right
    sums.wait_recv()
    for p in range(1, POINTS):
        first += main_recv[p, 0]
        second += main_recv[p, 1]
    for k, part in enumerate((first, second)):
        tall = jnp.concatenate([part, jnp.zeros((120, 128), jnp.float32)], axis=0)
        ordered[pl.ds(128 * k, 128), :] = tall.T
    total = ordered[pl.ds(0, 16, stride=16), :]
    for k in range(1, 16):
        total += pltpu.roll(ordered[pl.ds(k, 16, stride=16), :], 8 * k, 1)
    out_ref[...] = total

    all_points(points, points, point_send_sem, point_sem).wait_send()
    all_points(shapes, shapes, shape_send_sem, shape_sem).wait_send()
    pl.when(jnp.logical_not(stays))(lambda: lines_to(0, first_sem).wait_send())
    pltpu.make_async_remote_copy(
        src_ref=send.at[pl.ds(1, octets - 1)],
        dst_ref=recv.at[pl.ds(1, octets - 1)],
        send_sem=send_sem,
        recv_sem=recv_sem.at[1],
        device_id=(partner(1), tp),
        device_id_type=MESH,
    ).wait_send()
    sums.wait_send()
    for halo in halos:
        halo.wait_send()


def body(
    natural_logged_absorbance,
    lower_state_level,
    subgrid_shift_ratio,
    local_grid_slot,
    broadening_class,
    tallies_per_shard,
    heat_levels,
    sum_over_states_ratio,
    shape_kernels,
):
    n = lax.axis_size("seg")
    lines = natural_logged_absorbance.shape[0]
    tiles = lines // 128
    hbm = pl.BlockSpec(memory_space=pl.ANY)
    vmem = pl.BlockSpec(memory_space=pltpu.VMEM)
    f32, bf16, i32 = jnp.float32, jnp.bfloat16, jnp.int32
    dma = pltpu.SemaphoreType.DMA
    result = pl.pallas_call(
        functools.partial(kernel, n),
        out_shape=jax.ShapeDtypeStruct((16, 128), f32),
        in_specs=[hbm] * 9,
        out_specs=vmem,
        scratch_shapes=[
            pltpu.SMEM((1, 1), f32),
            pltpu.SMEM((1, 1), f32),
            pltpu.SMEM((8, n), i32),
            pltpu.VMEM((tiles + 16, 128), f32),
            pltpu.VMEM((tiles + 16, 128), f32),
            pltpu.VMEM((tiles + 16, 128), f32),
            pltpu.VMEM((tiles, 128), i32),
            pltpu.VMEM((tiles, 128), i32),
            pltpu.VMEM((tiles + 16, 128), f32),
            pltpu.VMEM((tiles + 16, 128), f32),
            pltpu.SMEM((n,), i32),
            pltpu.VMEM((n // 8, FIELDS, PARTS, 128), f32),
            pltpu.VMEM((n // 8, FIELDS, PARTS, 128), f32),
            pltpu.VMEM((POINTS, 1, 128), f32),
            pltpu.VMEM((POINTS, NW, 256), f32),
            pltpu.VMEM((CAP, BLOCKS), bf16),
            pltpu.VMEM((COLS, CAP), bf16),
            pltpu.VMEM((CAP, BLOCKS), bf16),
            pltpu.VMEM((COLS, CAP), bf16),
            pltpu.VMEM((COLS, BLOCKS), f32),
            pltpu.VMEM((POINTS, REACH, 2 * JW), bf16),
            pltpu.VMEM((POINTS, REACH, 2 * JW), bf16),
            pltpu.VMEM((COLS, BLOCKS), bf16),
            pltpu.VMEM((COLS, BLOCKS), bf16),
            pltpu.VMEM((POINTS, 2, 8, 128), f32),
            pltpu.VMEM((POINTS, 1, 128), f32),
            pltpu.VMEM((POINTS, 1, 128), f32),
            pltpu.VMEM((POINTS, 2, 8, 128), f32),
            pltpu.VMEM((POINTS, 1, 128), f32),
            pltpu.VMEM((POINTS, 1, 128), f32),
            pltpu.VMEM((BLOCKS, 128), f32),
            dma((9,)),
            dma,
            dma,
            dma((n // 8,)),
            dma,
            dma,
            dma,
            dma,
            dma,
            dma,
            dma((2,)),
            dma((2,)),
        ],
        compiler_params=pltpu.CompilerParams(
            collective_id=0, has_side_effects=True, vmem_limit_bytes=56541184
        ),
        cost_estimate=pl.CostEstimate(
            flops=2 * n * CAP // 8 * BLOCKS * COLS,
            bytes_accessed=300000,
            transcendentals=n * CAP // 8 * POINTS,
        ),
    )(
        heat_levels.reshape(1, 1),
        sum_over_states_ratio.reshape(1, 1),
        tallies_per_shard,
        natural_logged_absorbance.reshape(tiles, 128),
        lower_state_level.reshape(tiles, 128),
        subgrid_shift_ratio.reshape(tiles, 128),
        local_grid_slot.reshape(tiles, 128),
        broadening_class.reshape(tiles, 128),
        shape_kernels[0],
    )
    return result.reshape(1, G)


def solution(mesh):
    in_specs = (
        P("seg"),
        P("seg"),
        P("seg"),
        P("seg"),
        P("seg"),
        P(),
        P("tp"),
        P("tp"),
        P("tp", None, None),
    )
    out_specs = P("tp", "seg")
    return jax.shard_map(body, mesh=mesh, in_specs=in_specs, out_specs=out_specs, check_vma=False)
```

```python
import functools

import jax
import jax.numpy as jnp
from jax import lax
from jax.experimental import pallas as pl
from jax.experimental.pallas import tpu as pltpu
from jax.sharding import PartitionSpec as P

MESH = pl.DeviceIdType.MESH

G = 2048
NW = 16
POINTS = 8
CAP = 768
FIELDS = 5
J = 9
JW = 8 * NW
COLS = POINTS * JW + JW
BLOCKS = G // 8
PARTS = CAP // 128
REACH = 272
PACK = 4

planck_hc_over_boltzmann = 1.4388
baseline_heat_level = 900.0


def split(x):
    high = x.astype(jnp.bfloat16)
    return high, (x - high.astype(jnp.float32)).astype(jnp.bfloat16)


def kernel(
    n,
    heat_ref,
    ratio_ref,
    tallies_ref,
    absorb_ref,
    level_ref,
    shift_ref,
    slot_ref,
    class_ref,
    shape_ref,
    out_ref,
    heat,
    ratio,
    tallies,
    absorb,
    level,
    shift,
    slot,
    width,
    slot_value,
    width_value,
    starts,
    send,
    recv,
    points,
    shapes,
    rows0,
    cols0,
    rows1,
    cols1,
    acc,
    taps_high,
    taps_low,
    bins_high,
    bins_low,
    main_send,
    left_send,
    right_send,
    main_recv,
    left_recv,
    right_recv,
    ordered,
    in_sem,
    send_sem,
    first_sem,
    recv_sem,
    point_send_sem,
    point_sem,
    shape_send_sem,
    shape_sem,
    main_send_sem,
    main_sem,
    halo_send_sem,
    halo_sem,
):
    me = lax.axis_index("seg")
    tp = lax.axis_index("tp")
    left = lax.rem(me + n - 1, n)
    right = lax.rem(me + 1, n)

    tiles = slot.shape[0]
    eight = pl.multiple_of((me // 8) * 8, 8)
    copies = [
        pltpu.make_async_copy(src, dst, in_sem.at[k])
        for k, (src, dst) in enumerate(
            (
                (heat_ref, heat),
                (ratio_ref, ratio),
                (tallies_ref.at[pl.ds(eight, 8)], tallies),
                (absorb_ref, absorb.at[pl.ds(0, tiles)]),
                (level_ref, level.at[pl.ds(0, tiles)]),
                (shift_ref, shift.at[pl.ds(0, tiles)]),
                (slot_ref, slot),
                (class_ref, width),
                (shape_ref, shapes.at[0]),
            )
        )
    ]
    for copy in copies:
        copy.start()

    eighth = lax.rem(tp + n - lax.rem(me, 8), 8)
    stays = eighth == lax.rem(me, 8)
    octets = n // 8

    def partner(i):
        return eighth + 8 * lax.rem(me // 8 + i, octets)

    barrier = pltpu.get_barrier_semaphore()

    def greet(segment, point):
        pl.semaphore_signal(
            barrier, inc=1, device_id=(segment, point), device_id_type=MESH
        )

    for i in range(octets):
        if i == 0:
            pl.when(jnp.logical_not(stays))(lambda: greet(partner(0), tp))
        else:
            greet(partner(i), tp)
    for i in range(1, POINTS):
        for segment in (me, left, right):
            greet(segment, lax.rem(tp + i, POINTS))
    greet(left, tp)
    greet(right, tp)

    lane8 = lax.broadcasted_iota(jnp.int32, (8, 128), 1)
    sub8 = lax.broadcasted_iota(jnp.int32, (8, 128), 0)
    acc[...] = jnp.zeros_like(acc)

    for copy in copies[:3]:
        copy.wait()

    points[0] = jnp.where(lane8[:1] < 64, heat[0, 0], ratio[0, 0])

    def add_up(d, total):
        for u in range(8):
            starts[8 * d + u] = total
            total = total + tallies[lax.rem(me, 8), 8 * d + u]
        return total

    lax.fori_loop(0, octets, add_up, jnp.int32(0))

    for copy in copies[3:]:
        copy.wait()

    fields = (absorb, level, shift, slot_value, width_value)
    slot_value[pl.ds(0, tiles)] = slot[...].astype(jnp.float32)
    width_value[pl.ds(0, tiles)] = width[...].astype(jnp.float32)
    for field in fields:
        field[pl.ds(tiles, 16)] = jnp.zeros((16, 128), jnp.float32)
    position = 128 * sub8 + lane8

    def pack(target):
        begin = starts[target]
        count = tallies[lax.rem(me, 8), target]
        tile = lax.shift_right_logical(begin, 7)
        offset = jnp.full((8, 128), lax.bitwise_and(begin, 127))
        here, after = pl.ds(tile, 8), pl.ds(tile + 1, 8)
        windows = []
        for f, field in enumerate(fields):
            window = jnp.where(lane8 >= offset, field[here, :], field[after, :])
            for unit in (1, 4, 16):
                digit = lax.bitwise_and(offset, 3 * unit)
                turned = [pltpu.roll(window, 128 - k * unit, 1) for k in (1, 2, 3)]
                for k in (1, 2, 3):
                    window = jnp.where(digit == k * unit, turned[k - 1], window)
            turned = pltpu.roll(window, 64, 1)
            window = jnp.where(offset >= 64, turned, window)
            if f == FIELDS - 1:
                window = jnp.where(position >= count, float(NW), window)
            windows.append(window[:PARTS])
        return windows

    def pack_some(batch, _):
        first = batch * PACK
        packed = [pack(partner(first + u)) for u in range(PACK)]
        for u in range(PACK):
            for f in range(FIELDS):
                send[first + u, f] = packed[u][f]
        return 0

    lax.fori_loop(0, octets // PACK, pack_some, 0)

    pl.semaphore_wait(barrier, octets + 2 + 3 * (POINTS - 1) - jnp.where(stays, 1, 0))

    def share(src, dst, sem_send, sem_recv):
        for i in range(1, POINTS):
            pltpu.make_async_remote_copy(
                src_ref=src.at[0],
                dst_ref=dst.at[i],
                send_sem=sem_send,
                recv_sem=sem_recv,
                device_id=(me, lax.rem(tp + i, POINTS)),
                device_id_type=MESH,
            ).start()

    def lines_to(i, sem):
        return pltpu.make_async_remote_copy(
            src_ref=send.at[i],
            dst_ref=recv.at[i],
            send_sem=sem,
            recv_sem=recv_sem.at[i],
            device_id=(partner(i), tp),
            device_id_type=MESH,
        )

    pl.when(jnp.logical_not(stays))(lambda: lines_to(0, first_sem).start())
    pl.when(stays)(
        lambda: pltpu.make_async_copy(
            send.at[0], recv.at[0], recv_sem.at[0]
        ).start()
    )
    share(points, points, point_send_sem, point_sem)
    for i in range(1, octets):
        lines_to(i, send_sem).start()
    share(shapes, shapes, shape_send_sem, shape_sem)

    def all_points(src, dst, sem_send, sem_recv):
        return pltpu.make_async_remote_copy(
            src_ref=src.at[pl.ds(1, POINTS - 1)],
            dst_ref=dst.at[pl.ds(1, POINTS - 1)],
            send_sem=sem_send,
            recv_sem=sem_recv,
            device_id=(me, lax.rem(tp + 1, POINTS)),
            device_id_type=MESH,
        )

    all_points(points, points, point_send_sem, point_sem).wait_recv()
    both = jnp.concatenate([points[i] for i in range(POINTS)], axis=0)
    heats = jnp.where(lane8 < 64, both, pltpu.roll(both, 64, 1))
    ratios = jnp.where(lane8 < 64, pltpu.roll(both, 64, 1), both)
    inverse_gap = 1.0 / heats - 1.0 / baseline_heat_level

    block_ids = lax.broadcasted_iota(jnp.int32, (128, BLOCKS), 1).astype(jnp.float32)
    width_ids = lax.broadcasted_iota(jnp.int32, (NW, 128), 0).astype(jnp.float32)
    point_lane = lax.broadcasted_iota(jnp.int32, (REACH, JW), 1) // NW

    def spread(row):
        return jnp.broadcast_to(row, (NW, 128)).astype(jnp.bfloat16)

    def arrived(g):
        pltpu.make_async_remote_copy(
            src_ref=send.at[g],
            dst_ref=recv.at[g],
            send_sem=send_sem,
            recv_sem=recv_sem.at[g],
            device_id=(partner(1), tp),
            device_id_type=MESH,
        ).wait_recv()

    def one_hots(g, rows, cols):
        absorbs, levels, shifts, slots, widths = (recv[g, f] for f in range(FIELDS))
        blocks = jnp.floor(slots * 0.125)
        cells = slots - 8.0 * blocks
        halves = cells * 0.5
        even_cell = jnp.where(halves == jnp.floor(halves), 1.0, 0.0)
        here = [cells == float(j) for j in range(8)]
        touched = [
            here[0],
            *(jnp.logical_or(here[j], here[j - 1]) for j in range(1, 8)),
            here[7],
        ]
        touched = [jnp.where(t, 1.0, 0.0) for t in touched]
        tall = jnp.concatenate([blocks, blocks[: 8 - PARTS]], axis=0).T
        scaled = planck_hc_over_boltzmann * levels
        below = 1.0 - shifts

        def one_hot(part):
            line = slice(part, part + 1)
            at = part * 128
            hits = jnp.broadcast_to(tall[:, line], (128, BLOCKS)) == block_ids
            rows[pl.ds(at, 128), :] = jnp.where(hits, 1.0, 0.0).astype(jnp.bfloat16)
            strength = ratios * jnp.exp(absorbs[line] - scaled[line] * inverse_gap)
            low = strength * below[line]
            high = strength * shifts[line]
            is_even = jnp.broadcast_to(even_cell[line], (POINTS, 128)) > 0.5
            evens = jnp.where(is_even, low, high)
            odds = jnp.where(is_even, high, low)
            is_width = jnp.broadcast_to(widths[line], (NW, 128)) == width_ids
            is_width = jnp.where(is_width, 1.0, 0.0).astype(jnp.bfloat16)
            cell_hits = [spread(t[line]) for t in touched]
            for p in range(POINTS):
                even = spread(evens[p : p + 1]) * is_width
                odd = spread(odds[p : p + 1]) * is_width
                for j in range(J):
                    top = p * JW + j * NW if j < 8 else POINTS * JW + p * NW
                    value = (odd if j % 2 else even) * cell_hits[j]
                    cols[pl.ds(top, NW), pl.ds(at, 128)] = value

        return [functools.partial(one_hot, part) for part in range(PARTS)]

    def add_product(piece, rows, cols):
        some = pl.ds(piece * (COLS // PARTS), COLS // PARTS)
        acc[some] += jnp.dot(
            cols[some], rows[...], preferred_element_type=jnp.float32
        )

    def make_taps(p):
        taps = jnp.concatenate([shapes[p], jnp.zeros((NW, 128), jnp.float32)], axis=1)
        moved = [taps] + [pltpu.roll(taps, j, 1) for j in range(1, 8)]
        tall = jnp.concatenate(moved, axis=0).T[:REACH]
        ninth = jnp.concatenate([jnp.zeros((8, JW), jnp.float32), tall[:-8]], axis=0)
        ninth = jnp.where(point_lane == p, pltpu.roll(ninth, NW * p, 1), 0.0)
        high, low = split(jnp.concatenate([tall, ninth], axis=1))
        taps_high[p] = high
        taps_low[p] = low

    def step(g, rows, cols, last_rows, last_cols):
        for part, make in enumerate(one_hots(g, rows, cols)):
            add_product(part, last_rows, last_cols)
            make()

    make_taps(0)
    arrived(0)
    for make in one_hots(0, rows0, cols0):
        make()

    def deposit(h, _):
        arrived(2 * h + 1)
        arrived(2 * h + 2)
        step(2 * h + 1, rows1, cols1, rows0, cols0)
        step(2 * h + 2, rows0, cols0, rows1, cols1)
        return 0

    lax.fori_loop(0, octets // 2 - 2, deposit, 0)
    all_points(shapes, shapes, shape_send_sem, shape_sem).wait_recv()
    for g in range(octets - 3, octets):
        arrived(g)
    step(octets - 3, rows1, cols1, rows0, cols0)
    make_taps(1)
    make_taps(2)
    step(octets - 2, rows0, cols0, rows1, cols1)
    make_taps(3)
    make_taps(4)
    step(octets - 1, rows1, cols1, rows0, cols0)
    for p in range(5, POINTS):
        make_taps(p)
    for piece in range(PARTS):
        add_product(piece, rows1, cols1)
    high, low = split(acc[...])
    bins_high[...] = high
    bins_low[...] = low

    def fold(x):
        kept = jnp.where(lane8 < 16, x, 0.0)
        moved = pltpu.roll(kept, 0, 1, stride=16, stride_axis=0)
        return jnp.sum(moved, axis=0, keepdims=True)

    def unfold(row):
        wide = jnp.broadcast_to(row, (8, 128))
        moved = wide
        for i in range(1, 8):
            moved = jnp.where(sub8 == i, pltpu.roll(wide, 128 - 16 * i, 1), moved)
        return jnp.where(lane8 < 16, moved, 0.0)

    def convolve(p):
        own = pl.ds(pl.multiple_of(p * JW, JW), JW)
        ninth = pl.ds(POINTS * JW, JW)
        bin_high = jnp.concatenate([bins_high[own], bins_high[ninth]], axis=0)
        bin_low = jnp.concatenate([bins_low[own], bins_low[ninth]], axis=0)
        product = jnp.dot(taps_high[p], bin_high, preferred_element_type=jnp.float32)
        product += jnp.dot(taps_low[p], bin_high, preferred_element_type=jnp.float32)
        product += jnp.dot(taps_high[p], bin_low, preferred_element_type=jnp.float32)
        first, second = product[128:136, :128], product[128:136, 128:]
        outside = jnp.zeros((8, 128), jnp.float32)
        for m in range(33):
            by = m - 16
            if by == 0:
                continue
            front, back = product[8 * m : 8 * m + 8, :128], product[8 * m : 8 * m + 8, 128:]
            front = pltpu.roll(front, by % 128, 1)
            back = pltpu.roll(back, by % 128, 1)
            if by > 0:
                wraps = lane8 < by
                first += jnp.where(wraps, 0.0, front)
                second += jnp.where(wraps, front, back)
                outside += jnp.where(wraps, back, 0.0)
            else:
                wraps = lane8 >= 128 + by
                first += jnp.where(wraps, back, front)
                second += jnp.where(wraps, 0.0, back)
                outside += jnp.where(wraps, front, 0.0)
        main_send[p, 0] = first
        main_send[p, 1] = second
        left_send[p] = fold(pltpu.roll(outside, 16, 1))
        right_send[p] = fold(outside)

    def send_sums(p):
        point = lax.rem(tp + POINTS - p, POINTS)

        @pl.when(p > 0)
        def _():
            pltpu.make_async_remote_copy(
                src_ref=main_send.at[p],
                dst_ref=main_recv.at[p],
                send_sem=main_send_sem,
                recv_sem=main_sem,
                device_id=(me, point),
                device_id_type=MESH,
            ).start()

        for k, (src, dst, segment) in enumerate(
            ((left_send, left_recv, left), (right_send, right_recv, right))
        ):
            pltpu.make_async_remote_copy(
                src_ref=src.at[p],
                dst_ref=dst.at[p],
                send_sem=halo_send_sem.at[k],
                recv_sem=halo_sem.at[k],
                device_id=(segment, point),
                device_id_type=MESH,
            ).start()

    def convolve_two(h, _):
        pair = (POINTS // 2 + h, POINTS // 2 - 1 - h)
        for p in pair:
            convolve(p)
        for p in pair:
            send_sums(p)
        return 0

    lax.fori_loop(0, POINTS // 2, convolve_two, 0)

    sums = all_points(main_send, main_recv, main_send_sem, main_sem)
    halos = [
        pltpu.make_async_remote_copy(
            src_ref=src,
            dst_ref=dst,
            send_sem=halo_send_sem.at[k],
            recv_sem=halo_sem.at[k],
            device_id=(segment, tp),
            device_id_type=MESH,
        )
        for k, (src, dst, segment) in enumerate(
            ((left_send, left_recv, left), (right_send, right_recv, right))
        )
    ]
    for halo in halos:
        halo.wait_recv()
    from_right = unfold(jnp.sum(left_recv[...], axis=0))
    from_left = unfold(jnp.sum(right_recv[...], axis=0))
    from_right = jnp.where(me < n - 1, pltpu.roll(from_right, 112, 1), 0.0)
    from_left = jnp.where(me > 0, from_left, 0.0)
    first = main_send[0, 0] + from_left
    second = main_send[0, 1] + from_right
    sums.wait_recv()
    for p in range(1, POINTS):
        first += main_recv[p, 0]
        second += main_recv[p, 1]
    for k, part in enumerate((first, second)):
        tall = jnp.concatenate([part, jnp.zeros((120, 128), jnp.float32)], axis=0)
        ordered[pl.ds(128 * k, 128), :] = tall.T
    total = ordered[pl.ds(0, 16, stride=16), :]
    for k in range(1, 16):
        total += pltpu.roll(ordered[pl.ds(k, 16, stride=16), :], 8 * k, 1)
    out_ref[...] = total

    all_points(points, points, point_send_sem, point_sem).wait_send()
    all_points(shapes, shapes, shape_send_sem, shape_sem).wait_send()
    pl.when(jnp.logical_not(stays))(lambda: lines_to(0, first_sem).wait_send())
    pltpu.make_async_remote_copy(
        src_ref=send.at[pl.ds(1, octets - 1)],
        dst_ref=recv.at[pl.ds(1, octets - 1)],
        send_sem=send_sem,
        recv_sem=recv_sem.at[1],
        device_id=(partner(1), tp),
        device_id_type=MESH,
    ).wait_send()
    sums.wait_send()
    for halo in halos:
        halo.wait_send()


def body(
    natural_logged_absorbance,
    lower_state_level,
    subgrid_shift_ratio,
    local_grid_slot,
    broadening_class,
    tallies_per_shard,
    heat_levels,
    sum_over_states_ratio,
    shape_kernels,
):
    n = lax.axis_size("seg")
    lines = natural_logged_absorbance.shape[0]
    tiles = lines // 128
    hbm = pl.BlockSpec(memory_space=pl.ANY)
    vmem = pl.BlockSpec(memory_space=pltpu.VMEM)
    f32, bf16, i32 = jnp.float32, jnp.bfloat16, jnp.int32
    dma = pltpu.SemaphoreType.DMA
    result = pl.pallas_call(
        functools.partial(kernel, n),
        out_shape=jax.ShapeDtypeStruct((16, 128), f32),
        in_specs=[hbm] * 9,
        out_specs=vmem,
        scratch_shapes=[
            pltpu.SMEM((1, 1), f32),
            pltpu.SMEM((1, 1), f32),
            pltpu.SMEM((8, n), i32),
            pltpu.VMEM((tiles + 16, 128), f32),
            pltpu.VMEM((tiles + 16, 128), f32),
            pltpu.VMEM((tiles + 16, 128), f32),
            pltpu.VMEM((tiles, 128), i32),
            pltpu.VMEM((tiles, 128), i32),
            pltpu.VMEM((tiles + 16, 128), f32),
            pltpu.VMEM((tiles + 16, 128), f32),
            pltpu.SMEM((n,), i32),
            pltpu.VMEM((n // 8, FIELDS, PARTS, 128), f32),
            pltpu.VMEM((n // 8, FIELDS, PARTS, 128), f32),
            pltpu.VMEM((POINTS, 1, 128), f32),
            pltpu.VMEM((POINTS, NW, 256), f32),
            pltpu.VMEM((CAP, BLOCKS), bf16),
            pltpu.VMEM((COLS, CAP), bf16),
            pltpu.VMEM((CAP, BLOCKS), bf16),
            pltpu.VMEM((COLS, CAP), bf16),
            pltpu.VMEM((COLS, BLOCKS), f32),
            pltpu.VMEM((POINTS, REACH, 2 * JW), bf16),
            pltpu.VMEM((POINTS, REACH, 2 * JW), bf16),
            pltpu.VMEM((COLS, BLOCKS), bf16),
            pltpu.VMEM((COLS, BLOCKS), bf16),
            pltpu.VMEM((POINTS, 2, 8, 128), f32),
            pltpu.VMEM((POINTS, 1, 128), f32),
            pltpu.VMEM((POINTS, 1, 128), f32),
            pltpu.VMEM((POINTS, 2, 8, 128), f32),
            pltpu.VMEM((POINTS, 1, 128), f32),
            pltpu.VMEM((POINTS, 1, 128), f32),
            pltpu.VMEM((BLOCKS, 128), f32),
            dma((9,)),
            dma,
            dma,
            dma((n // 8,)),
            dma,
            dma,
            dma,
            dma,
            dma,
            dma,
            dma((2,)),
            dma((2,)),
        ],
        compiler_params=pltpu.CompilerParams(
            collective_id=0, has_side_effects=True, vmem_limit_bytes=56541184
        ),
        cost_estimate=pl.CostEstimate(
            flops=2 * n * CAP // 8 * BLOCKS * COLS,
            bytes_accessed=300000,
            transcendentals=n * CAP // 8 * POINTS,
        ),
    )(
        heat_levels.reshape(1, 1),
        sum_over_states_ratio.reshape(1, 1),
        tallies_per_shard,
        natural_logged_absorbance.reshape(tiles, 128),
        lower_state_level.reshape(tiles, 128),
        subgrid_shift_ratio.reshape(tiles, 128),
        local_grid_slot.reshape(tiles, 128),
        broadening_class.reshape(tiles, 128),
        shape_kernels[0],
    )
    return result.reshape(1, G)


def solution(mesh):
    in_specs = (
        P("seg"),
        P("seg"),
        P("seg"),
        P("seg"),
        P("seg"),
        P(),
        P("tp"),
        P("tp"),
        P("tp", None, None),
    )
    out_specs = P("tp", "seg")
    return jax.shard_map(body, mesh=mesh, in_specs=in_specs, out_specs=out_specs, check_vma=False)
```

```python
import functools

import jax
import jax.numpy as jnp
from jax import lax
from jax.experimental import pallas as pl
from jax.experimental.pallas import tpu as pltpu
from jax.sharding import PartitionSpec as P

MESH = pl.DeviceIdType.MESH

G = 2048
NW = 16
POINTS = 8
CAP = 768
FIELDS = 5
J = 9
JW = 8 * NW
COLS = POINTS * JW + JW
BLOCKS = G // 8
PARTS = CAP // 128
REACH = 272
PACK = 4

planck_hc_over_boltzmann = 1.4388
baseline_heat_level = 900.0


def split(x):
    high = x.astype(jnp.bfloat16)
    return high, (x - high.astype(jnp.float32)).astype(jnp.bfloat16)


def kernel(
    n,
    heat_ref,
    ratio_ref,
    tallies_ref,
    absorb_ref,
    level_ref,
    shift_ref,
    slot_ref,
    class_ref,
    shape_ref,
    out_ref,
    heat,
    ratio,
    tallies,
    absorb,
    level,
    shift,
    slot,
    width,
    slot_value,
    width_value,
    starts,
    send,
    recv,
    points,
    shapes,
    rows0,
    cols0,
    rows1,
    cols1,
    acc,
    taps_high,
    taps_low,
    bins_high,
    bins_low,
    main_send,
    left_send,
    right_send,
    main_recv,
    left_recv,
    right_recv,
    ordered,
    in_sem,
    send_sem,
    first_sem,
    recv_sem,
    point_send_sem,
    point_sem,
    shape_send_sem,
    shape_sem,
    main_send_sem,
    main_sem,
    halo_send_sem,
    halo_sem,
):
    me = lax.axis_index("seg")
    tp = lax.axis_index("tp")
    left = lax.rem(me + n - 1, n)
    right = lax.rem(me + 1, n)

    tiles = slot.shape[0]
    eight = pl.multiple_of((me // 8) * 8, 8)
    copies = [
        pltpu.make_async_copy(src, dst, in_sem.at[k])
        for k, (src, dst) in enumerate(
            (
                (heat_ref, heat),
                (ratio_ref, ratio),
                (tallies_ref.at[pl.ds(eight, 8)], tallies),
                (absorb_ref, absorb.at[pl.ds(0, tiles)]),
                (level_ref, level.at[pl.ds(0, tiles)]),
                (shift_ref, shift.at[pl.ds(0, tiles)]),
                (slot_ref, slot),
                (class_ref, width),
                (shape_ref, shapes.at[0]),
            )
        )
    ]
    for copy in copies:
        copy.start()

    eighth = lax.rem(tp + n - lax.rem(me, 8), 8)
    stays = eighth == lax.rem(me, 8)
    octets = n // 8

    def partner(i):
        return eighth + 8 * lax.rem(me // 8 + i, octets)

    barrier = pltpu.get_barrier_semaphore()

    def greet(segment, point):
        pl.semaphore_signal(
            barrier, inc=1, device_id=(segment, point), device_id_type=MESH
        )

    for i in range(octets):
        if i == 0:
            pl.when(jnp.logical_not(stays))(lambda: greet(partner(0), tp))
        else:
            greet(partner(i), tp)
    for i in range(1, POINTS):
        for segment in (me, left, right):
            greet(segment, lax.rem(tp + i, POINTS))
    greet(left, tp)
    greet(right, tp)

    lane8 = lax.broadcasted_iota(jnp.int32, (8, 128), 1)
    sub8 = lax.broadcasted_iota(jnp.int32, (8, 128), 0)
    acc[...] = jnp.zeros_like(acc)

    for copy in copies[:3]:
        copy.wait()

    points[0] = jnp.where(lane8[:1] < 64, heat[0, 0], ratio[0, 0])

    def add_up(d, total):
        for u in range(8):
            starts[8 * d + u] = total
            total = total + tallies[lax.rem(me, 8), 8 * d + u]
        return total

    lax.fori_loop(0, octets, add_up, jnp.int32(0))

    for copy in copies[3:]:
        copy.wait()

    fields = (absorb, level, shift, slot_value, width_value)
    slot_value[pl.ds(0, tiles)] = slot[...].astype(jnp.float32)
    width_value[pl.ds(0, tiles)] = width[...].astype(jnp.float32)
    for field in fields:
        field[pl.ds(tiles, 16)] = jnp.zeros((16, 128), jnp.float32)
    position = 128 * sub8 + lane8

    def pack(target):
        begin = starts[target]
        count = tallies[lax.rem(me, 8), target]
        tile = lax.shift_right_logical(begin, 7)
        offset = jnp.full((8, 128), lax.bitwise_and(begin, 127))
        here, after = pl.ds(tile, 8), pl.ds(tile + 1, 8)
        windows = []
        for f, field in enumerate(fields):
            window = jnp.where(lane8 >= offset, field[here, :], field[after, :])
            for unit in (1, 4, 16):
                digit = lax.bitwise_and(offset, 3 * unit)
                turned = [pltpu.roll(window, 128 - k * unit, 1) for k in (1, 2, 3)]
                for k in (1, 2, 3):
                    window = jnp.where(digit == k * unit, turned[k - 1], window)
            turned = pltpu.roll(window, 64, 1)
            window = jnp.where(offset >= 64, turned, window)
            if f == FIELDS - 1:
                window = jnp.where(position >= count, float(NW), window)
            windows.append(window[:PARTS])
        return windows

    def pack_some(batch, _):
        first = batch * PACK
        packed = [pack(partner(first + u)) for u in range(PACK)]
        for u in range(PACK):
            for f in range(FIELDS):
                send[first + u, f] = packed[u][f]
        return 0

    lax.fori_loop(0, octets // PACK, pack_some, 0)

    pl.semaphore_wait(barrier, octets + 2 + 3 * (POINTS - 1) - jnp.where(stays, 1, 0))

    def share(src, dst, sem_send, sem_recv):
        for i in range(1, POINTS):
            pltpu.make_async_remote_copy(
                src_ref=src.at[0],
                dst_ref=dst.at[i],
                send_sem=sem_send,
                recv_sem=sem_recv,
                device_id=(me, lax.rem(tp + i, POINTS)),
                device_id_type=MESH,
            ).start()

    def lines_to(i, sem):
        return pltpu.make_async_remote_copy(
            src_ref=send.at[i],
            dst_ref=recv.at[i],
            send_sem=sem,
            recv_sem=recv_sem.at[i],
            device_id=(partner(i), tp),
            device_id_type=MESH,
        )

    pl.when(jnp.logical_not(stays))(lambda: lines_to(0, first_sem).start())
    pl.when(stays)(
        lambda: pltpu.make_async_copy(
            send.at[0], recv.at[0], recv_sem.at[0]
        ).start()
    )
    share(points, points, point_send_sem, point_sem)
    for i in range(1, octets):
        lines_to(i, send_sem).start()
    share(shapes, shapes, shape_send_sem, shape_sem)

    def all_points(src, dst, sem_send, sem_recv):
        return pltpu.make_async_remote_copy(
            src_ref=src.at[pl.ds(1, POINTS - 1)],
            dst_ref=dst.at[pl.ds(1, POINTS - 1)],
            send_sem=sem_send,
            recv_sem=sem_recv,
            device_id=(me, lax.rem(tp + 1, POINTS)),
            device_id_type=MESH,
        )

    all_points(points, points, point_send_sem, point_sem).wait_recv()
    both = jnp.concatenate([points[i] for i in range(POINTS)], axis=0)
    heats = jnp.where(lane8 < 64, both, pltpu.roll(both, 64, 1))
    ratios = jnp.where(lane8 < 64, pltpu.roll(both, 64, 1), both)
    inverse_gap = 1.0 / heats - 1.0 / baseline_heat_level

    block_ids = lax.broadcasted_iota(jnp.int32, (128, BLOCKS), 1).astype(jnp.float32)
    width_ids = lax.broadcasted_iota(jnp.int32, (NW, 128), 0).astype(jnp.float32)
    point_lane = lax.broadcasted_iota(jnp.int32, (REACH, JW), 1) // NW

    def spread(row):
        return jnp.broadcast_to(row, (NW, 128)).astype(jnp.bfloat16)

    def arrived(g):
        pltpu.make_async_remote_copy(
            src_ref=send.at[g],
            dst_ref=recv.at[g],
            send_sem=send_sem,
            recv_sem=recv_sem.at[g],
            device_id=(partner(1), tp),
            device_id_type=MESH,
        ).wait_recv()

    def one_hots(g, rows, cols):
        absorbs, levels, shifts, slots, widths = (recv[g, f] for f in range(FIELDS))
        blocks = jnp.floor(slots * 0.125)
        cells = slots - 8.0 * blocks
        halves = cells * 0.5
        even_cell = jnp.where(halves == jnp.floor(halves), 1.0, 0.0)
        here = [cells == float(j) for j in range(8)]
        touched = [
            here[0],
            *(jnp.logical_or(here[j], here[j - 1]) for j in range(1, 8)),
            here[7],
        ]
        touched = [jnp.where(t, 1.0, 0.0) for t in touched]
        tall = jnp.concatenate([blocks, blocks[: 8 - PARTS]], axis=0).T
        scaled = planck_hc_over_boltzmann * levels
        below = 1.0 - shifts

        def one_hot(part):
            line = slice(part, part + 1)
            at = part * 128
            hits = jnp.broadcast_to(tall[:, line], (128, BLOCKS)) == block_ids
            rows[pl.ds(at, 128), :] = jnp.where(hits, 1.0, 0.0).astype(jnp.bfloat16)
            strength = ratios * jnp.exp(absorbs[line] - scaled[line] * inverse_gap)
            low = strength * below[line]
            high = strength * shifts[line]
            is_even = jnp.broadcast_to(even_cell[line], (POINTS, 128)) > 0.5
            evens = jnp.where(is_even, low, high)
            odds = jnp.where(is_even, high, low)
            is_width = jnp.broadcast_to(widths[line], (NW, 128)) == width_ids
            is_width = jnp.where(is_width, 1.0, 0.0).astype(jnp.bfloat16)
            cell_hits = [spread(t[line]) for t in touched]
            for p in range(POINTS):
                even = spread(evens[p : p + 1]) * is_width
                odd = spread(odds[p : p + 1]) * is_width
                for j in range(J):
                    top = p * JW + j * NW if j < 8 else POINTS * JW + p * NW
                    value = (odd if j % 2 else even) * cell_hits[j]
                    cols[pl.ds(top, NW), pl.ds(at, 128)] = value

        return [functools.partial(one_hot, part) for part in range(PARTS)]

    def rows_of(piece):
        return pl.ds(piece * (COLS // PARTS), COLS // PARTS)

    def added(piece, rows, cols):
        some = rows_of(piece)
        return acc[some] + jnp.dot(
            cols[some], rows[...], preferred_element_type=jnp.float32
        )

    def add_product(piece, rows, cols):
        acc[rows_of(piece)] = added(piece, rows, cols)

    def make_taps(p):
        taps = jnp.concatenate([shapes[p], jnp.zeros((NW, 128), jnp.float32)], axis=1)
        moved = [taps] + [pltpu.roll(taps, j, 1) for j in range(1, 8)]
        tall = jnp.concatenate(moved, axis=0).T[:REACH]
        ninth = jnp.concatenate([jnp.zeros((8, JW), jnp.float32), tall[:-8]], axis=0)
        ninth = jnp.where(point_lane == p, pltpu.roll(ninth, NW * p, 1), 0.0)
        high, low = split(jnp.concatenate([tall, ninth], axis=1))
        taps_high[p] = high
        taps_low[p] = low

    def step(g, rows, cols, last_rows, last_cols):
        for part, make in enumerate(one_hots(g, rows, cols)):
            add_product(part, last_rows, last_cols)
            make()

    make_taps(0)
    arrived(0)
    for make in one_hots(0, rows0, cols0):
        make()

    def deposit(h, _):
        arrived(2 * h + 1)
        step(2 * h + 1, rows1, cols1, rows0, cols0)
        arrived(2 * h + 2)
        step(2 * h + 2, rows0, cols0, rows1, cols1)
        return 0

    lax.fori_loop(0, octets // 2 - 2, deposit, 0)
    all_points(shapes, shapes, shape_send_sem, shape_sem).wait_recv()
    for g in range(octets - 3, octets):
        arrived(g)
    step(octets - 3, rows1, cols1, rows0, cols0)
    make_taps(1)
    make_taps(2)
    step(octets - 2, rows0, cols0, rows1, cols1)
    make_taps(3)
    make_taps(4)
    step(octets - 1, rows1, cols1, rows0, cols0)
    for p in range(5, POINTS):
        make_taps(p)
    for piece in range(PARTS):
        high, low = split(added(piece, rows1, cols1))
        bins_high[rows_of(piece)] = high
        bins_low[rows_of(piece)] = low

    def fold(x):
        kept = jnp.where(lane8 < 16, x, 0.0)
        moved = pltpu.roll(kept, 0, 1, stride=16, stride_axis=0)
        return jnp.sum(moved, axis=0, keepdims=True)

    def unfold(row):
        wide = jnp.broadcast_to(row, (8, 128))
        moved = wide
        for i in range(1, 8):
            moved = jnp.where(sub8 == i, pltpu.roll(wide, 128 - 16 * i, 1), moved)
        return jnp.where(lane8 < 16, moved, 0.0)

    def convolve(p):
        own = pl.ds(pl.multiple_of(p * JW, JW), JW)
        ninth = pl.ds(POINTS * JW, JW)
        bin_high = jnp.concatenate([bins_high[own], bins_high[ninth]], axis=0)
        bin_low = jnp.concatenate([bins_low[own], bins_low[ninth]], axis=0)
        product = jnp.dot(taps_high[p], bin_high, preferred_element_type=jnp.float32)
        product += jnp.dot(taps_low[p], bin_high, preferred_element_type=jnp.float32)
        product += jnp.dot(taps_high[p], bin_low, preferred_element_type=jnp.float32)
        first, second = product[128:136, :128], product[128:136, 128:]
        outside = jnp.zeros((8, 128), jnp.float32)
        for m in range(33):
            by = m - 16
            if by == 0:
                continue
            front, back = product[8 * m : 8 * m + 8, :128], product[8 * m : 8 * m + 8, 128:]
            front = pltpu.roll(front, by % 128, 1)
            back = pltpu.roll(back, by % 128, 1)
            if by > 0:
                wraps = lane8 < by
                first += jnp.where(wraps, 0.0, front)
                second += jnp.where(wraps, front, back)
                outside += jnp.where(wraps, back, 0.0)
            else:
                wraps = lane8 >= 128 + by
                first += jnp.where(wraps, back, front)
                second += jnp.where(wraps, 0.0, back)
                outside += jnp.where(wraps, front, 0.0)
        main_send[p, 0] = first
        main_send[p, 1] = second
        left_send[p] = fold(pltpu.roll(outside, 16, 1))
        right_send[p] = fold(outside)

    def send_sums(p):
        point = lax.rem(tp + POINTS - p, POINTS)

        @pl.when(p > 0)
        def _():
            pltpu.make_async_remote_copy(
                src_ref=main_send.at[p],
                dst_ref=main_recv.at[p],
                send_sem=main_send_sem,
                recv_sem=main_sem,
                device_id=(me, point),
                device_id_type=MESH,
            ).start()

        for k, (src, dst, segment) in enumerate(
            ((left_send, left_recv, left), (right_send, right_recv, right))
        ):
            pltpu.make_async_remote_copy(
                src_ref=src.at[p],
                dst_ref=dst.at[p],
                send_sem=halo_send_sem.at[k],
                recv_sem=halo_sem.at[k],
                device_id=(segment, point),
                device_id_type=MESH,
            ).start()

    def convolve_two(h, _):
        pair = (POINTS // 2 + h, POINTS // 2 - 1 - h)
        for p in pair:
            convolve(p)
        for p in pair:
            send_sums(p)
        return 0

    lax.fori_loop(0, POINTS // 2, convolve_two, 0)

    sums = all_points(main_send, main_recv, main_send_sem, main_sem)
    halos = [
        pltpu.make_async_remote_copy(
            src_ref=src,
            dst_ref=dst,
            send_sem=halo_send_sem.at[k],
            recv_sem=halo_sem.at[k],
            device_id=(segment, tp),
            device_id_type=MESH,
        )
        for k, (src, dst, segment) in enumerate(
            ((left_send, left_recv, left), (right_send, right_recv, right))
        )
    ]
    for halo in halos:
        halo.wait_recv()
    from_right = unfold(jnp.sum(left_recv[...], axis=0))
    from_left = unfold(jnp.sum(right_recv[...], axis=0))
    from_right = jnp.where(me < n - 1, pltpu.roll(from_right, 112, 1), 0.0)
    from_left = jnp.where(me > 0, from_left, 0.0)
    first = main_send[0, 0] + from_left
    second = main_send[0, 1] + from_right
    sums.wait_recv()
    for p in range(1, POINTS):
        first += main_recv[p, 0]
        second += main_recv[p, 1]
    for k, part in enumerate((first, second)):
        tall = jnp.concatenate([part, jnp.zeros((120, 128), jnp.float32)], axis=0)
        ordered[pl.ds(128 * k, 128), :] = tall.T
    total = ordered[pl.ds(0, 16, stride=16), :]
    for k in range(1, 16):
        total += pltpu.roll(ordered[pl.ds(k, 16, stride=16), :], 8 * k, 1)
    out_ref[...] = total

    all_points(points, points, point_send_sem, point_sem).wait_send()
    all_points(shapes, shapes, shape_send_sem, shape_sem).wait_send()
    pl.when(jnp.logical_not(stays))(lambda: lines_to(0, first_sem).wait_send())
    pltpu.make_async_remote_copy(
        src_ref=send.at[pl.ds(1, octets - 1)],
        dst_ref=recv.at[pl.ds(1, octets - 1)],
        send_sem=send_sem,
        recv_sem=recv_sem.at[1],
        device_id=(partner(1), tp),
        device_id_type=MESH,
    ).wait_send()
    sums.wait_send()
    for halo in halos:
        halo.wait_send()


def body(
    natural_logged_absorbance,
    lower_state_level,
    subgrid_shift_ratio,
    local_grid_slot,
    broadening_class,
    tallies_per_shard,
    heat_levels,
    sum_over_states_ratio,
    shape_kernels,
):
    n = lax.axis_size("seg")
    lines = natural_logged_absorbance.shape[0]
    tiles = lines // 128
    hbm = pl.BlockSpec(memory_space=pl.ANY)
    vmem = pl.BlockSpec(memory_space=pltpu.VMEM)
    f32, bf16, i32 = jnp.float32, jnp.bfloat16, jnp.int32
    dma = pltpu.SemaphoreType.DMA
    result = pl.pallas_call(
        functools.partial(kernel, n),
        out_shape=jax.ShapeDtypeStruct((16, 128), f32),
        in_specs=[hbm] * 9,
        out_specs=vmem,
        scratch_shapes=[
            pltpu.SMEM((1, 1), f32),
            pltpu.SMEM((1, 1), f32),
            pltpu.SMEM((8, n), i32),
            pltpu.VMEM((tiles + 16, 128), f32),
            pltpu.VMEM((tiles + 16, 128), f32),
            pltpu.VMEM((tiles + 16, 128), f32),
            pltpu.VMEM((tiles, 128), i32),
            pltpu.VMEM((tiles, 128), i32),
            pltpu.VMEM((tiles + 16, 128), f32),
            pltpu.VMEM((tiles + 16, 128), f32),
            pltpu.SMEM((n,), i32),
            pltpu.VMEM((n // 8, FIELDS, PARTS, 128), f32),
            pltpu.VMEM((n // 8, FIELDS, PARTS, 128), f32),
            pltpu.VMEM((POINTS, 1, 128), f32),
            pltpu.VMEM((POINTS, NW, 256), f32),
            pltpu.VMEM((CAP, BLOCKS), bf16),
            pltpu.VMEM((COLS, CAP), bf16),
            pltpu.VMEM((CAP, BLOCKS), bf16),
            pltpu.VMEM((COLS, CAP), bf16),
            pltpu.VMEM((COLS, BLOCKS), f32),
            pltpu.VMEM((POINTS, REACH, 2 * JW), bf16),
            pltpu.VMEM((POINTS, REACH, 2 * JW), bf16),
            pltpu.VMEM((COLS, BLOCKS), bf16),
            pltpu.VMEM((COLS, BLOCKS), bf16),
            pltpu.VMEM((POINTS, 2, 8, 128), f32),
            pltpu.VMEM((POINTS, 1, 128), f32),
            pltpu.VMEM((POINTS, 1, 128), f32),
            pltpu.VMEM((POINTS, 2, 8, 128), f32),
            pltpu.VMEM((POINTS, 1, 128), f32),
            pltpu.VMEM((POINTS, 1, 128), f32),
            pltpu.VMEM((BLOCKS, 128), f32),
            dma((9,)),
            dma,
            dma,
            dma((n // 8,)),
            dma,
            dma,
            dma,
            dma,
            dma,
            dma,
            dma((2,)),
            dma((2,)),
        ],
        compiler_params=pltpu.CompilerParams(
            collective_id=0, has_side_effects=True, vmem_limit_bytes=56541184
        ),
        cost_estimate=pl.CostEstimate(
            flops=2 * n * CAP // 8 * BLOCKS * COLS,
            bytes_accessed=300000,
            transcendentals=n * CAP // 8 * POINTS,
        ),
    )(
        heat_levels.reshape(1, 1),
        sum_over_states_ratio.reshape(1, 1),
        tallies_per_shard,
        natural_logged_absorbance.reshape(tiles, 128),
        lower_state_level.reshape(tiles, 128),
        subgrid_shift_ratio.reshape(tiles, 128),
        local_grid_slot.reshape(tiles, 128),
        broadening_class.reshape(tiles, 128),
        shape_kernels[0],
    )
    return result.reshape(1, G)


def solution(mesh):
    in_specs = (
        P("seg"),
        P("seg"),
        P("seg"),
        P("seg"),
        P("seg"),
        P(),
        P("tp"),
        P("tp"),
        P("tp", None, None),
    )
    out_specs = P("tp", "seg")
    return jax.shard_map(body, mesh=mesh, in_specs=in_specs, out_specs=out_specs, check_vma=False)
```

```python
import functools

import jax
import jax.numpy as jnp
from jax import lax
from jax.experimental import pallas as pl
from jax.experimental.pallas import tpu as pltpu
from jax.sharding import PartitionSpec as P

MESH = pl.DeviceIdType.MESH

G = 2048
NW = 16
POINTS = 8
CAP = 768
FIELDS = 5
J = 9
JW = 8 * NW
COLS = POINTS * JW + JW
BLOCKS = G // 8
PARTS = CAP // 128
REACH = 272
PACK = 4

planck_hc_over_boltzmann = 1.4388
baseline_heat_level = 900.0


def split(x):
    high = x.astype(jnp.bfloat16)
    return high, (x - high.astype(jnp.float32)).astype(jnp.bfloat16)


def kernel(
    n,
    heat_ref,
    ratio_ref,
    tallies_ref,
    absorb_ref,
    level_ref,
    shift_ref,
    slot_ref,
    class_ref,
    shape_ref,
    out_ref,
    heat,
    ratio,
    tallies,
    absorb,
    level,
    shift,
    slot,
    width,
    slot_value,
    width_value,
    starts,
    send,
    recv,
    points,
    shapes,
    rows0,
    cols0,
    rows1,
    cols1,
    acc,
    taps_high,
    taps_low,
    bins_high,
    bins_low,
    main_send,
    left_send,
    right_send,
    main_recv,
    left_recv,
    right_recv,
    ordered,
    in_sem,
    send_sem,
    first_sem,
    recv_sem,
    point_send_sem,
    point_sem,
    shape_send_sem,
    shape_sem,
    main_send_sem,
    main_sem,
    halo_send_sem,
    halo_sem,
):
    me = lax.axis_index("seg")
    tp = lax.axis_index("tp")
    left = lax.rem(me + n - 1, n)
    right = lax.rem(me + 1, n)

    tiles = slot.shape[0]
    eight = pl.multiple_of((me // 8) * 8, 8)
    copies = [
        pltpu.make_async_copy(src, dst, in_sem.at[k])
        for k, (src, dst) in enumerate(
            (
                (heat_ref, heat),
                (ratio_ref, ratio),
                (tallies_ref.at[pl.ds(eight, 8)], tallies),
                (absorb_ref, absorb.at[pl.ds(0, tiles)]),
                (level_ref, level.at[pl.ds(0, tiles)]),
                (shift_ref, shift.at[pl.ds(0, tiles)]),
                (slot_ref, slot),
                (class_ref, width),
                (shape_ref, shapes.at[0]),
            )
        )
    ]
    for copy in copies:
        copy.start()

    eighth = lax.rem(tp + n - lax.rem(me, 8), 8)
    stays = eighth == lax.rem(me, 8)
    octets = n // 8

    def partner(i):
        return eighth + 8 * lax.rem(me // 8 + i, octets)

    barrier = pltpu.get_barrier_semaphore()

    def greet(segment, point):
        pl.semaphore_signal(
            barrier, inc=1, device_id=(segment, point), device_id_type=MESH
        )

    for i in range(octets):
        if i == 0:
            pl.when(jnp.logical_not(stays))(lambda: greet(partner(0), tp))
        else:
            greet(partner(i), tp)
    for i in range(1, POINTS):
        for segment in (me, left, right):
            greet(segment, lax.rem(tp + i, POINTS))
    greet(left, tp)
    greet(right, tp)

    lane8 = lax.broadcasted_iota(jnp.int32, (8, 128), 1)
    sub8 = lax.broadcasted_iota(jnp.int32, (8, 128), 0)
    acc[...] = jnp.zeros_like(acc)

    for copy in copies[:3]:
        copy.wait()

    points[0] = jnp.where(lane8[:1] < 64, heat[0, 0], ratio[0, 0])

    def add_up(d, total):
        for u in range(8):
            starts[8 * d + u] = total
            total = total + tallies[lax.rem(me, 8), 8 * d + u]
        return total

    lax.fori_loop(0, octets, add_up, jnp.int32(0))

    for copy in copies[3:]:
        copy.wait()

    fields = (absorb, level, shift, slot_value, width_value)
    slot_value[pl.ds(0, tiles)] = slot[...].astype(jnp.float32)
    width_value[pl.ds(0, tiles)] = width[...].astype(jnp.float32)
    for field in fields:
        field[pl.ds(tiles, 16)] = jnp.zeros((16, 128), jnp.float32)
    position = 128 * sub8 + lane8

    def pack(target):
        begin = starts[target]
        count = tallies[lax.rem(me, 8), target]
        tile = lax.shift_right_logical(begin, 7)
        offset = jnp.full((8, 128), lax.bitwise_and(begin, 127))
        here, after = pl.ds(tile, 8), pl.ds(tile + 1, 8)
        windows = []
        for f, field in enumerate(fields):
            window = jnp.where(lane8 >= offset, field[here, :], field[after, :])
            for unit in (1, 4, 16):
                digit = lax.bitwise_and(offset, 3 * unit)
                turned = [pltpu.roll(window, 128 - k * unit, 1) for k in (1, 2, 3)]
                for k in (1, 2, 3):
                    window = jnp.where(digit == k * unit, turned[k - 1], window)
            turned = pltpu.roll(window, 64, 1)
            window = jnp.where(offset >= 64, turned, window)
            if f == FIELDS - 1:
                window = jnp.where(position >= count, float(NW), window)
            windows.append(window[:PARTS])
        return windows

    def pack_some(batch, _):
        first = batch * PACK
        packed = [pack(partner(first + u)) for u in range(PACK)]
        for u in range(PACK):
            for f in range(FIELDS):
                send[first + u, f] = packed[u][f]
        return 0

    lax.fori_loop(0, octets // PACK, pack_some, 0)

    pl.semaphore_wait(barrier, octets + 2 + 3 * (POINTS - 1) - jnp.where(stays, 1, 0))

    def share(src, dst, sem_send, sem_recv):
        for i in range(1, POINTS):
            pltpu.make_async_remote_copy(
                src_ref=src.at[0],
                dst_ref=dst.at[i],
                send_sem=sem_send,
                recv_sem=sem_recv,
                device_id=(me, lax.rem(tp + i, POINTS)),
                device_id_type=MESH,
            ).start()

    def lines_to(i, sem):
        return pltpu.make_async_remote_copy(
            src_ref=send.at[i],
            dst_ref=recv.at[i],
            send_sem=sem,
            recv_sem=recv_sem.at[i],
            device_id=(partner(i), tp),
            device_id_type=MESH,
        )

    pl.when(jnp.logical_not(stays))(lambda: lines_to(0, first_sem).start())
    pl.when(stays)(
        lambda: pltpu.make_async_copy(
            send.at[0], recv.at[0], recv_sem.at[0]
        ).start()
    )
    share(points, points, point_send_sem, point_sem)
    for i in range(1, octets):
        lines_to(i, send_sem).start()
    share(shapes, shapes, shape_send_sem, shape_sem)

    def all_points(src, dst, sem_send, sem_recv):
        return pltpu.make_async_remote_copy(
            src_ref=src.at[pl.ds(1, POINTS - 1)],
            dst_ref=dst.at[pl.ds(1, POINTS - 1)],
            send_sem=sem_send,
            recv_sem=sem_recv,
            device_id=(me, lax.rem(tp + 1, POINTS)),
            device_id_type=MESH,
        )

    all_points(points, points, point_send_sem, point_sem).wait_recv()
    both = jnp.concatenate([points[i] for i in range(POINTS)], axis=0)
    heats = jnp.where(lane8 < 64, both, pltpu.roll(both, 64, 1))
    ratios = jnp.where(lane8 < 64, pltpu.roll(both, 64, 1), both)
    inverse_gap = 1.0 / heats - 1.0 / baseline_heat_level

    block_ids = lax.broadcasted_iota(jnp.int32, (128, BLOCKS), 1).astype(jnp.float32)
    width_ids = lax.broadcasted_iota(jnp.int32, (NW, 128), 0).astype(jnp.float32)
    point_lane = lax.broadcasted_iota(jnp.int32, (REACH, JW), 1) // NW

    def spread(row):
        return jnp.broadcast_to(row, (NW, 128)).astype(jnp.bfloat16)

    def arrived(g):
        pltpu.make_async_remote_copy(
            src_ref=send.at[g],
            dst_ref=recv.at[g],
            send_sem=send_sem,
            recv_sem=recv_sem.at[g],
            device_id=(partner(1), tp),
            device_id_type=MESH,
        ).wait_recv()

    def one_hots(g, rows, cols):
        absorbs, levels, shifts, slots, widths = (recv[g, f] for f in range(FIELDS))
        blocks = jnp.floor(slots * 0.125)
        cells = slots - 8.0 * blocks
        halves = cells * 0.5
        even_cell = jnp.where(halves == jnp.floor(halves), 1.0, 0.0)
        here = [cells == float(j) for j in range(8)]
        touched = [
            here[0],
            *(jnp.logical_or(here[j], here[j - 1]) for j in range(1, 8)),
            here[7],
        ]
        touched = [jnp.where(t, 1.0, 0.0) for t in touched]
        tall = jnp.concatenate([blocks, blocks[: 8 - PARTS]], axis=0).T
        scaled = planck_hc_over_boltzmann * levels
        below = 1.0 - shifts

        def one_hot(part):
            line = slice(part, part + 1)
            at = part * 128
            hits = jnp.broadcast_to(tall[:, line], (128, BLOCKS)) == block_ids
            rows[pl.ds(at, 128), :] = jnp.where(hits, 1.0, 0.0).astype(jnp.bfloat16)
            strength = ratios * jnp.exp(absorbs[line] - scaled[line] * inverse_gap)
            low = strength * below[line]
            high = strength * shifts[line]
            is_even = jnp.broadcast_to(even_cell[line], (POINTS, 128)) > 0.5
            evens = jnp.where(is_even, low, high)
            odds = jnp.where(is_even, high, low)
            is_width = jnp.broadcast_to(widths[line], (NW, 128)) == width_ids
            is_width = jnp.where(is_width, 1.0, 0.0).astype(jnp.bfloat16)
            cell_hits = [spread(t[line]) for t in touched]
            for p in range(POINTS):
                even = spread(evens[p : p + 1]) * is_width
                odd = spread(odds[p : p + 1]) * is_width
                for j in range(J):
                    top = p * JW + j * NW if j < 8 else POINTS * JW + p * NW
                    value = (odd if j % 2 else even) * cell_hits[j]
                    cols[pl.ds(top, NW), pl.ds(at, 128)] = value

        return [functools.partial(one_hot, part) for part in range(PARTS)]

    def rows_of(piece):
        return pl.ds(piece * (COLS // PARTS), COLS // PARTS)

    def added(piece, rows, cols):
        some = rows_of(piece)
        return acc[some] + jnp.dot(
            cols[some], rows[...], preferred_element_type=jnp.float32
        )

    def add_product(piece, rows, cols):
        acc[rows_of(piece)] = added(piece, rows, cols)

    def make_taps(p):
        taps = jnp.concatenate([shapes[p], jnp.zeros((NW, 128), jnp.float32)], axis=1)
        moved = [taps] + [pltpu.roll(taps, j, 1) for j in range(1, 8)]
        tall = jnp.concatenate(moved, axis=0).T[:REACH]
        ninth = jnp.concatenate([jnp.zeros((8, JW), jnp.float32), tall[:-8]], axis=0)
        ninth = jnp.where(point_lane == p, pltpu.roll(ninth, NW * p, 1), 0.0)
        high, low = split(jnp.concatenate([tall, ninth], axis=1))
        taps_high[p] = high
        taps_low[p] = low

    def step(g, rows, cols, last_rows, last_cols):
        for part, make in enumerate(one_hots(g, rows, cols)):
            add_product(part, last_rows, last_cols)
            make()

    make_taps(0)
    arrived(0)
    for make in one_hots(0, rows0, cols0):
        make()

    def deposit(h, _):
        arrived(2 * h + 1)
        arrived(2 * h + 2)
        step(2 * h + 1, rows1, cols1, rows0, cols0)
        step(2 * h + 2, rows0, cols0, rows1, cols1)
        return 0

    lax.fori_loop(0, octets // 2 - 2, deposit, 0)
    all_points(shapes, shapes, shape_send_sem, shape_sem).wait_recv()
    for g in range(octets - 3, octets):
        arrived(g)
    step(octets - 3, rows1, cols1, rows0, cols0)
    make_taps(1)
    make_taps(2)
    step(octets - 2, rows0, cols0, rows1, cols1)
    make_taps(3)
    make_taps(4)
    step(octets - 1, rows1, cols1, rows0, cols0)
    for p in range(5, POINTS):
        make_taps(p)
    for piece in range(PARTS):
        high, low = split(added(piece, rows1, cols1))
        bins_high[rows_of(piece)] = high
        bins_low[rows_of(piece)] = low

    def fold(x):
        kept = jnp.where(lane8 < 16, x, 0.0)
        moved = pltpu.roll(kept, 0, 1, stride=16, stride_axis=0)
        return jnp.sum(moved, axis=0, keepdims=True)

    def unfold(row):
        wide = jnp.broadcast_to(row, (8, 128))
        moved = wide
        for i in range(1, 8):
            moved = jnp.where(sub8 == i, pltpu.roll(wide, 128 - 16 * i, 1), moved)
        return jnp.where(lane8 < 16, moved, 0.0)

    def convolve(p):
        own = pl.ds(pl.multiple_of(p * JW, JW), JW)
        ninth = pl.ds(POINTS * JW, JW)
        bin_high = jnp.concatenate([bins_high[own], bins_high[ninth]], axis=0)
        bin_low = jnp.concatenate([bins_low[own], bins_low[ninth]], axis=0)
        product = jnp.dot(taps_high[p], bin_high, preferred_element_type=jnp.float32)
        product += jnp.dot(taps_low[p], bin_high, preferred_element_type=jnp.float32)
        product += jnp.dot(taps_high[p], bin_low, preferred_element_type=jnp.float32)
        first, second = product[128:136, :128], product[128:136, 128:]
        outside = jnp.zeros((8, 128), jnp.float32)
        for m in range(33):
            by = m - 16
            if by == 0:
                continue
            front, back = product[8 * m : 8 * m + 8, :128], product[8 * m : 8 * m + 8, 128:]
            front = pltpu.roll(front, by % 128, 1)
            back = pltpu.roll(back, by % 128, 1)
            if by > 0:
                wraps = lane8 < by
                first += jnp.where(wraps, 0.0, front)
                second += jnp.where(wraps, front, back)
                outside += jnp.where(wraps, back, 0.0)
            else:
                wraps = lane8 >= 128 + by
                first += jnp.where(wraps, back, front)
                second += jnp.where(wraps, 0.0, back)
                outside += jnp.where(wraps, front, 0.0)
        main_send[p, 0] = first
        main_send[p, 1] = second
        left_send[p] = fold(pltpu.roll(outside, 16, 1))
        right_send[p] = fold(outside)

    def send_sums(p):
        point = lax.rem(tp + POINTS - p, POINTS)

        @pl.when(p > 0)
        def _():
            pltpu.make_async_remote_copy(
                src_ref=main_send.at[p],
                dst_ref=main_recv.at[p],
                send_sem=main_send_sem,
                recv_sem=main_sem,
                device_id=(me, point),
                device_id_type=MESH,
            ).start()

        for k, (src, dst, segment) in enumerate(
            ((left_send, left_recv, left), (right_send, right_recv, right))
        ):
            pltpu.make_async_remote_copy(
                src_ref=src.at[p],
                dst_ref=dst.at[p],
                send_sem=halo_send_sem.at[k],
                recv_sem=halo_sem.at[k],
                device_id=(segment, point),
                device_id_type=MESH,
            ).start()

    def convolve_two(h, _):
        pair = (POINTS // 2 + h, POINTS // 2 - 1 - h)
        for p in pair:
            convolve(p)
        for p in pair:
            send_sums(p)
        return 0

    lax.fori_loop(0, POINTS // 2, convolve_two, 0)

    sums = all_points(main_send, main_recv, main_send_sem, main_sem)
    halos = [
        pltpu.make_async_remote_copy(
            src_ref=src,
            dst_ref=dst,
            send_sem=halo_send_sem.at[k],
            recv_sem=halo_sem.at[k],
            device_id=(segment, tp),
            device_id_type=MESH,
        )
        for k, (src, dst, segment) in enumerate(
            ((left_send, left_recv, left), (right_send, right_recv, right))
        )
    ]
    for halo in halos:
        halo.wait_recv()
    from_right = unfold(jnp.sum(left_recv[...], axis=0))
    from_left = unfold(jnp.sum(right_recv[...], axis=0))
    from_right = jnp.where(me < n - 1, pltpu.roll(from_right, 112, 1), 0.0)
    from_left = jnp.where(me > 0, from_left, 0.0)
    first = main_send[0, 0] + from_left
    second = main_send[0, 1] + from_right
    sums.wait_recv()
    for p in range(1, POINTS):
        first += main_recv[p, 0]
        second += main_recv[p, 1]
    for k, part in enumerate((first, second)):
        tall = jnp.concatenate([part, jnp.zeros((120, 128), jnp.float32)], axis=0)
        ordered[pl.ds(128 * k, 128), :] = tall.T
    total = ordered[pl.ds(0, 16, stride=16), :]
    for k in range(1, 16):
        total += pltpu.roll(ordered[pl.ds(k, 16, stride=16), :], 8 * k, 1)
    out_ref[...] = total

    all_points(points, points, point_send_sem, point_sem).wait_send()
    all_points(shapes, shapes, shape_send_sem, shape_sem).wait_send()
    pl.when(jnp.logical_not(stays))(lambda: lines_to(0, first_sem).wait_send())
    pltpu.make_async_remote_copy(
        src_ref=send.at[pl.ds(1, octets - 1)],
        dst_ref=recv.at[pl.ds(1, octets - 1)],
        send_sem=send_sem,
        recv_sem=recv_sem.at[1],
        device_id=(partner(1), tp),
        device_id_type=MESH,
    ).wait_send()
    sums.wait_send()
    for halo in halos:
        halo.wait_send()


def body(
    natural_logged_absorbance,
    lower_state_level,
    subgrid_shift_ratio,
    local_grid_slot,
    broadening_class,
    tallies_per_shard,
    heat_levels,
    sum_over_states_ratio,
    shape_kernels,
):
    n = lax.axis_size("seg")
    lines = natural_logged_absorbance.shape[0]
    tiles = lines // 128
    hbm = pl.BlockSpec(memory_space=pl.ANY)
    vmem = pl.BlockSpec(memory_space=pltpu.VMEM)
    f32, bf16, i32 = jnp.float32, jnp.bfloat16, jnp.int32
    dma = pltpu.SemaphoreType.DMA
    result = pl.pallas_call(
        functools.partial(kernel, n),
        out_shape=jax.ShapeDtypeStruct((16, 128), f32),
        in_specs=[hbm] * 9,
        out_specs=vmem,
        scratch_shapes=[
            pltpu.SMEM((1, 1), f32),
            pltpu.SMEM((1, 1), f32),
            pltpu.SMEM((8, n), i32),
            pltpu.VMEM((tiles + 16, 128), f32),
            pltpu.VMEM((tiles + 16, 128), f32),
            pltpu.VMEM((tiles + 16, 128), f32),
            pltpu.VMEM((tiles, 128), i32),
            pltpu.VMEM((tiles, 128), i32),
            pltpu.VMEM((tiles + 16, 128), f32),
            pltpu.VMEM((tiles + 16, 128), f32),
            pltpu.SMEM((n,), i32),
            pltpu.VMEM((n // 8, FIELDS, PARTS, 128), f32),
            pltpu.VMEM((n // 8, FIELDS, PARTS, 128), f32),
            pltpu.VMEM((POINTS, 1, 128), f32),
            pltpu.VMEM((POINTS, NW, 256), f32),
            pltpu.VMEM((CAP, BLOCKS), bf16),
            pltpu.VMEM((COLS, CAP), bf16),
            pltpu.VMEM((CAP, BLOCKS), bf16),
            pltpu.VMEM((COLS, CAP), bf16),
            pltpu.VMEM((COLS, BLOCKS), f32),
            pltpu.VMEM((POINTS, REACH, 2 * JW), bf16),
            pltpu.VMEM((POINTS, REACH, 2 * JW), bf16),
            pltpu.VMEM((COLS, BLOCKS), bf16),
            pltpu.VMEM((COLS, BLOCKS), bf16),
            pltpu.VMEM((POINTS, 2, 8, 128), f32),
            pltpu.VMEM((POINTS, 1, 128), f32),
            pltpu.VMEM((POINTS, 1, 128), f32),
            pltpu.VMEM((POINTS, 2, 8, 128), f32),
            pltpu.VMEM((POINTS, 1, 128), f32),
            pltpu.VMEM((POINTS, 1, 128), f32),
            pltpu.VMEM((BLOCKS, 128), f32),
            dma((9,)),
            dma,
            dma,
            dma((n // 8,)),
            dma,
            dma,
            dma,
            dma,
            dma,
            dma,
            dma((2,)),
            dma((2,)),
        ],
        compiler_params=pltpu.CompilerParams(
            collective_id=0, has_side_effects=True, vmem_limit_bytes=56541184
        ),
        cost_estimate=pl.CostEstimate(
            flops=2 * n * CAP // 8 * BLOCKS * COLS,
            bytes_accessed=300000,
            transcendentals=n * CAP // 8 * POINTS,
        ),
    )(
        heat_levels.reshape(1, 1),
        sum_over_states_ratio.reshape(1, 1),
        tallies_per_shard,
        natural_logged_absorbance.reshape(tiles, 128),
        lower_state_level.reshape(tiles, 128),
        subgrid_shift_ratio.reshape(tiles, 128),
        local_grid_slot.reshape(tiles, 128),
        broadening_class.reshape(tiles, 128),
        shape_kernels[0],
    )
    return result.reshape(1, G)


def solution(mesh):
    in_specs = (
        P("seg"),
        P("seg"),
        P("seg"),
        P("seg"),
        P("seg"),
        P(),
        P("tp"),
        P("tp"),
        P("tp", None, None),
    )
    out_specs = P("tp", "seg")
    return jax.shard_map(body, mesh=mesh, in_specs=in_specs, out_specs=out_specs, check_vma=False)
```
